256 devices in a mesh: prow: 8 (over y, core), pcol: 32 (over x, z).
Axes of the slice: x: 4, y: 4, z: 8, core: 2. Of those that a mesh axis runs over, the one named last changes fastest.
Arguments:
- state: float32 [3, 176, 4096], P(None, 'prow', 'pcol'), may hold values from -6 to 6
- adjoint: float32 [3, 176, 4096], P(None, 'prow', 'pcol'), may hold values from -6 to 6
- thickness: float32 [32768], P(('prow', 'pcol')), may hold values from 0.5 to 1.5
- direction: float32 [32768], P(('prow', 'pcol')), may hold values from -4 to 4
- design_map: int32 [176, 4096], P('prow', 'pcol'), may hold values from 0 to 32767, as said below
- levels: int32 [8, 32], P('prow', 'pcol'), may hold values from 1 to 4, as said below
- blocks: float32 [576, 72, 4096], P('prow', None, 'pcol'), may hold values from -1 to 1.5, as said below
Outputs:
- tangent: float32 [3, 176, 4096], P(None, 'prow', 'pcol')
- second_adjoint: float32 [3, 176, 4096], P(None, 'prow', 'pcol')
- hess: float32 [32768], P(('prow', 'pcol'))
The draws below stay inside these ranges and needn't reach their ends.
Inputs may be any that keep to these rules, and one draw needn't show every extreme that they name: `design_map`: each design thickness covers a contiguous region of the shell of about 22 rows by 1 column, with ragged edges; every thickness is taken by some cell; the numbering of the regions is unrelated to their place on the grid. `levels`: each patch's refinement level; some patch has level 4 and some has level 1. `blocks`: each column's block is symmetric with a diagonal that exceeds the sum of the magnitudes of the rest of its row.
All inputs are finite; a program needn't handle non-finite values.
Results may differ from the reference program's by a relative error of at most 0.0003.
Values sent between devices are 32-bit elements; how exact they have to be, the bound alone decides.
No kernel may reach another device: no remote copies, remote signals or barrier semaphores. Data moves between devices by JAX's collectives and lax.ppermute only.
A program may use at most 64 MiB of HBM per device.

```python
import jax
import jax.numpy as jnp
from jax import lax

CR = 22
CC = 128
DV_DEV = 128
ITERS = 2
MAXLEVEL = 4
BLK = 72
NR = 176
NC = 4096
NDV = 32768
N_PROW = 8
N_PCOL = 32


def draw_design_map(key, part):
    key = jax.random.fold_in(key, 17)
    first, second = jax.random.split(key)
    width = CC // DV_DEV
    rows = jnp.arange(NR, dtype=jnp.int32)[:, None]
    cols = jnp.arange(NC, dtype=jnp.int32)[None, :]
    jump = jax.random.randint(first, (NR, NC), -1, 2)
    jump = jnp.where(rows % CR == CR // 2, 0, jump)
    moved = jnp.clip(rows + jump, 0, NR - 1)
    owner = moved // CR * N_PCOL + cols // CC
    region = owner * DV_DEV + cols % CC // width
    order = jax.random.permutation(second, NDV)
    return order[region].astype(jnp.int32)


def draw_levels(key, part):
    key = jax.random.fold_in(key, 5)
    first, second = jax.random.split(key)
    count = N_PROW * N_PCOL
    base = jax.random.randint(first, (N_PROW, N_PCOL), 1, MAXLEVEL + 1)
    spot = jax.random.randint(second, (), 0, count)
    flat = jnp.arange(count).reshape(N_PROW, N_PCOL)
    base = jnp.where(flat == spot, MAXLEVEL, base)
    base = jnp.where(flat == (spot + 1) % count, 1, base)
    return base.astype(jnp.int32)


def draw_blocks(key, part):
    key = jax.random.fold_in(key, 11)
    first, second = jax.random.split(key)
    width = 0.45 / BLK
    raw = jax.random.uniform(first, (N_PROW, BLK, BLK, NC), jnp.float32, -1.0, 1.0)
    middle = jax.random.uniform(second, (N_PROW, BLK, 1, NC), jnp.float32, 0.75, 1.25)
    paired = 0.5 * width * (raw + jnp.swapaxes(raw, 1, 2))
    diagonal = (jnp.arange(BLK)[:, None] == jnp.arange(BLK)[None, :])[None, :, :, None]
    result = jnp.where(diagonal, middle, paired)
    return result.reshape(N_PROW * BLK, BLK, NC).astype(jnp.float32)


def level_of(own_key, shape, pieces, low, top_value):
    factor_of = 1.0
    for position, parts in pieces:
        heights = jax.random.uniform(jax.random.fold_in(jax.random.fold_in(own_key, 6), position), (parts,), jnp.float32, low / len(pieces), top_value / len(pieces))
        factor_of = factor_of * jnp.repeat(jnp.exp(heights), shape[position] // parts).reshape((-1,) + (1,) * (len(shape) - 1 - position))
    return factor_of


def gaussian(own_key, shape, deviation, bound, cuts=(), kind=jnp.bfloat16):
    gain = level_of(own_key, shape, cuts, -0.22, 0.18) if cuts else 1.0
    values = jax.random.normal(own_key, shape, jnp.float32) * deviation * gain
    return jnp.minimum(jnp.maximum(values, -bound), bound).astype(kind)


def setup_inputs(seed: int = 0) -> dict:
    seeds = jax.random.split(jax.random.key(seed), 8)
    state = gaussian(seeds[0], (3, NR, NC), 1.0, 6.0, ((1, 8), (2, 32)), jnp.float32)
    adjoint = gaussian(seeds[1], (3, NR, NC), 1.0, 6.0, ((1, 8), (2, 32)), jnp.float32)
    thickness = jnp.clip(0.5 + 1.0 * jax.random.uniform(seeds[2], (NDV,), jnp.float32) ** level_of(seeds[2], (NDV,), ((0, 256),), -0.2, 0.2), 0.5, 1.5)
    direction = gaussian(seeds[3], (NDV,), 1.0, 4.0, ((0, 256),), jnp.float32)
    design_map = draw_design_map(jax.random.fold_in(seeds[7], 71), 0)
    levels = draw_levels(jax.random.fold_in(seeds[7], 71), 0)
    blocks = draw_blocks(jax.random.fold_in(seeds[7], 71), 0)
    return {"state": state, "adjoint": adjoint, "thickness": thickness, "direction": direction, "design_map": design_map, "levels": levels, "blocks": blocks}


HIGH = lax.Precision.HIGHEST


def neighbours(field):
    zero_row = jnp.zeros_like(field[..., :1, :])
    above = jnp.concatenate([zero_row, field[..., :-1, :]], axis=-2)
    below = jnp.concatenate([field[..., 1:, :], zero_row], axis=-2)
    left_side = jnp.roll(field, 1, axis=-1)
    right_side = jnp.roll(field, -1, axis=-1)
    return (above, below, left_side, right_side)


def stiffness_with(weights, field, around, shift):
    total = shift * field
    for weight, other in zip(weights, around):
        total = total + weight * (field - other)
    return total


def precondition(resid, levels, blocks):
    padded = jnp.pad(resid, ((0, 0), (0, 0), (1, 1), (0, 0)))
    row_index = (jnp.arange(N_PROW, dtype=jnp.int32)[:, None] * CR
                 + jnp.arange(CR + 2, dtype=jnp.int32)[None, :])
    extended = padded[:, :, row_index, :]
    extended = jnp.transpose(extended, (2, 0, 1, 3, 4)).reshape(N_PROW, 2, BLK, NC)
    matrices = blocks.reshape(N_PROW, BLK, BLK, NC)
    level_cols = jnp.repeat(levels, CC, axis=1)[:, None, None, :]
    term = jnp.einsum("rabj,rnbj->rnaj", matrices, extended, precision=HIGH)
    total = term
    for order in range(1, MAXLEVEL):
        term = 0.5 * jnp.einsum("rabj,rnbj->rnaj", matrices, term, precision=HIGH)
        total = total + jnp.where(level_cols > order, term, jnp.float32(0.0))
    total = jnp.transpose(total.reshape(N_PROW, 2, 3, CR + 2, NC), (1, 2, 0, 3, 4))
    placed = jnp.zeros((2, 3, NR + 2, NC), jnp.float32).at[:, :, row_index, :].add(total)
    return placed[:, :, 1:-1, :]


def inner_sums(first, second):
    return jnp.sum(first * second, axis=(1, 2, 3))


def reference(state, adjoint, thickness, direction, design_map, levels, blocks):
    t_cell = thickness[design_map]
    d_cell = direction[design_map]
    stiff = t_cell * t_cell * t_cell
    slope = 3.0 * t_cell * t_cell * d_cell
    curve = 6.0 * t_cell * d_cell
    stiff_n = neighbours(stiff)
    slope_n = neighbours(slope)
    weights = tuple(0.5 * (stiff + other) for other in stiff_n)
    dweights = tuple(0.5 * (slope + other) for other in slope_n)
    known = jnp.stack([state, adjoint])
    known_n = neighbours(known)
    rhs = -stiffness_with(dweights, known, known_n, 0.0)
    solved = jnp.zeros_like(rhs)
    resid = rhs
    pre = precondition(resid, levels, blocks)
    search = pre
    gamma = inner_sums(resid, pre)
    for step in range(ITERS):
        image = stiffness_with(weights, search, neighbours(search), 1.0)
        alpha = gamma / inner_sums(search, image)
        solved = solved + alpha[:, None, None, None] * search
        if step + 1 < ITERS:
            resid = resid - alpha[:, None, None, None] * image
            pre = precondition(resid, levels, blocks)
            gamma_new = inner_sums(resid, pre)
            search = pre + (gamma_new / gamma)[:, None, None, None] * search
            gamma = gamma_new
    solved_n = neighbours(solved)
    first_acc = jnp.zeros_like(stiff)
    second_acc = jnp.zeros_like(stiff)
    for known_o, solved_o in zip(known_n, solved_n):
        known_d = known - known_o
        solved_d = solved - solved_o
        first_acc = first_acc + jnp.sum(solved_d[1] * known_d[0] + known_d[1] * solved_d[0], axis=0)
        second_acc = second_acc + jnp.sum(known_d[1] * known_d[0], axis=0)
    cellterm = -(0.5 * 3.0 * t_cell * t_cell * first_acc + 0.5 * curve * second_acc)
    hess = jax.ops.segment_sum(cellterm.reshape(-1), design_map.reshape(-1), num_segments=NDV)
    return solved[0], solved[1], hess
```

```python
import functools

import jax
import jax.numpy as jnp
from jax import lax
from jax.experimental import pallas as pl
from jax.experimental.pallas import tpu as pltpu
from jax.sharding import PartitionSpec as P

CR = 22
CC = 128
DV = 128
BLK = 72
EXT = CR + 2
FR = 32
BOTH = ("prow", "pcol")
F32 = jnp.float32
BF16 = jnp.bfloat16

VMEM = pl.BlockSpec(memory_space=pltpu.VMEM)
SMEM = pl.BlockSpec(memory_space=pltpu.SMEM)
ANY = pl.BlockSpec(memory_space=pl.ANY)


def call(kernel, out_shapes, in_specs, scratch=(), out_specs=None):
    return pl.pallas_call(
        kernel,
        out_shape=[jax.ShapeDtypeStruct(s, F32) for s in out_shapes],
        in_specs=list(in_specs),
        out_specs=[VMEM] * len(out_shapes) if out_specs is None else out_specs,
        scratch_shapes=list(scratch),
        compiler_params=pltpu.CompilerParams(vmem_limit_bytes=48 * 1024 * 1024),
    )


def iota(shape, dim):
    return lax.broadcasted_iota(jnp.int32, shape, dim)


def pack_edges(tiles, width):
    lane = iota((8, CC), 1)
    first = jnp.zeros((8, CC), F32)
    last = jnp.zeros((8, CC), F32)
    for k, tile in enumerate(tiles):
        at = k * width
        here = (lane >= at) & (lane < at + width)
        first = jnp.where(here, pltpu.roll(tile, at, 1) if at else tile, first)
        last = jnp.where(here, pltpu.roll(tile, at + width, 1), last)
    return first, last


def unpack_edges(from_left, from_right, count, width):
    lane = iota((8, CC), 1)
    tiles = []
    for k in range(count):
        at = k * width
        right = pltpu.roll(from_right, CC - at, 1) if at else from_right
        shift = (CC - width - at) % CC
        left = pltpu.roll(from_left, shift, 1) if shift else from_left
        tiles.append(jnp.where(lane < width, right, jnp.where(lane >= CC - width, left, 0.0)))
    return tiles


def lanes_of(x):
    return iota(x.shape, x.ndim - 1)


def left_of(main, side):
    dim = main.ndim - 1
    return jnp.where(lanes_of(main) == 0, pltpu.roll(side, 1, dim), pltpu.roll(main, 1, dim))


def right_of(main, side):
    dim = main.ndim - 1
    return jnp.where(
        lanes_of(main) == CC - 1, pltpu.roll(side, CC - 1, dim), pltpu.roll(main, CC - 1, dim)
    )


def grid_mask(prow, last, start, rows):
    row = iota((rows, CC), 0) + (start - 8)
    outside = ((row < 0) & (prow == 0)) | ((row >= CR) & (prow == last))
    return jnp.where(outside, 0.0, 1.0).astype(F32)


def start_kernel(state, adjoint, dmap, first_out, last_out, scr):
    scr[...] = jnp.zeros_like(scr)
    scr[0:3, 0:CR, :] = state[...]
    scr[3:6, 0:CR, :] = adjoint[...]
    scr[6, 0:CR, :] = dmap[...].astype(F32)
    tiles = [scr[f, 8 * g:8 * g + 8, :] for f in range(7) for g in range(3)]
    first, last = pack_edges(tiles, 1)
    first_out[...] = first
    last_out[...] = last


def rows_kernel(state, adjoint, dmap, from_left, from_right, side_out, up_out, down_out, scr):
    scr[...] = jnp.zeros_like(scr)
    scr[0:3, 0:CR, :] = state[...]
    scr[3:6, 0:CR, :] = adjoint[...]
    scr[6, 0:CR, :] = dmap[...].astype(F32)
    tiles = unpack_edges(from_left[...], from_right[...], 21, 1)
    for f in range(7):
        for g in range(3):
            side_out[f, 8 * g:8 * g + 8, :] = tiles[3 * f + g]
    up_out[...] = jnp.zeros_like(up_out)
    down_out[...] = jnp.zeros_like(down_out)
    for f in range(7):
        up_out[0, 2 * f:2 * f + 2, :] = scr[f, 0:2, :]
        up_out[1, 2 * f:2 * f + 2, :] = side_out[f, 0:2, :]
        down_out[0, 2 * f:2 * f + 2, :] = scr[f, CR - 2:CR, :]
        down_out[1, 2 * f:2 * f + 2, :] = side_out[f, CR - 2:CR, :]


def apply_blocks(mats, vec):
    def rows(step, carry):
        one, two = carry
        for u in range(8):
            at = step * 8 + u
            mat = mats[at]
            one = one + mat * vec[0, pl.ds(at, 1), :]
            two = two + mat * vec[1, pl.ds(at, 1), :]
        return one, two

    zero = jnp.zeros((BLK, CC), F32)
    return lax.fori_loop(0, BLK // 8, rows, (zero, zero))


def local_solve(mats, vec, total, level):
    one, two = apply_blocks(mats, vec)
    total[0] = one
    total[1] = two
    vec[0] = one
    vec[1] = two

    def further(_, carry):
        one, two = apply_blocks(mats, vec)
        one = 0.5 * one
        two = 0.5 * two
        vec[0] = one
        vec[1] = two
        total[0] += one
        total[1] += two
        return carry

    lax.fori_loop(1, level, further, 0)


def look_up(table, index, tcell, dcell):
    flipped = table[...].T
    part0 = flipped.astype(BF16)
    part1 = (flipped - part0.astype(F32)).astype(BF16)
    lhs = jnp.concatenate([part0, part1], axis=0)
    high = [ix // DV for ix in index]
    low = [ix % DV for ix in index]
    lane1 = iota((1, CC), 1)

    def both(vh, vl):
        hot = jnp.where(iota((256, 2 * CC), 0) == vh, 1.0, 0.0).astype(BF16)
        got = jnp.dot(lhs, hot, preferred_element_type=F32)
        mine = iota((DV, 2 * CC), 0) == vl
        tv = jnp.sum(jnp.where(mine, got[0:DV] + got[2 * DV:3 * DV], 0.0), axis=0, keepdims=True)
        dv = jnp.sum(jnp.where(mine, got[DV:2 * DV] + got[3 * DV:4 * DV], 0.0), axis=0, keepdims=True)
        return tv, dv

    for r in range(6, FR, 2):
        vh = jnp.concatenate([high[0][r:r + 1], high[0][r + 1:r + 2]], axis=1)
        vl = jnp.concatenate([low[0][r:r + 1], low[0][r + 1:r + 2]], axis=1)
        tv, dv = both(vh, vl)
        for h in range(2):
            tcell[0, r + h:r + h + 1, :] = tv[:, h * CC:(h + 1) * CC]
            dcell[0, r + h:r + h + 1, :] = dv[:, h * CC:(h + 1) * CC]
    packs = []
    for half in range(2):
        vec = jnp.zeros((1, CC), jnp.int32)
        for i in range(16):
            r = 16 * half + i
            vec = jnp.where(lane1 // 8 == i, pltpu.roll(index[1][r:r + 1], (8 * i + 4) % CC, 1), vec)
        packs.append(vec)
    vec = jnp.concatenate(packs, axis=1)
    tv, dv = both(vec // DV, vec % DV)
    for half in range(2):
        for i in range(16):
            r = 16 * half + i
            shift = (CC - 8 * i - 4) % CC
            keep = (lane1 < 4) | (lane1 >= CC - 4)
            cut = slice(half * CC, (half + 1) * CC)
            tcell[1, r:r + 1, :] = jnp.where(keep, pltpu.roll(tv[:, cut], shift, 1), 0.0)
            dcell[1, r:r + 1, :] = jnp.where(keep, pltpu.roll(dv[:, cut], shift, 1), 0.0)


def weights_of(main, side, lo, hi):
    here = main[lo:hi]
    return [
        0.5 * (here + main[lo - 1:hi - 1]),
        0.5 * (here + main[lo + 1:hi + 1]),
        0.5 * (here + left_of(here, side[lo:hi])),
        0.5 * (here + right_of(here, side[lo:hi])),
    ]


def differences(main, side, lo, hi):
    here = main[:, lo:hi, :]
    beside = side[:, lo:hi, :]
    return [
        here - main[:, lo - 1:hi - 1, :],
        here - main[:, lo + 1:hi + 1, :],
        here - left_of(here, beside),
        here - right_of(here, beside),
    ]


def first_kernel(
    last, info, table, state, adjoint, dmap, side, from_up, from_down, blocks,
    resid_out, local_out, up_out, down_out, main_f, side_f, tcell, dcell,
    mats, vec, total, index_scr, sem,
):
    copy = pltpu.make_async_copy(blocks, mats, sem)
    copy.start()
    level, prow = info[0], info[1]
    main_f[...] = jnp.zeros_like(main_f)
    side_f[...] = jnp.zeros_like(side_f)
    index_scr[...] = jnp.zeros_like(index_scr)
    main_f[0:3, 8:8 + CR, :] = state[...]
    main_f[3:6, 8:8 + CR, :] = adjoint[...]
    for f in range(6):
        side_f[f, 8:8 + CR, :] = side[f, 0:CR, :]
        for tile, ref in ((0, main_f), (1, side_f)):
            ref[f, 6:8, :] = from_up[tile, 2 * f:2 * f + 2, :]
            ref[f, 8 + CR:10 + CR, :] = from_down[tile, 2 * f:2 * f + 2, :]
    index_scr[0, 8:8 + CR, :] = dmap[...].astype(F32)
    index_scr[1, 8:8 + CR, :] = side[6, 0:CR, :]
    for tile in range(2):
        index_scr[tile, 6:8, :] = from_up[tile, 12:14, :]
        index_scr[tile, 8 + CR:10 + CR, :] = from_down[tile, 12:14, :]
    index = [index_scr[tile].astype(jnp.int32) for tile in range(2)]
    tcell[...] = jnp.zeros_like(tcell)
    dcell[...] = jnp.zeros_like(dcell)
    look_up(table, index, tcell, dcell)
    inside = grid_mask(prow, last, 0, FR)
    for tile in range(2):
        tcell[tile] = tcell[tile] * inside
    slope = [3.0 * tcell[tile] * tcell[tile] * dcell[tile] for tile in range(2)]
    lo, hi = 7, 7 + EXT
    parts = differences(main_f, side_f, lo, hi)
    rhs = jnp.zeros((6, EXT, CC), F32)
    for weight, diff in zip(weights_of(slope[0], slope[1], lo, hi), parts):
        rhs = rhs - weight[None] * diff
    rhs = rhs * inside[lo:hi][None]
    resid_out[...] = rhs
    vec[...] = rhs.reshape(2, BLK, CC)
    copy.wait()
    local_solve(mats, vec, total, level)
    local = total[...].reshape(6, EXT, CC)
    local_out[...] = local
    up_out[...] = local[:, 0:8, :]
    down_out[...] = local[:, EXT - 8:EXT, :]


def join_kernel(last, info, local, from_up, from_down, frame_out, first_out, last_out):
    prow = info[1]
    frame_out[...] = jnp.zeros_like(frame_out)
    frame_out[:, 7:7 + EXT, :] = local[...]
    frame_out[:, 6:9, :] += from_up[:, 5:8, :]
    frame_out[:, 7 + CR:10 + CR, :] += from_down[:, 0:3, :]
    inside = grid_mask(prow, last, 0, FR)
    frame_out[...] = frame_out[...] * inside[None]
    tiles = []
    for f in range(6):
        field = frame_out[f, 7:7 + EXT, :]
        tiles += [field[8 * g:8 * g + 8] for g in range(3)]
    first, last_lanes = pack_edges(tiles, 1)
    first_out[...] = first
    last_out[...] = last_lanes


def fill_side(side_f, from_left, from_right):
    tiles = unpack_edges(from_left[...], from_right[...], 18, 1)
    side_f[...] = jnp.zeros_like(side_f)
    for f in range(6):
        for g in range(3):
            side_f[f, 7 + 8 * g:15 + 8 * g, :] = tiles[3 * f + g]


def stiffness(main_f, side_f, tcell, lo, hi):
    stiff = [tcell[tile] * tcell[tile] * tcell[tile] for tile in range(2)]
    out = main_f[:, lo:hi, :]
    parts = differences(main_f, side_f, lo, hi)
    for weight, diff in zip(weights_of(stiff[0], stiff[1], lo, hi), parts):
        out = out + weight[None] * diff
    return out


def second_kernel(
    last, info, frame, from_left, from_right, tcell, blocks,
    image_out, side_out, local_out, up_out, down_out, mats, vec, total, sem,
):
    copy = pltpu.make_async_copy(blocks, mats, sem)
    copy.start()
    level, prow = info[0], info[1]
    fill_side(side_out, from_left, from_right)
    lo, hi = 7, 7 + EXT
    image = stiffness(frame, side_out, tcell, lo, hi)
    image = image * grid_mask(prow, last, lo, EXT)[None]
    image_out[...] = image
    vec[...] = image.reshape(2, BLK, CC)
    copy.wait()
    local_solve(mats, vec, total, level)
    local = total[...].reshape(6, EXT, CC)
    local_out[...] = local
    up_out[...] = local[:, 0:8, :]
    down_out[...] = local[:, EXT - 8:EXT, :]


def third_kernel(
    dmap, resid, image, zframe, zside, wframe, from_left, from_right, tcell, dcell, main_f, side_f,
    sums_out, wside, left_op, right_op,
):
    fill_side(wside, from_left, from_right)
    lo, hi = 8, 8 + CR
    v = stiffness(wframe, wside, tcell, lo, hi)
    r = resid[:, 1:1 + CR, :]
    q = image[:, 1:1 + CR, :]
    z = zframe[:, lo:hi, :]
    w = wframe[:, lo:hi, :]
    lane = iota((1, CC), 1)
    dots = jnp.zeros((1, CC), F32)
    pairs = ((r, z), (z, q), (r, w), (q, w), (z, v), (w, v))
    for k, (a, b) in enumerate(pairs):
        ab = a * b
        for s in range(2):
            part = ab[3 * s] + ab[3 * s + 1] + ab[3 * s + 2]
            value = jnp.sum(jnp.sum(part, axis=0, keepdims=True), axis=1, keepdims=True)
            dots = jnp.where(lane == 2 * k + s, value, dots)
    t = tcell[0, lo:hi, :]
    d = dcell[0, lo:hi, :]
    known_d = differences(main_f, side_f, lo, hi)
    z_d = differences(zframe, zside, lo, hi)
    w_d = differences(wframe, wside, lo, hi)

    def dot3(a, b, i, j):
        out = jnp.zeros((CR, CC), F32)
        for an, bn in zip(a, b):
            for c in range(3):
                out = out + an[i + c] * bn[j + c]
        return out

    slope2 = -1.5 * t * t
    values = [
        (-3.0 * t * d) * dot3(known_d, known_d, 3, 0),
        slope2 * dot3(z_d, known_d, 3, 0),
        slope2 * dot3(w_d, known_d, 3, 0),
        slope2 * dot3(known_d, z_d, 3, 0),
        slope2 * dot3(known_d, w_d, 3, 0),
    ]
    high = dmap[...] // DV
    low = dmap[...] % DV
    for row in range(CR):
        hot = jnp.where(iota((256, CC), 0) == high[row:row + 1], 1.0, 0.0).astype(BF16)
        at = 2 * CC * row
        left_op[:, at:at + CC] = hot
        left_op[:, at + CC:at + 2 * CC] = hot
        mine = iota((DV, CC), 0) == low[row:row + 1]
        for k, value in enumerate(values):
            one = value[row:row + 1]
            top = one.astype(BF16).astype(F32)
            right_op[k * DV:(k + 1) * DV, at:at + CC] = jnp.where(mine, top, 0.0).astype(BF16)
            right_op[k * DV:(k + 1) * DV, at + CC:at + 2 * CC] = jnp.where(mine, one - top, 0.0).astype(BF16)
    sums = lax.dot_general(
        left_op[...], right_op[...], (((1,), (1,)), ((), ())), preferred_element_type=F32
    )
    sums_out[:, 0:CC] = jnp.broadcast_to(dots, (256, CC))
    sums_out[:, CC:] = sums


def last_kernel(got, zframe, wframe, tangent, second, owned):
    sums = jnp.sum(got[...], axis=0, keepdims=True)
    dots = sums[:, 0:CC]
    lane = iota((1, CC), 1)

    def pick(k):
        return jnp.sum(jnp.where(lane == k, dots, 0.0), axis=1, keepdims=True)

    coeffs = []
    for s in range(2):
        rz, zq, rw, qw, zv, wv = (pick(2 * k + s) for k in range(6))
        alpha = rz / zq
        rz1 = rz - alpha * (zq + rw) + alpha * alpha * qw
        grow = 1.0 + rz1 / rz
        pq = grow * grow * zq - grow * alpha * (zv + qw) + alpha * alpha * wv
        alpha1 = rz1 / pq
        coeffs.append((alpha + alpha1 * grow, -alpha1 * alpha))
    for s, out in ((0, tangent), (1, second)):
        c0, c1 = coeffs[s]
        for f in range(3):
            out[f] = c0 * zframe[3 * s + f, 8:8 + CR, :] + c1 * wframe[3 * s + f, 8:8 + CR, :]
    h = [sums[:, (k + 1) * CC:(k + 2) * CC] for k in range(5)]
    owned[...] = (
        h[0] + coeffs[1][0] * h[1] + coeffs[1][1] * h[2] + coeffs[0][0] * h[3] + coeffs[0][1] * h[4]
    )


def shift_pair(axis, count, periodic, to_next, to_previous):
    forward = [(i, i + 1) for i in range(count - 1)]
    if periodic:
        forward.append((count - 1, 0))
    backward = [(b, a) for a, b in forward]
    return lax.ppermute(to_next, axis, forward), lax.ppermute(to_previous, axis, backward)


def per_device(state, adjoint, thickness, direction, design_map, levels, blocks):
    n_row, n_col = lax.axis_size("prow"), lax.axis_size("pcol")
    n_dev = n_row * n_col
    last = n_row - 1
    info = jnp.stack([levels[0, 0], lax.axis_index("prow").astype(jnp.int32)])
    rows = functools.partial(shift_pair, "prow", n_row, False)
    cols = functools.partial(shift_pair, "pcol", n_col, True)

    first, end = call(start_kernel, [(8, CC)] * 2, [VMEM] * 3, [pltpu.VMEM((7, EXT, CC), F32)])(
        state, adjoint, design_map
    )
    from_left, from_right = cols(end, first)
    own = jnp.concatenate([thickness, direction])
    table = lax.all_to_all(
        jnp.broadcast_to(own[None], (n_col, 2 * DV)), "pcol", 0, 0, tiled=True
    )
    side, up, down = call(
        rows_kernel, [(7, EXT, CC), (2, 16, CC), (2, 16, CC)], [VMEM] * 5,
        [pltpu.VMEM((7, EXT, CC), F32)],
    )(state, adjoint, design_map, from_left, from_right)
    from_up, from_down = rows(down, up)
    table = lax.all_to_all(
        jnp.broadcast_to(table[None], (n_row, n_col, 2 * DV)), "prow", 0, 0, tiled=True
    ).reshape(n_dev, 2 * DV)
    if n_dev < 256:
        table = jnp.concatenate([table, jnp.zeros((256 - n_dev, 2 * DV), F32)], axis=0)

    solve_scratch = [
        pltpu.VMEM((BLK, BLK, CC), F32), pltpu.VMEM((2, BLK, CC), F32), pltpu.VMEM((2, BLK, CC), F32)
    ]
    resid, local, up, down, main_f, side_f, tcell, dcell = call(
        functools.partial(first_kernel, last),
        [(6, EXT, CC), (6, EXT, CC), (6, 8, CC), (6, 8, CC), (6, FR, CC), (6, FR, CC), (2, FR, CC), (2, FR, CC)],
        [SMEM] + [VMEM] * 7 + [ANY],
        solve_scratch + [pltpu.VMEM((2, FR, CC), F32), pltpu.SemaphoreType.DMA(())],
    )(info, table, state, adjoint, design_map, side, from_up, from_down, blocks)

    join = call(
        functools.partial(join_kernel, last), [(6, FR, CC), (8, CC), (8, CC)], [SMEM] + [VMEM] * 3
    )
    zframe, first, end = join(info, local, *rows(down, up))
    image, zside, local, up, down = call(
        functools.partial(second_kernel, last),
        [(6, EXT, CC), (6, FR, CC), (6, EXT, CC), (6, 8, CC), (6, 8, CC)],
        [SMEM] + [VMEM] * 4 + [ANY],
        solve_scratch + [pltpu.SemaphoreType.DMA(())],
    )(info, zframe, *cols(end, first), tcell, blocks)
    wframe, first, end = join(info, local, *rows(down, up))
    (sums,) = call(
        third_kernel, [(256, 6 * CC)], [VMEM] * 12,
        [
            pltpu.VMEM((6, FR, CC), F32), pltpu.VMEM((256, CR * 2 * CC), BF16),
            pltpu.VMEM((5 * DV, CR * 2 * CC), BF16),
        ],
    )(design_map, resid, image, zframe, zside, wframe, *cols(end, first), tcell, dcell, main_f, side_f)
    got = lax.all_to_all(sums[:n_dev], BOTH, 0, 0, tiled=True)
    tangent, second, owned = call(
        last_kernel, [(3, CR, CC), (3, CR, CC), (1, CC)], [VMEM] * 3
    )(got, zframe, wframe)
    return tangent, second, owned.reshape(DV)


def solution(mesh):
    placed = (
        P(None, "prow", "pcol"),
        P(None, "prow", "pcol"),
        P(("prow", "pcol")),
        P(("prow", "pcol")),
        P("prow", "pcol"),
        P("prow", "pcol"),
        P("prow", None, "pcol"),
    )
    return jax.shard_map(
        per_device,
        mesh=mesh,
        in_specs=placed,
        out_specs=(P(None, "prow", "pcol"), P(None, "prow", "pcol"), P(("prow", "pcol"))),
        check_vma=False,
    )
```

```python
import functools

import jax
import jax.numpy as jnp
from jax import lax
from jax.experimental import pallas as pl
from jax.experimental.pallas import tpu as pltpu
from jax.sharding import PartitionSpec as P

CR = 22
CC = 128
DV = 128
BLK = 72
EXT = CR + 2
FR = 32
ROW = ("y", "core")
F32 = jnp.float32
BF16 = jnp.bfloat16

VMEM = pl.BlockSpec(memory_space=pltpu.VMEM)
SMEM = pl.BlockSpec(memory_space=pltpu.SMEM)
HBM = pl.BlockSpec(memory_space=pltpu.HBM)


def call(kernel, out_shapes, in_specs, scratch=(), out_specs=None):
    return pl.pallas_call(
        kernel,
        out_shape=[jax.ShapeDtypeStruct(s, F32) for s in out_shapes],
        in_specs=list(in_specs),
        out_specs=[VMEM] * len(out_shapes) if out_specs is None else out_specs,
        scratch_shapes=list(scratch),
        compiler_params=pltpu.CompilerParams(vmem_limit_bytes=20 * 1024 * 1024),
    )


def iota(shape, dim):
    return lax.broadcasted_iota(jnp.int32, shape, dim)


def pack_edges(tiles, width):
    lane = iota((8, CC), 1)
    first = jnp.zeros((8, CC), F32)
    last = jnp.zeros((8, CC), F32)
    for k, tile in enumerate(tiles):
        at = k * width
        here = (lane >= at) & (lane < at + width)
        first = jnp.where(here, pltpu.roll(tile, at, 1) if at else tile, first)
        last = jnp.where(here, pltpu.roll(tile, at + width, 1), last)
    return first, last


def unpack_edges(from_left, from_right, count, width):
    lane = iota((8, CC), 1)
    tiles = []
    for k in range(count):
        at = k * width
        right = pltpu.roll(from_right, CC - at, 1) if at else from_right
        shift = (CC - width - at) % CC
        left = pltpu.roll(from_left, shift, 1) if shift else from_left
        tiles.append(jnp.where(lane < width, right, jnp.where(lane >= CC - width, left, 0.0)))
    return tiles


def lanes_of(x):
    return iota(x.shape, x.ndim - 1)


def left_of(main, side):
    dim = main.ndim - 1
    return jnp.where(lanes_of(main) == 0, pltpu.roll(side, 1, dim), pltpu.roll(main, 1, dim))


def right_of(main, side):
    dim = main.ndim - 1
    return jnp.where(
        lanes_of(main) == CC - 1, pltpu.roll(side, CC - 1, dim), pltpu.roll(main, CC - 1, dim)
    )


def grid_mask(prow, last, start, rows):
    row = iota((rows, CC), 0) + (start - 8)
    outside = ((row < 0) & (prow == 0)) | ((row >= CR) & (prow == last))
    return jnp.where(outside, 0.0, 1.0).astype(F32)


def start_kernel(
    state, adjoint, dmap, thickness, direction, frame_out, own_out, first_out, last_out,
    known, cells, own, sem,
):
    copies = [
        pltpu.make_async_copy(thickness, own.at[0], sem.at[0]),
        pltpu.make_async_copy(direction, own.at[1], sem.at[1]),
        pltpu.make_async_copy(state, known.at[0:3], sem.at[2]),
        pltpu.make_async_copy(adjoint, known.at[3:6], sem.at[3]),
        pltpu.make_async_copy(dmap, cells, sem.at[4]),
    ]
    for copy in copies:
        copy.start()
    frame_out[...] = jnp.zeros_like(frame_out)
    for copy in copies:
        copy.wait()
    for k in range(2):
        own_out[:, k * DV:(k + 1) * DV] = jnp.broadcast_to(own[k], (own_out.shape[0], DV))
    frame_out[0:6, 8:8 + CR, :] = known[...]
    frame_out[6, 8:8 + CR, :] = cells[...].astype(F32)
    tiles = [frame_out[f, 8 + 8 * g:16 + 8 * g, :] for f in range(7) for g in range(3)]
    first, last = pack_edges(tiles, 1)
    first_out[...] = first
    last_out[...] = last


def rows_kernel(frame, from_left, from_right, table, side_out, up_out, down_out, table_out):
    tiles = unpack_edges(from_left[...], from_right[...], 21, 1)
    side_out[...] = jnp.zeros_like(side_out)
    for f in range(7):
        for g in range(3):
            side_out[f, 8 + 8 * g:16 + 8 * g, :] = tiles[3 * f + g]
    up_out[...] = jnp.zeros_like(up_out)
    down_out[...] = jnp.zeros_like(down_out)
    for tile, ref in ((0, frame), (1, side_out)):
        for f in range(7):
            up_out[tile, 2 * f:2 * f + 2, :] = ref[f, 8:10, :]
            down_out[tile, 2 * f:2 * f + 2, :] = ref[f, 6 + CR:8 + CR, :]
    table_out[...] = jnp.broadcast_to(table[...][None], table_out.shape)


def apply_blocks(mats, vec):
    def rows(step, carry):
        one, two = carry
        for u in range(8):
            at = step * 8 + u
            mat = mats[at]
            one = one + mat * vec[0, pl.ds(at, 1), :]
            two = two + mat * vec[1, pl.ds(at, 1), :]
        return one, two

    zero = jnp.zeros((BLK, CC), F32)
    return lax.fori_loop(0, BLK // 8, rows, (zero, zero))


def local_solve(mats, vec, total, level):
    one, two = apply_blocks(mats, vec)
    total[0] = one
    total[1] = two
    vec[0] = one
    vec[1] = two

    def further(_, carry):
        one, two = apply_blocks(mats, vec)
        one = 0.5 * one
        two = 0.5 * two
        vec[0] = one
        vec[1] = two
        total[0] += one
        total[1] += two
        return carry

    lax.fori_loop(1, level, further, 0)


def look_up(table, index, tcell, dcell):
    flipped = table[...].T
    part0 = flipped.astype(BF16)
    part1 = (flipped - part0.astype(F32)).astype(BF16)
    lhs = jnp.concatenate([part0, part1], axis=0)
    high = [ix // DV for ix in index]
    low = [ix % DV for ix in index]
    lane1 = iota((1, CC), 1)

    def both(vh, vl):
        hot = jnp.where(iota((256, 2 * CC), 0) == vh, 1.0, 0.0).astype(BF16)
        got = jnp.dot(lhs, hot, preferred_element_type=F32)
        mine = iota((DV, 2 * CC), 0) == vl
        tv = jnp.sum(jnp.where(mine, got[0:DV] + got[2 * DV:3 * DV], 0.0), axis=0, keepdims=True)
        dv = jnp.sum(jnp.where(mine, got[DV:2 * DV] + got[3 * DV:4 * DV], 0.0), axis=0, keepdims=True)
        return tv, dv

    for r in range(6, FR, 2):
        vh = jnp.concatenate([high[0][r:r + 1], high[0][r + 1:r + 2]], axis=1)
        vl = jnp.concatenate([low[0][r:r + 1], low[0][r + 1:r + 2]], axis=1)
        tv, dv = both(vh, vl)
        for h in range(2):
            tcell[0, r + h:r + h + 1, :] = tv[:, h * CC:(h + 1) * CC]
            dcell[0, r + h:r + h + 1, :] = dv[:, h * CC:(h + 1) * CC]
    packs = []
    for half in range(2):
        vec = jnp.zeros((1, CC), jnp.int32)
        for i in range(16):
            r = 16 * half + i
            vec = jnp.where(lane1 // 8 == i, pltpu.roll(index[1][r:r + 1], (8 * i + 4) % CC, 1), vec)
        packs.append(vec)
    vec = jnp.concatenate(packs, axis=1)
    tv, dv = both(vec // DV, vec % DV)
    for half in range(2):
        for i in range(16):
            r = 16 * half + i
            shift = (CC - 8 * i - 4) % CC
            keep = (lane1 < 4) | (lane1 >= CC - 4)
            cut = slice(half * CC, (half + 1) * CC)
            tcell[1, r:r + 1, :] = jnp.where(keep, pltpu.roll(tv[:, cut], shift, 1), 0.0)
            dcell[1, r:r + 1, :] = jnp.where(keep, pltpu.roll(dv[:, cut], shift, 1), 0.0)


def weights_of(main, side, lo, hi):
    here = main[lo:hi]
    return [
        0.5 * (here + main[lo - 1:hi - 1]),
        0.5 * (here + main[lo + 1:hi + 1]),
        0.5 * (here + left_of(here, side[lo:hi])),
        0.5 * (here + right_of(here, side[lo:hi])),
    ]


def differences(main, side, lo, hi):
    here = main[:, lo:hi, :]
    beside = side[:, lo:hi, :]
    return [
        here - main[:, lo - 1:hi - 1, :],
        here - main[:, lo + 1:hi + 1, :],
        here - left_of(here, beside),
        here - right_of(here, beside),
    ]


def first_kernel(
    last, info, table, frame, side, from_up, from_down, blocks,
    resid_out, local_out, up_out, down_out, main_f, side_f, tcell, dcell, mats,
    vec, total, index_scr, sem,
):
    copy = pltpu.make_async_copy(blocks, mats, sem)
    copy.start()
    level, prow = info[0], info[1]
    inside = grid_mask(prow, last, 0, FR)
    for tile, ref, source in ((0, main_f, frame), (1, side_f, side)):
        for f in range(7):
            out = ref.at[f] if f < 6 else index_scr.at[tile]
            out[...] = source[f]
            out[6:8, :] = from_up[tile, 2 * f:2 * f + 2, :] * inside[6:8]
            out[8 + CR:10 + CR, :] = from_down[tile, 2 * f:2 * f + 2, :] * inside[8 + CR:10 + CR]
    index = [index_scr[tile].astype(jnp.int32) for tile in range(2)]
    tcell[...] = jnp.zeros_like(tcell)
    dcell[...] = jnp.zeros_like(dcell)
    look_up(table, index, tcell, dcell)
    for tile in range(2):
        tcell[tile] = tcell[tile] * inside
    slope = [3.0 * tcell[tile] * tcell[tile] * dcell[tile] for tile in range(2)]
    lo, hi = 7, 7 + EXT
    parts = differences(main_f, side_f, lo, hi)
    rhs = jnp.zeros((6, EXT, CC), F32)
    for weight, diff in zip(weights_of(slope[0], slope[1], lo, hi), parts):
        rhs = rhs - weight[None] * diff
    rhs = rhs * inside[lo:hi][None]
    resid_out[...] = rhs
    vec[...] = rhs.reshape(2, BLK, CC)
    copy.wait()
    local_solve(mats, vec, total, level)
    local = total[...].reshape(6, EXT, CC)
    local_out[...] = local
    up_out[...] = local[:, 0:8, :]
    down_out[...] = local[:, EXT - 8:EXT, :]


def join_kernel(last, info, local, from_up, from_down, frame_out, first_out, last_out):
    prow = info[1]
    frame_out[...] = jnp.zeros_like(frame_out)
    frame_out[:, 7:7 + EXT, :] = local[...]
    frame_out[:, 6:9, :] += jnp.where(prow == 0, 0.0, from_up[:, 5:8, :])
    frame_out[:, 7 + CR:10 + CR, :] += jnp.where(prow == last, 0.0, from_down[:, 0:3, :])
    inside = grid_mask(prow, last, 0, FR)
    frame_out[...] = frame_out[...] * inside[None]
    tiles = []
    for f in range(6):
        field = frame_out[f, 7:7 + EXT, :]
        tiles += [field[8 * g:8 * g + 8] for g in range(3)]
    first, last_lanes = pack_edges(tiles, 1)
    first_out[...] = first
    last_out[...] = last_lanes


def fill_side(side_f, from_left, from_right):
    tiles = unpack_edges(from_left[...], from_right[...], 18, 1)
    side_f[...] = jnp.zeros_like(side_f)
    for f in range(6):
        for g in range(3):
            side_f[f, 7 + 8 * g:15 + 8 * g, :] = tiles[3 * f + g]


def stiffness(main_f, side_f, tcell, lo, hi):
    stiff = [tcell[tile] * tcell[tile] * tcell[tile] for tile in range(2)]
    out = main_f[:, lo:hi, :]
    parts = differences(main_f, side_f, lo, hi)
    for weight, diff in zip(weights_of(stiff[0], stiff[1], lo, hi), parts):
        out = out + weight[None] * diff
    return out


def second_kernel(
    last, info, frame, from_left, from_right, tcell, mats,
    image_out, side_out, local_out, up_out, down_out, vec, total,
):
    level, prow = info[0], info[1]
    fill_side(side_out, from_left, from_right)
    lo, hi = 7, 7 + EXT
    image = stiffness(frame, side_out, tcell, lo, hi)
    image = image * grid_mask(prow, last, lo, EXT)[None]
    image_out[...] = image
    vec[...] = image.reshape(2, BLK, CC)
    local_solve(mats, vec, total, level)
    local = total[...].reshape(6, EXT, CC)
    local_out[...] = local
    up_out[...] = local[:, 0:8, :]
    down_out[...] = local[:, EXT - 8:EXT, :]


def third_kernel(
    n_col, info, frame, resid, image, zframe, zside, wframe, from_left, from_right, tcell, dcell, main_f, side_f,
    keep_out, send_out, wside, left_op, right_op,
):
    fill_side(wside, from_left, from_right)
    lo, hi = 8, 8 + CR
    v = stiffness(wframe, wside, tcell, lo, hi)
    r = resid[:, 1:1 + CR, :]
    q = image[:, 1:1 + CR, :]
    z = zframe[:, lo:hi, :]
    w = wframe[:, lo:hi, :]
    lane = iota((1, CC), 1)
    dots = jnp.zeros((1, CC), F32)
    pairs = ((r, z), (z, q), (r, w), (q, w), (z, v), (w, v))
    for k, (a, b) in enumerate(pairs):
        ab = a * b
        for s in range(2):
            part = ab[3 * s] + ab[3 * s + 1] + ab[3 * s + 2]
            value = jnp.sum(jnp.sum(part, axis=0, keepdims=True), axis=1, keepdims=True)
            dots = jnp.where(lane == 2 * k + s, value, dots)
    t = tcell[0, lo:hi, :]
    d = dcell[0, lo:hi, :]
    known_d = differences(main_f, side_f, lo, hi)
    z_d = differences(zframe, zside, lo, hi)
    w_d = differences(wframe, wside, lo, hi)

    def dot3(a, b, i, j):
        out = jnp.zeros((CR, CC), F32)
        for an, bn in zip(a, b):
            for c in range(3):
                out = out + an[i + c] * bn[j + c]
        return out

    slope2 = -1.5 * t * t
    values = [
        (-3.0 * t * d) * dot3(known_d, known_d, 3, 0),
        slope2 * dot3(z_d, known_d, 3, 0),
        slope2 * dot3(w_d, known_d, 3, 0),
        slope2 * dot3(known_d, z_d, 3, 0),
        slope2 * dot3(known_d, w_d, 3, 0),
    ]
    cells = frame[6, lo:hi, :].astype(jnp.int32)
    owner = cells // DV
    low = cells % DV
    other = jnp.where((owner // n_col) % 2 == info[1] % 2, 0, 128)
    high = other + (owner // (2 * n_col)) * n_col + owner % n_col
    for row in range(CR):
        hot = jnp.where(iota((256, CC), 0) == high[row:row + 1], 1.0, 0.0).astype(BF16)
        at = 2 * CC * row
        left_op[:, at:at + CC] = hot
        left_op[:, at + CC:at + 2 * CC] = hot
        mine = iota((DV, CC), 0) == low[row:row + 1]
        for k, value in enumerate(values):
            one = value[row:row + 1]
            top = one.astype(BF16).astype(F32)
            right_op[k * DV:(k + 1) * DV, at:at + CC] = jnp.where(mine, top, 0.0).astype(BF16)
            right_op[k * DV:(k + 1) * DV, at + CC:at + 2 * CC] = jnp.where(mine, one - top, 0.0).astype(BF16)
    sums = lax.dot_general(
        left_op[...], right_op[...], (((1,), (1,)), ((), ())), preferred_element_type=F32
    )
    for half, out in ((0, keep_out), (1, send_out)):
        count = out.shape[0]
        out[:, 0:CC] = jnp.broadcast_to(dots, (count, CC))
        out[:, CC:] = sums[128 * half:128 * half + count]


def last_kernel(got, zframe, wframe, tangent, second, owned):
    sums = jnp.sum(got[...], axis=0, keepdims=True)
    dots = sums[:, 0:CC]
    lane = iota((1, CC), 1)

    def pick(k):
        return jnp.sum(jnp.where(lane == k, dots, 0.0), axis=1, keepdims=True)

    coeffs = []
    for s in range(2):
        rz, zq, rw, qw, zv, wv = (pick(2 * k + s) for k in range(6))
        alpha = rz / zq
        rz1 = rz - alpha * (zq + rw) + alpha * alpha * qw
        grow = 1.0 + rz1 / rz
        pq = grow * grow * zq - grow * alpha * (zv + qw) + alpha * alpha * wv
        alpha1 = rz1 / pq
        coeffs.append((alpha + alpha1 * grow, -alpha1 * alpha))
    for s, out in ((0, tangent), (1, second)):
        c0, c1 = coeffs[s]
        for f in range(3):
            out[f] = c0 * zframe[3 * s + f, 8:8 + CR, :] + c1 * wframe[3 * s + f, 8:8 + CR, :]
    h = [sums[:, (k + 1) * CC:(k + 2) * CC] for k in range(5)]
    owned[...] = (
        h[0] + coeffs[1][0] * h[1] + coeffs[1][1] * h[2] + coeffs[0][0] * h[3] + coeffs[0][1] * h[4]
    )


def ring(axis, count, to_next, to_previous):
    forward = [(i, (i + 1) % count) for i in range(count)]
    backward = [(b, a) for a, b in forward]
    return lax.ppermute(to_next, axis, forward), lax.ppermute(to_previous, axis, backward)


def per_device(state, adjoint, thickness, direction, design_map, levels, blocks):
    n_row, n_col = lax.axis_size(ROW), lax.axis_size("pcol")
    n_dev = n_row * n_col
    last = n_row - 1
    info = jnp.stack([levels[0, 0], lax.axis_index(ROW).astype(jnp.int32)])
    rows = functools.partial(ring, ROW, n_row)
    cols = functools.partial(ring, "pcol", n_col)

    frame, own, first, end = call(
        start_kernel, [(7, FR, CC), (n_col, 2 * DV), (8, CC), (8, CC)], [HBM] * 5,
        [
            pltpu.VMEM((6, CR, CC), F32), pltpu.VMEM((CR, CC), jnp.int32),
            pltpu.VMEM((2, 1, DV), F32), pltpu.SemaphoreType.DMA((5,)),
        ],
    )(state, adjoint, design_map, thickness.reshape(1, DV), direction.reshape(1, DV))
    from_left, from_right = cols(end, first)
    table = lax.all_to_all(own, "pcol", 0, 0, tiled=True)
    side, up, down, table = call(
        rows_kernel, [(7, FR, CC), (2, 16, CC), (2, 16, CC), (n_row, n_col, 2 * DV)], [VMEM] * 4,
    )(frame, from_left, from_right, table)
    from_up, from_down = rows(down, up)
    table = lax.all_to_all(table, ROW, 0, 0, tiled=True).reshape(n_dev, 2 * DV)
    if n_dev < 256:
        table = jnp.concatenate([table, jnp.zeros((256 - n_dev, 2 * DV), F32)], axis=0)

    solve_scratch = [pltpu.VMEM((2, BLK, CC), F32), pltpu.VMEM((2, BLK, CC), F32)]
    resid, local, up, down, main_f, side_f, tcell, dcell, mats = call(
        functools.partial(first_kernel, last),
        [
            (6, EXT, CC), (6, EXT, CC), (6, 8, CC), (6, 8, CC), (6, FR, CC), (6, FR, CC),
            (2, FR, CC), (2, FR, CC), (BLK, BLK, CC),
        ],
        [SMEM] + [VMEM] * 5 + [HBM],
        solve_scratch + [pltpu.VMEM((2, FR, CC), F32), pltpu.SemaphoreType.DMA(())],
    )(info, table, frame, side, from_up, from_down, blocks)

    join = call(
        functools.partial(join_kernel, last), [(6, FR, CC), (8, CC), (8, CC)], [SMEM] + [VMEM] * 3
    )
    zframe, first, end = join(info, local, *rows(down, up))
    image, zside, local, up, down = call(
        functools.partial(second_kernel, last),
        [(6, EXT, CC), (6, FR, CC), (6, EXT, CC), (6, 8, CC), (6, 8, CC)],
        [SMEM] + [VMEM] * 5,
        solve_scratch,
    )(info, zframe, *cols(end, first), tcell, mats)
    wframe, first, end = join(info, local, *rows(down, up))
    keep, send = call(
        functools.partial(third_kernel, n_col), [(n_dev // 2, 6 * CC)] * 2, [SMEM] + [VMEM] * 12,
        [
            pltpu.VMEM((6, FR, CC), F32), pltpu.VMEM((256, CR * 2 * CC), BF16),
            pltpu.VMEM((5 * DV, CR * 2 * CC), BF16),
        ],
    )(info, frame, resid, image, zframe, zside, wframe, *cols(end, first), tcell, dcell, main_f, side_f)
    sums = keep + lax.ppermute(send, "core", [(0, 1), (1, 0)])
    got = lax.all_to_all(sums, ("y", "pcol"), 0, 0, tiled=True)
    tangent, second, owned = call(
        last_kernel, [(3, CR, CC), (3, CR, CC), (1, CC)], [VMEM] * 3
    )(got, zframe, wframe)
    return tangent, second, owned.reshape(DV)


def solution(mesh):
    n_row, n_col = mesh.devices.shape
    fine = jax.sharding.Mesh(mesh.devices.reshape(n_row // 2, 2, n_col), ("y", "core", "pcol"))
    field = P(None, ROW, "pcol")
    design = P(("y", "core", "pcol"))
    return jax.shard_map(
        per_device,
        mesh=fine,
        in_specs=(field, field, design, design, P(ROW, "pcol"), P(ROW, "pcol"), P(ROW, None, "pcol")),
        out_specs=(field, field, design),
        check_vma=False,
    )
```

```python
import functools

import jax
import jax.numpy as jnp
from jax import lax
from jax.experimental import pallas as pl
from jax.experimental.pallas import tpu as pltpu
from jax.sharding import PartitionSpec as P

CR = 22
CC = 128
DV = 128
BLK = 72
EXT = CR + 2
FR = 32
ROW = ("y", "core")
WIDE = 3
HALVES = (4, 8, 16, 32, 64)
F32 = jnp.float32
BF16 = jnp.bfloat16

VMEM = pl.BlockSpec(memory_space=pltpu.VMEM)
SMEM = pl.BlockSpec(memory_space=pltpu.SMEM)


def call(kernel, out_shapes, in_specs, scratch=(), out_specs=None):
    return pl.pallas_call(
        kernel,
        out_shape=[jax.ShapeDtypeStruct(s, F32) for s in out_shapes],
        in_specs=list(in_specs),
        out_specs=[VMEM] * len(out_shapes) if out_specs is None else out_specs,
        scratch_shapes=list(scratch),
        compiler_params=pltpu.CompilerParams(vmem_limit_bytes=20 * 1024 * 1024),
    )


def iota(shape, dim):
    return lax.broadcasted_iota(jnp.int32, shape, dim)


def pack_edges(tiles, width):
    lane = iota((8, CC), 1)
    first = jnp.zeros((8, CC), F32)
    last = jnp.zeros((8, CC), F32)
    for k, tile in enumerate(tiles):
        at = k * width
        here = (lane >= at) & (lane < at + width)
        first = jnp.where(here, pltpu.roll(tile, at, 1) if at else tile, first)
        last = jnp.where(here, pltpu.roll(tile, at + width, 1), last)
    return first, last


def unpack_edges(from_left, from_right, count, width):
    lane = iota((8, CC), 1)
    tiles = []
    for k in range(count):
        at = k * width
        right = pltpu.roll(from_right, CC - at, 1) if at else from_right
        shift = (CC - width - at) % CC
        left = pltpu.roll(from_left, shift, 1) if shift else from_left
        tiles.append(jnp.where(lane < width, right, jnp.where(lane >= CC - width, left, 0.0)))
    return tiles


def lanes_of(x):
    return iota(x.shape, x.ndim - 1)


def left_of(main, side):
    dim = main.ndim - 1
    return jnp.where(lanes_of(main) == 0, pltpu.roll(side, 1, dim), pltpu.roll(main, 1, dim))


def right_of(main, side):
    dim = main.ndim - 1
    return jnp.where(
        lanes_of(main) == CC - 1, pltpu.roll(side, CC - 1, dim), pltpu.roll(main, CC - 1, dim)
    )


def grid_mask(prow, last, start, rows):
    row = iota((rows, CC), 0) + (start - 8)
    outside = ((row < 0) & (prow == 0)) | ((row >= CR) & (prow == last))
    return jnp.where(outside, 0.0, 1.0).astype(F32)


def start_kernel(info, state, adjoint, dmap, mats, frame_out, first_out, last_out, edge_out):
    frame_out[...] = jnp.zeros_like(frame_out)
    frame_out[0:3, 8:8 + CR, :] = state[...]
    frame_out[3:6, 8:8 + CR, :] = adjoint[...]
    frame_out[6, 8:8 + CR, :] = dmap[...].astype(F32)
    tiles = [frame_out[f, 8 + 8 * g:16 + 8 * g, :] for f in range(7) for g in range(3)]
    first, last = pack_edges(tiles, WIDE)
    upper = iota((8, CC), 1) >= 64
    level = info[0].astype(F32)
    first_out[...] = jnp.where(upper, level, first)
    last_out[...] = jnp.where(upper, level, last)
    lane = iota((BLK, CC), 1)
    for c in range(3):
        packed = jnp.zeros((BLK, CC), F32)
        for i in range(min(32, BLK - 32 * c)):
            mat = mats[32 * c + i]
            here = ((lane - 4 * i + 2) & (CC - 1)) < 4
            packed = jnp.where(here, pltpu.roll(mat, 4 * i, 1) if i else mat, packed)
        edge_out[c] = packed


def rows_kernel(
    frame, from_left, from_right, left_edge, right_edge,
    side_out, up_out, down_out, edge_out, levels_out,
):
    tiles = unpack_edges(from_left[...], from_right[...], 21, WIDE)
    side_out[...] = jnp.zeros_like(side_out)
    for f in range(7):
        for g in range(3):
            side_out[f, 8 + 8 * g:16 + 8 * g, :] = tiles[3 * f + g]
    up_out[...] = jnp.zeros_like(up_out)
    down_out[...] = jnp.zeros_like(down_out)
    for tile, ref in ((0, frame), (1, side_out)):
        for f in range(7):
            up_out[tile, 2 * f:2 * f + 2, :] = ref[f, 8:10, :]
            down_out[tile, 2 * f:2 * f + 2, :] = ref[f, 6 + CR:8 + CR, :]
    upper = iota((8, CC), 1) >= 64
    levels_out[...] = jnp.where(upper, from_left[...], pltpu.roll(from_right[...], 64, 1))
    lane = iota((BLK, CC), 1)
    for c in range(3):
        edge_out[c] = jnp.where(lane % 4 < 2, right_edge[c], pltpu.roll(left_edge[c], 4, 1))


def apply_blocks(mats, vec):
    def rows(step, carry):
        one, two = carry
        for u in range(8):
            at = step * 8 + u
            mat = mats[at]
            one = one + mat * vec[0, pl.ds(at, 1), :]
            two = two + mat * vec[1, pl.ds(at, 1), :]
        return one, two

    zero = jnp.zeros((BLK, CC), F32)
    return lax.fori_loop(0, BLK // 8, rows, (zero, zero))


def over_columns(x):
    for shift in HALVES:
        x = x + pltpu.roll(x, shift, 1)
    return x


def apply_edge(edge, vec):
    row = iota((BLK, CC), 0)
    place = iota((BLK, CC), 1) // 4
    out = jnp.zeros((BLK, CC), F32)
    for c in range(3):
        low, high = 32 * c, min(32 * c + 32, BLK)
        mine = row[low:high] == place[low:high] + 32 * c
        flat = jnp.sum(jnp.where(mine, vec[low:high], 0.0), axis=0, keepdims=True)
        out = out + edge[c] * flat
    return over_columns(out)


def local_solve(mats, edge, vec, total, side_vec, side_total, level, levels):
    lane = iota((BLK, CC), 1)
    ours = (lane < 2) | (lane >= CC - 2)
    for n in range(2):
        side_vec[n] = over_columns(jnp.where(ours, side_vec[n], 0.0))
    total[...] = jnp.zeros_like(total)
    side_total[...] = jnp.zeros_like(side_total)
    top = jnp.maximum(level, jnp.max(levels[...]).astype(jnp.int32))

    def term(order, carry):
        scale = jnp.where(order == 0, 1.0, 0.5).astype(F32)
        keep = jnp.where(order < level, 1.0, 0.0).astype(F32)
        side_keep = levels[0:1, :] > order.astype(F32)
        for n in range(2):
            out = scale * apply_edge(edge, side_vec[n])
            side_vec[n] = out
            side_total[n] += jnp.where(side_keep, out, 0.0)
        for n, out in enumerate(apply_blocks(mats, vec)):
            out = scale * out
            vec[n] = out
            total[n] += keep * out
        return carry

    lax.fori_loop(0, top, term, 0)


def put_results(total, side_total, local_out, up_out, down_out):
    up_out[...] = jnp.zeros_like(up_out)
    down_out[...] = jnp.zeros_like(down_out)
    for tile, ref in ((0, total), (1, side_total)):
        local_out[tile] = ref[...].reshape(6, EXT, CC)
        for f in range(6):
            up_out[tile, 3 * f:3 * f + 3, :] = local_out[tile, f, 0:3, :]
            down_out[tile, 3 * f:3 * f + 3, :] = local_out[tile, f, EXT - 3:EXT, :]


def join(prow, last, local, from_up, from_down, frames):
    inside = grid_mask(prow, last, 0, FR)
    for tile, frame in enumerate(frames):
        frame[...] = jnp.zeros_like(frame)
        frame[:, 7:7 + EXT, :] = local[tile]
        for f in range(6):
            frame[f, 6:9, :] += jnp.where(prow == 0, 0.0, from_up[tile, 3 * f:3 * f + 3, :])
            frame[f, 7 + CR:10 + CR, :] += jnp.where(prow == last, 0.0, from_down[tile, 3 * f:3 * f + 3, :])
        frame[...] = frame[...] * inside[None]


def look_up(table, index, tcell, dcell):
    flipped = table[...].T
    part0 = flipped.astype(BF16)
    part1 = (flipped - part0.astype(F32)).astype(BF16)
    lhs = jnp.concatenate([part0, part1], axis=0)
    high = [ix // DV for ix in index]
    low = [ix % DV for ix in index]
    lane1 = iota((1, CC), 1)

    def both(vh, vl):
        hot = jnp.where(iota((256, 2 * CC), 0) == vh, 1.0, 0.0).astype(BF16)
        got = jnp.dot(lhs, hot, preferred_element_type=F32)
        mine = iota((DV, 2 * CC), 0) == vl
        tv = jnp.sum(jnp.where(mine, got[0:DV] + got[2 * DV:3 * DV], 0.0), axis=0, keepdims=True)
        dv = jnp.sum(jnp.where(mine, got[DV:2 * DV] + got[3 * DV:4 * DV], 0.0), axis=0, keepdims=True)
        return tv, dv

    for r in range(6, FR, 2):
        vh = jnp.concatenate([high[0][r:r + 1], high[0][r + 1:r + 2]], axis=1)
        vl = jnp.concatenate([low[0][r:r + 1], low[0][r + 1:r + 2]], axis=1)
        tv, dv = both(vh, vl)
        for h in range(2):
            tcell[0, r + h:r + h + 1, :] = tv[:, h * CC:(h + 1) * CC]
            dcell[0, r + h:r + h + 1, :] = dv[:, h * CC:(h + 1) * CC]
    packs = []
    for half in range(2):
        vec = jnp.zeros((1, CC), jnp.int32)
        for i in range(16):
            r = 16 * half + i
            vec = jnp.where(lane1 // 8 == i, pltpu.roll(index[1][r:r + 1], (8 * i + 4) % CC, 1), vec)
        packs.append(vec)
    vec = jnp.concatenate(packs, axis=1)
    tv, dv = both(vec // DV, vec % DV)
    for half in range(2):
        for i in range(16):
            r = 16 * half + i
            shift = (CC - 8 * i - 4) % CC
            keep = (lane1 < 4) | (lane1 >= CC - 4)
            cut = slice(half * CC, (half + 1) * CC)
            tcell[1, r:r + 1, :] = jnp.where(keep, pltpu.roll(tv[:, cut], shift, 1), 0.0)
            dcell[1, r:r + 1, :] = jnp.where(keep, pltpu.roll(dv[:, cut], shift, 1), 0.0)


def weights_of(main, side, lo, hi):
    here = main[lo:hi]
    return [
        0.5 * (here + main[lo - 1:hi - 1]),
        0.5 * (here + main[lo + 1:hi + 1]),
        0.5 * (here + left_of(here, side[lo:hi])),
        0.5 * (here + right_of(here, side[lo:hi])),
    ]


def differences(main, side, lo, hi):
    here = main[:, lo:hi, :]
    beside = side[:, lo:hi, :]
    return [
        here - main[:, lo - 1:hi - 1, :],
        here - main[:, lo + 1:hi + 1, :],
        here - left_of(here, beside),
        here - right_of(here, beside),
    ]


def first_kernel(
    last, info, table, frame, side, from_up, from_down, mats, edge, levels,
    resid_out, local_out, up_out, down_out, main_f, side_f, tcell, dcell,
    vec, total, side_vec, side_total, index_scr,
):
    level, prow = info[0], info[1]
    inside = grid_mask(prow, last, 0, FR)
    for tile, ref, source in ((0, main_f, frame), (1, side_f, side)):
        for f in range(7):
            out = ref.at[f] if f < 6 else index_scr.at[tile]
            out[...] = source[f]
            out[6:8, :] = from_up[tile, 2 * f:2 * f + 2, :] * inside[6:8]
            out[8 + CR:10 + CR, :] = from_down[tile, 2 * f:2 * f + 2, :] * inside[8 + CR:10 + CR]
    index = [index_scr[tile].astype(jnp.int32) for tile in range(2)]
    tcell[...] = jnp.zeros_like(tcell)
    dcell[...] = jnp.zeros_like(dcell)
    look_up(table, index, tcell, dcell)
    for tile in range(2):
        tcell[tile] = tcell[tile] * inside
    slope = [3.0 * tcell[tile] * tcell[tile] * dcell[tile] for tile in range(2)]
    lo, hi = 7, 7 + EXT
    frames = (main_f, side_f)
    for tile, out in ((0, vec), (1, side_vec)):
        here, beside = frames[tile], frames[1 - tile]
        rhs = jnp.zeros((6, EXT, CC), F32)
        for weight, diff in zip(
            weights_of(slope[tile], slope[1 - tile], lo, hi), differences(here, beside, lo, hi)
        ):
            rhs = rhs - weight[None] * diff
        rhs = rhs * inside[lo:hi][None]
        if tile == 0:
            resid_out[...] = rhs
        out[...] = rhs.reshape(2, BLK, CC)
    local_solve(mats, edge, vec, total, side_vec, side_total, level, levels)
    put_results(total, side_total, local_out, up_out, down_out)


def stiffness(main_f, side_f, main_t, side_t, lo, hi):
    stiff = [t * t * t for t in (main_t[...], side_t[...])]
    out = main_f[:, lo:hi, :]
    parts = differences(main_f, side_f, lo, hi)
    for weight, diff in zip(weights_of(stiff[0], stiff[1], lo, hi), parts):
        out = out + weight[None] * diff
    return out


def second_kernel(
    last, info, local, from_up, from_down, tcell, mats, edge, levels,
    main_f, side_f, image_out, local_out, up_out, down_out, vec, total, side_vec, side_total,
):
    level, prow = info[0], info[1]
    frames = (main_f, side_f)
    join(prow, last, local, from_up, from_down, frames)
    lo, hi = 7, 7 + EXT
    inside = grid_mask(prow, last, lo, EXT)
    for tile, out in ((0, vec), (1, side_vec)):
        image = stiffness(
            frames[tile], frames[1 - tile], tcell.at[tile], tcell.at[1 - tile], lo, hi
        ) * inside[None]
        if tile == 0:
            image_out[...] = image
        out[...] = image.reshape(2, BLK, CC)
    local_solve(mats, edge, vec, total, side_vec, side_total, level, levels)
    put_results(total, side_total, local_out, up_out, down_out)


def third_kernel(
    last, n_col, info, frame, resid, image, zframe, zside, local, from_up, from_down,
    tcell, dcell, main_f, side_f,
    wframe, keep_out, send_out, wside, left_op, right_op,
):
    join(info[1], last, local, from_up, from_down, (wframe, wside))
    lo, hi = 8, 8 + CR
    v = stiffness(wframe, wside, tcell.at[0], tcell.at[1], lo, hi)
    r = resid[:, 1:1 + CR, :]
    q = image[:, 1:1 + CR, :]
    z = zframe[:, lo:hi, :]
    w = wframe[:, lo:hi, :]
    lane = iota((1, CC), 1)
    dots = jnp.zeros((1, CC), F32)
    pairs = ((r, z), (z, q), (r, w), (q, w), (z, v), (w, v))
    for k, (a, b) in enumerate(pairs):
        ab = a * b
        for s in range(2):
            part = ab[3 * s] + ab[3 * s + 1] + ab[3 * s + 2]
            value = jnp.sum(jnp.sum(part, axis=0, keepdims=True), axis=1, keepdims=True)
            dots = jnp.where(lane == 2 * k + s, value, dots)
    t = tcell[0, lo:hi, :]
    d = dcell[0, lo:hi, :]
    known_d = differences(main_f, side_f, lo, hi)
    z_d = differences(zframe, zside, lo, hi)
    w_d = differences(wframe, wside, lo, hi)

    def dot3(a, b, i, j):
        out = jnp.zeros((CR, CC), F32)
        for an, bn in zip(a, b):
            for c in range(3):
                out = out + an[i + c] * bn[j + c]
        return out

    slope2 = -1.5 * t * t
    values = [
        (-3.0 * t * d) * dot3(known_d, known_d, 3, 0),
        slope2 * dot3(z_d, known_d, 3, 0),
        slope2 * dot3(w_d, known_d, 3, 0),
        slope2 * dot3(known_d, z_d, 3, 0),
        slope2 * dot3(known_d, w_d, 3, 0),
    ]
    cells = frame[6, lo:hi, :].astype(jnp.int32)
    owner = cells // DV
    low = cells % DV
    other = jnp.where((owner // n_col) % 2 == info[1] % 2, 0, 128)
    high = other + (owner // (2 * n_col)) * n_col + owner % n_col
    for row in range(CR):
        hot = jnp.where(iota((256, CC), 0) == high[row:row + 1], 1.0, 0.0).astype(BF16)
        at = 2 * CC * row
        left_op[:, at:at + CC] = hot
        left_op[:, at + CC:at + 2 * CC] = hot
        mine = iota((DV, CC), 0) == low[row:row + 1]
        for k, value in enumerate(values):
            one = value[row:row + 1]
            top = one.astype(BF16).astype(F32)
            right_op[k * DV:(k + 1) * DV, at:at + CC] = jnp.where(mine, top, 0.0).astype(BF16)
            right_op[k * DV:(k + 1) * DV, at + CC:at + 2 * CC] = jnp.where(mine, one - top, 0.0).astype(BF16)
    sums = lax.dot_general(
        left_op[...], right_op[...], (((1,), (1,)), ((), ())), preferred_element_type=F32
    )
    for half, out in ((0, keep_out), (1, send_out)):
        count = out.shape[0]
        out[:, 0:CC] = jnp.broadcast_to(dots, (count, CC))
        out[:, CC:] = sums[128 * half:128 * half + count]


def last_kernel(got, zframe, wframe, tangent, second, owned):
    sums = jnp.sum(got[...], axis=0, keepdims=True)
    dots = sums[:, 0:CC]
    lane = iota((1, CC), 1)

    def pick(k):
        return jnp.sum(jnp.where(lane == k, dots, 0.0), axis=1, keepdims=True)

    coeffs = []
    for s in range(2):
        rz, zq, rw, qw, zv, wv = (pick(2 * k + s) for k in range(6))
        alpha = rz / zq
        rz1 = rz - alpha * (zq + rw) + alpha * alpha * qw
        grow = 1.0 + rz1 / rz
        pq = grow * grow * zq - grow * alpha * (zv + qw) + alpha * alpha * wv
        alpha1 = rz1 / pq
        coeffs.append((alpha + alpha1 * grow, -alpha1 * alpha))
    for s, out in ((0, tangent), (1, second)):
        c0, c1 = coeffs[s]
        for f in range(3):
            out[f] = c0 * zframe[3 * s + f, 8:8 + CR, :] + c1 * wframe[3 * s + f, 8:8 + CR, :]
    h = [sums[:, (k + 1) * CC:(k + 2) * CC] for k in range(5)]
    owned[...] = (
        h[0] + coeffs[1][0] * h[1] + coeffs[1][1] * h[2] + coeffs[0][0] * h[3] + coeffs[0][1] * h[4]
    )


def ring(axis, count, to_next, to_previous):
    forward = [(i, (i + 1) % count) for i in range(count)]
    backward = [(b, a) for a, b in forward]
    return lax.ppermute(to_next, axis, forward), lax.ppermute(to_previous, axis, backward)


def per_device(state, adjoint, thickness, direction, design_map, levels, blocks):
    n_row, n_col = lax.axis_size(ROW), lax.axis_size("pcol")
    n_dev = n_row * n_col
    last = n_row - 1
    info = jnp.stack([levels[0, 0], lax.axis_index(ROW).astype(jnp.int32)])
    rows = functools.partial(ring, ROW, n_row)
    cols = functools.partial(ring, "pcol", n_col)

    own = jnp.concatenate([thickness, direction])
    table = lax.all_to_all(
        jnp.broadcast_to(own[None], (n_dev, 2 * DV)), ROW + ("pcol",), 0, 0, tiled=True
    )
    if n_dev < 256:
        table = jnp.concatenate([table, jnp.zeros((256 - n_dev, 2 * DV), F32)], axis=0)
    frame, first, end, edge = call(
        start_kernel, [(7, FR, CC), (8, CC), (8, CC), (3, BLK, CC)], [SMEM] + [VMEM] * 4
    )(info, state, adjoint, design_map, blocks)
    side, up, down, edge, around = call(
        rows_kernel, [(7, FR, CC), (2, 16, CC), (2, 16, CC), (3, BLK, CC), (8, CC)], [VMEM] * 5
    )(frame, *cols(end, first), *cols(edge, edge))

    solve_scratch = [pltpu.VMEM((2, BLK, CC), F32)] * 4
    resid, local, up, down, main_f, side_f, tcell, dcell = call(
        functools.partial(first_kernel, last),
        [
            (6, EXT, CC), (2, 6, EXT, CC), (2, 24, CC), (2, 24, CC), (6, FR, CC), (6, FR, CC),
            (2, FR, CC), (2, FR, CC),
        ],
        [SMEM] + [VMEM] * 8,
        solve_scratch + [pltpu.VMEM((2, FR, CC), F32)],
    )(info, table, frame, side, *rows(down, up), blocks, edge, around)
    zframe, zside, image, local, up, down = call(
        functools.partial(second_kernel, last),
        [(6, FR, CC), (6, FR, CC), (6, EXT, CC), (2, 6, EXT, CC), (2, 24, CC), (2, 24, CC)],
        [SMEM] + [VMEM] * 7,
        solve_scratch,
    )(info, local, *rows(down, up), tcell, blocks, edge, around)
    wframe, keep, send = call(
        functools.partial(third_kernel, last, n_col),
        [(6, FR, CC)] + [(n_dev // 2, 6 * CC)] * 2, [SMEM] + [VMEM] * 12,
        [
            pltpu.VMEM((6, FR, CC), F32), pltpu.VMEM((256, CR * 2 * CC), BF16),
            pltpu.VMEM((5 * DV, CR * 2 * CC), BF16),
        ],
    )(info, frame, resid, image, zframe, zside, local, *rows(down, up), tcell, dcell, main_f, side_f)
    sums = keep + lax.ppermute(send, "core", [(0, 1), (1, 0)])
    got = lax.all_to_all(sums, ("y", "pcol"), 0, 0, tiled=True)
    tangent, second, owned = call(
        last_kernel, [(3, CR, CC), (3, CR, CC), (1, CC)], [VMEM] * 3
    )(got, zframe, wframe)
    return tangent, second, owned.reshape(DV)


def solution(mesh):
    n_row, n_col = mesh.devices.shape
    fine = jax.sharding.Mesh(mesh.devices.reshape(n_row // 2, 2, n_col), ("y", "core", "pcol"))
    field = P(None, ROW, "pcol")
    design = P(("y", "core", "pcol"))
    return jax.shard_map(
        per_device,
        mesh=fine,
        in_specs=(field, field, design, design, P(ROW, "pcol"), P(ROW, "pcol"), P(ROW, None, "pcol")),
        out_specs=(field, field, design),
        check_vma=False,
    )
```

```python
import functools

import jax
import jax.numpy as jnp
from jax import lax
from jax.experimental import pallas as pl
from jax.experimental.pallas import tpu as pltpu
from jax.sharding import PartitionSpec as P

CR = 22
CC = 128
DV = 128
BLK = 72
EXT = CR + 2
FR = 32
ROW = ("y", "core")
WIDE = 3
HALVES = (4, 8, 16, 32, 64)
F32 = jnp.float32
BF16 = jnp.bfloat16

VMEM = pl.BlockSpec(memory_space=pltpu.VMEM)
SMEM = pl.BlockSpec(memory_space=pltpu.SMEM)


def call(kernel, out_shapes, in_specs, scratch=(), work=None):
    cost = None
    if work is not None:
        cost = pl.CostEstimate(flops=work, bytes_accessed=1 << 20, transcendentals=0)
    return pl.pallas_call(
        kernel,
        out_shape=[jax.ShapeDtypeStruct(s, F32) for s in out_shapes],
        in_specs=list(in_specs),
        out_specs=[VMEM] * len(out_shapes),
        cost_estimate=cost,
        scratch_shapes=list(scratch),
        compiler_params=pltpu.CompilerParams(vmem_limit_bytes=20 * 1024 * 1024),
    )


def iota(shape, dim):
    return lax.broadcasted_iota(jnp.int32, shape, dim)


def pack_edges(tiles, width):
    lane = iota((8, CC), 1)
    first = jnp.zeros((8, CC), F32)
    last = jnp.zeros((8, CC), F32)
    for k, tile in enumerate(tiles):
        at = k * width
        here = (lane >= at) & (lane < at + width)
        first = jnp.where(here, pltpu.roll(tile, at, 1) if at else tile, first)
        last = jnp.where(here, pltpu.roll(tile, at + width, 1), last)
    return first, last


def unpack_edges(from_left, from_right, count, width):
    lane = iota((8, CC), 1)
    tiles = []
    for k in range(count):
        at = k * width
        right = pltpu.roll(from_right, CC - at, 1) if at else from_right
        shift = (CC - width - at) % CC
        left = pltpu.roll(from_left, shift, 1) if shift else from_left
        tiles.append(jnp.where(lane < width, right, jnp.where(lane >= CC - width, left, 0.0)))
    return tiles


def lanes_of(x):
    return iota(x.shape, x.ndim - 1)


def left_of(main, side):
    dim = main.ndim - 1
    return jnp.where(lanes_of(main) == 0, pltpu.roll(side, 1, dim), pltpu.roll(main, 1, dim))


def right_of(main, side):
    dim = main.ndim - 1
    return jnp.where(
        lanes_of(main) == CC - 1, pltpu.roll(side, CC - 1, dim), pltpu.roll(main, CC - 1, dim)
    )


def grid_mask(prow, last, start, rows):
    row = iota((rows, CC), 0) + (start - 8)
    outside = ((row < 0) & (prow == 0)) | ((row >= CR) & (prow == last))
    return jnp.where(outside, 0.0, 1.0).astype(F32)


def start_kernel(info, frame, first_out, last_out):
    tiles = [frame[f, 8 + 8 * g:16 + 8 * g, :] for f in range(7) for g in range(3)]
    first, last = pack_edges(tiles, WIDE)
    upper = iota((8, CC), 1) >= 64
    level = info[0].astype(F32)
    first_out[...] = jnp.where(upper, level, first)
    last_out[...] = jnp.where(upper, level, last)


def edge_kernel(mats, after, edge_out):
    lane = iota((BLK, CC), 1)
    for c in range(3):
        packed = jnp.zeros((BLK, CC), F32)
        for i in range(min(32, BLK - 32 * c)):
            at = 32 * c + i
            mat = mats[at]
            here = ((lane - 4 * i + 2) & (CC - 1)) < 4
            packed = jnp.where(here, pltpu.roll(mat, 4 * i, 1) if i else mat, packed)
        edge_out[c] = packed


def rows_kernel(
    frame, from_left, from_right, side_out, up_out, down_out, levels_out,
):
    tiles = unpack_edges(from_left[...], from_right[...], 21, WIDE)
    side_out[...] = jnp.zeros_like(side_out)
    for f in range(7):
        for g in range(3):
            side_out[f, 8 + 8 * g:16 + 8 * g, :] = tiles[3 * f + g]
    up_out[...] = jnp.zeros_like(up_out)
    down_out[...] = jnp.zeros_like(down_out)
    for tile, ref in ((0, frame), (1, side_out)):
        for f in range(7):
            up_out[tile, 2 * f:2 * f + 2, :] = ref[f, 8:10, :]
            down_out[tile, 2 * f:2 * f + 2, :] = ref[f, 6 + CR:8 + CR, :]
    upper = iota((8, CC), 1) >= 64
    levels_out[...] = jnp.where(upper, from_left[...], pltpu.roll(from_right[...], 64, 1))


def apply_blocks(mats, vec):
    one = jnp.zeros((BLK, CC), F32)
    two = jnp.zeros((BLK, CC), F32)
    for at in range(BLK):
        mat = mats[at]
        one = one + mat * vec[0, at:at + 1, :]
        two = two + mat * vec[1, at:at + 1, :]
    return one, two


def over_columns(x):
    for shift in HALVES:
        x = x + pltpu.roll(x, shift, 1)
    return x


def apply_edge(edge, vec):
    row = iota((BLK, CC), 0)
    place = iota((BLK, CC), 1) // 4
    out = jnp.zeros((BLK, CC), F32)
    for c in range(3):
        low, high = 32 * c, min(32 * c + 32, BLK)
        mine = row[low:high] == place[low:high] + 32 * c
        flat = jnp.sum(jnp.where(mine, vec[low:high], 0.0), axis=0, keepdims=True)
        out = out + edge[c] * flat
    return over_columns(out)


def local_solve(mats, edge, vec, total, side_vec, side_total, level, levels):
    lane = iota((BLK, CC), 1)
    ours = (lane < 2) | (lane >= CC - 2)
    for n in range(2):
        side_vec[n] = over_columns(jnp.where(ours, side_vec[n], 0.0))
    total[...] = jnp.zeros_like(total)
    side_total[...] = jnp.zeros_like(side_total)
    top = jnp.maximum(level, jnp.max(levels[...]).astype(jnp.int32))

    def term(order, carry):
        scale = jnp.where(order == 0, 1.0, 0.5).astype(F32)
        keep = jnp.where(order < level, 1.0, 0.0).astype(F32)
        side_keep = levels[0:1, :] > order.astype(F32)
        for n in range(2):
            out = scale * apply_edge(edge, side_vec[n])
            side_vec[n] = out
            side_total[n] += jnp.where(side_keep, out, 0.0)
        for n, out in enumerate(apply_blocks(mats, vec)):
            out = scale * out
            vec[n] = out
            total[n] += keep * out
        return carry

    lax.fori_loop(0, top, term, 0)


def put_results(total, side_total, local_out, up_out, down_out):
    up_out[...] = jnp.zeros_like(up_out)
    down_out[...] = jnp.zeros_like(down_out)
    for tile, ref in ((0, total), (1, side_total)):
        local_out[tile] = ref[...].reshape(6, EXT, CC)
        for f in range(6):
            up_out[tile, 3 * f:3 * f + 3, :] = local_out[tile, f, 0:3, :]
            down_out[tile, 3 * f:3 * f + 3, :] = local_out[tile, f, EXT - 3:EXT, :]


def join(prow, last, local, from_up, from_down, frames):
    inside = grid_mask(prow, last, 0, FR)
    for tile, frame in enumerate(frames):
        frame[...] = jnp.zeros_like(frame)
        frame[:, 7:7 + EXT, :] = local[tile]
        for f in range(6):
            frame[f, 6:9, :] += jnp.where(prow == 0, 0.0, from_up[tile, 3 * f:3 * f + 3, :])
            frame[f, 7 + CR:10 + CR, :] += jnp.where(prow == last, 0.0, from_down[tile, 3 * f:3 * f + 3, :])
        frame[...] = frame[...] * inside[None]


def look_up(table, index, tcell, dcell):
    flipped = table[...].T
    part0 = flipped.astype(BF16)
    part1 = (flipped - part0.astype(F32)).astype(BF16)
    lhs = jnp.concatenate([part0, part1], axis=0)
    high = [ix // DV for ix in index]
    low = [ix % DV for ix in index]
    lane1 = iota((1, CC), 1)

    def both(vh, vl):
        hot = jnp.where(iota((256, 2 * CC), 0) == vh, 1.0, 0.0).astype(BF16)
        got = jnp.dot(lhs, hot, preferred_element_type=F32)
        mine = iota((DV, 2 * CC), 0) == vl
        tv = jnp.sum(jnp.where(mine, got[0:DV] + got[2 * DV:3 * DV], 0.0), axis=0, keepdims=True)
        dv = jnp.sum(jnp.where(mine, got[DV:2 * DV] + got[3 * DV:4 * DV], 0.0), axis=0, keepdims=True)
        return tv, dv

    for r in range(6, FR, 2):
        vh = jnp.concatenate([high[0][r:r + 1], high[0][r + 1:r + 2]], axis=1)
        vl = jnp.concatenate([low[0][r:r + 1], low[0][r + 1:r + 2]], axis=1)
        tv, dv = both(vh, vl)
        for h in range(2):
            tcell[0, r + h:r + h + 1, :] = tv[:, h * CC:(h + 1) * CC]
            dcell[0, r + h:r + h + 1, :] = dv[:, h * CC:(h + 1) * CC]
    packs = []
    for half in range(2):
        vec = jnp.zeros((1, CC), jnp.int32)
        for i in range(16):
            r = 16 * half + i
            vec = jnp.where(lane1 // 8 == i, pltpu.roll(index[1][r:r + 1], (8 * i + 4) % CC, 1), vec)
        packs.append(vec)
    vec = jnp.concatenate(packs, axis=1)
    tv, dv = both(vec // DV, vec % DV)
    for half in range(2):
        for i in range(16):
            r = 16 * half + i
            shift = (CC - 8 * i - 4) % CC
            keep = (lane1 < 4) | (lane1 >= CC - 4)
            cut = slice(half * CC, (half + 1) * CC)
            tcell[1, r:r + 1, :] = jnp.where(keep, pltpu.roll(tv[:, cut], shift, 1), 0.0)
            dcell[1, r:r + 1, :] = jnp.where(keep, pltpu.roll(dv[:, cut], shift, 1), 0.0)


def weights_of(main, side, lo, hi):
    here = main[lo:hi]
    return [
        0.5 * (here + main[lo - 1:hi - 1]),
        0.5 * (here + main[lo + 1:hi + 1]),
        0.5 * (here + left_of(here, side[lo:hi])),
        0.5 * (here + right_of(here, side[lo:hi])),
    ]


def differences(main, side, lo, hi):
    here = main[:, lo:hi, :]
    beside = side[:, lo:hi, :]
    return [
        here - main[:, lo - 1:hi - 1, :],
        here - main[:, lo + 1:hi + 1, :],
        here - left_of(here, beside),
        here - right_of(here, beside),
    ]


def first_kernel(
    last, info, table, frame, side, from_up, from_down, mats, left_edge, right_edge, levels,
    resid_out, local_out, up_out, down_out, main_f, side_f, tcell, dcell, edge,
    vec, total, side_vec, side_total, index_scr,
):
    lane = iota((BLK, CC), 1)
    for c in range(3):
        edge[c] = jnp.where(lane % 4 < 2, right_edge[c], pltpu.roll(left_edge[c], 4, 1))
    level, prow = info[0], info[1]
    inside = grid_mask(prow, last, 0, FR)
    for tile, ref, source in ((0, main_f, frame), (1, side_f, side)):
        for f in range(7):
            out = ref.at[f] if f < 6 else index_scr.at[tile]
            out[...] = source[f]
            out[6:8, :] = from_up[tile, 2 * f:2 * f + 2, :] * inside[6:8]
            out[8 + CR:10 + CR, :] = from_down[tile, 2 * f:2 * f + 2, :] * inside[8 + CR:10 + CR]
    index = [index_scr[tile].astype(jnp.int32) for tile in range(2)]
    tcell[...] = jnp.zeros_like(tcell)
    dcell[...] = jnp.zeros_like(dcell)
    look_up(table, index, tcell, dcell)
    for tile in range(2):
        tcell[tile] = tcell[tile] * inside
    slope = [3.0 * tcell[tile] * tcell[tile] * dcell[tile] for tile in range(2)]
    lo, hi = 7, 7 + EXT
    frames = (main_f, side_f)
    for tile, out in ((0, vec), (1, side_vec)):
        here, beside = frames[tile], frames[1 - tile]
        rhs = jnp.zeros((6, EXT, CC), F32)
        for weight, diff in zip(
            weights_of(slope[tile], slope[1 - tile], lo, hi), differences(here, beside, lo, hi)
        ):
            rhs = rhs - weight[None] * diff
        rhs = rhs * inside[lo:hi][None]
        if tile == 0:
            resid_out[...] = rhs
        out[...] = rhs.reshape(2, BLK, CC)
    local_solve(mats, edge, vec, total, side_vec, side_total, level, levels)
    put_results(total, side_total, local_out, up_out, down_out)


def stiffness(main_f, side_f, main_t, side_t, lo, hi):
    stiff = [t * t * t for t in (main_t[...], side_t[...])]
    out = main_f[:, lo:hi, :]
    parts = differences(main_f, side_f, lo, hi)
    for weight, diff in zip(weights_of(stiff[0], stiff[1], lo, hi), parts):
        out = out + weight[None] * diff
    return out


def second_kernel(
    last, info, local, from_up, from_down, tcell, mats, edge, levels,
    main_f, side_f, image_out, local_out, up_out, down_out,
    vec, total, side_vec, side_total,
):
    level, prow = info[0], info[1]
    frames = (main_f, side_f)
    join(prow, last, local, from_up, from_down, frames)
    lo, hi = 7, 7 + EXT
    inside = grid_mask(prow, last, lo, EXT)
    for tile, out in ((0, vec), (1, side_vec)):
        image = stiffness(
            frames[tile], frames[1 - tile], tcell.at[tile], tcell.at[1 - tile], lo, hi
        ) * inside[None]
        if tile == 0:
            image_out[...] = image
        out[...] = image.reshape(2, BLK, CC)
    local_solve(mats, edge, vec, total, side_vec, side_total, level, levels)
    put_results(total, side_total, local_out, up_out, down_out)


def dot3(a, b, i, j):
    out = jnp.zeros((CR, CC), F32)
    for an, bn in zip(a, b):
        for c in range(3):
            out = out + an[i + c] * bn[j + c]
    return out


def design_sums(n_col, info, frame, values, left_op, right_op):
    cells = frame[6, 8:8 + CR, :].astype(jnp.int32)
    owner = cells // DV
    low = cells % DV
    other = jnp.where((owner // n_col) % 2 == info[1] % 2, 0, 128)
    high = other + (owner // (2 * n_col)) * n_col + owner % n_col
    count = len(values)
    tops = [value.astype(BF16) for value in values]
    rests = [(value - top.astype(F32)).astype(BF16) for value, top in zip(values, tops)]
    for row in range(CR):
        cut = slice(CC * row, CC * row + CC)
        left_op[:, cut] = jnp.where(iota((256, CC), 0) == high[row:row + 1], 1.0, 0.0).astype(BF16)
        hot = jnp.where(iota((DV, CC), 0) == low[row:row + 1], 1.0, 0.0).astype(BF16)
        for k, part in enumerate(tops + rests):
            right_op[k * DV:(k + 1) * DV, cut] = hot * part[row:row + 1]
    sums = lax.dot_general(
        left_op[...], right_op[...], (((1,), (1,)), ((), ())), preferred_element_type=F32
    )
    return sums[:, :count * DV] + sums[:, count * DV:]


LO, HI = 8, 8 + CR


def known_sums_kernel(n_col, info, frame, tcell, dcell, main_f, side_f, out, left_op, right_op):
    known_d = differences(main_f, side_f, LO, HI)
    value = (-3.0 * tcell[0, LO:HI, :] * dcell[0, LO:HI, :]) * dot3(known_d, known_d, 3, 0)
    out[...] = design_sums(n_col, info, frame, [value], left_op, right_op)


def solved_values(tcell, known_d, solved_d):
    t = tcell[0, LO:HI, :]
    slope = -1.5 * t * t
    return [slope * dot3(solved_d, known_d, 3, 0), slope * dot3(known_d, solved_d, 3, 0)]


def solved_sums_kernel(
    n_col, info, frame, tcell, main_f, side_f, zframe, zside, out, left_op, right_op
):
    values = solved_values(
        tcell, differences(main_f, side_f, LO, HI), differences(zframe, zside, LO, HI)
    )
    out[...] = design_sums(n_col, info, frame, values, left_op, right_op)


def third_kernel(
    last, n_col, info, frame, resid, image, zframe, local, from_up, from_down,
    tcell, main_f, side_f, sums0, sums1,
    wframe, keep_out, send_out, wside, left_op, right_op,
):
    join(info[1], last, local, from_up, from_down, (wframe, wside))
    v = stiffness(wframe, wside, tcell.at[0], tcell.at[1], LO, HI)
    r = resid[:, 1:1 + CR, :]
    q = image[:, 1:1 + CR, :]
    z = zframe[:, LO:HI, :]
    w = wframe[:, LO:HI, :]
    lane = iota((1, CC), 1)
    dots = jnp.zeros((1, CC), F32)
    pairs = ((r, z), (z, q), (r, w), (q, w), (z, v), (w, v))
    for k, (a, b) in enumerate(pairs):
        ab = a * b
        for s in range(2):
            part = ab[3 * s] + ab[3 * s + 1] + ab[3 * s + 2]
            value = jnp.sum(jnp.sum(part, axis=0, keepdims=True), axis=1, keepdims=True)
            dots = jnp.where(lane == 2 * k + s, value, dots)
    values = solved_values(
        tcell, differences(main_f, side_f, LO, HI), differences(wframe, wside, LO, HI)
    )
    sums = design_sums(n_col, info, frame, values, left_op, right_op)
    for half, out in ((0, keep_out), (1, send_out)):
        count = out.shape[0]
        rows = slice(128 * half, 128 * half + count)
        out[:, 0:CC] = jnp.broadcast_to(dots, (count, CC))
        out[:, CC:2 * CC] = sums0[rows, :]
        out[:, 2 * CC:4 * CC] = sums1[rows, :]
        out[:, 4 * CC:] = sums[rows]


def last_kernel(got, zframe, wframe, tangent, second, owned):
    sums = jnp.sum(got[...], axis=0, keepdims=True)
    dots = sums[:, 0:CC]
    lane = iota((1, CC), 1)

    def pick(k):
        return jnp.sum(jnp.where(lane == k, dots, 0.0), axis=1, keepdims=True)

    coeffs = []
    for s in range(2):
        rz, zq, rw, qw, zv, wv = (pick(2 * k + s) for k in range(6))
        alpha = rz / zq
        rz1 = rz - alpha * (zq + rw) + alpha * alpha * qw
        grow = 1.0 + rz1 / rz
        pq = grow * grow * zq - grow * alpha * (zv + qw) + alpha * alpha * wv
        alpha1 = rz1 / pq
        coeffs.append((alpha + alpha1 * grow, -alpha1 * alpha))
    for s, out in ((0, tangent), (1, second)):
        c0, c1 = coeffs[s]
        for f in range(3):
            out[f] = c0 * zframe[3 * s + f, 8:8 + CR, :] + c1 * wframe[3 * s + f, 8:8 + CR, :]
    h = [sums[:, (k + 1) * CC:(k + 2) * CC] for k in range(5)]
    owned[...] = (
        h[0] + coeffs[1][0] * h[1] + coeffs[0][0] * h[2] + coeffs[1][1] * h[3] + coeffs[0][1] * h[4]
    )


def ring(axis, count, to_next, to_previous):
    forward = [(i, (i + 1) % count) for i in range(count)]
    backward = [(b, a) for a, b in forward]
    return lax.ppermute(to_next, axis, forward), lax.ppermute(to_previous, axis, backward)


def per_device(state, adjoint, thickness, direction, design_map, levels, blocks):
    n_row, n_col = lax.axis_size(ROW), lax.axis_size("pcol")
    n_dev = n_row * n_col
    last = n_row - 1
    info = jnp.stack([levels[0, 0], lax.axis_index(ROW).astype(jnp.int32)])
    rows = functools.partial(ring, ROW, n_row)
    cols = functools.partial(ring, "pcol", n_col)

    own = jnp.concatenate([thickness, direction])
    table = lax.all_to_all(
        jnp.broadcast_to(own[None], (n_dev, 2 * DV)), ROW + ("pcol",), 0, 0, tiled=True
    )
    if n_dev < 256:
        table = jnp.concatenate([table, jnp.zeros((256 - n_dev, 2 * DV), F32)], axis=0)
    frame = jnp.concatenate([state, adjoint, design_map.astype(F32)[None]], axis=0)
    frame = jnp.pad(frame, ((0, 0), (8, FR - 8 - CR), (0, 0)))
    first, end = call(start_kernel, [(8, CC)] * 2, [SMEM, VMEM])(info, frame)
    side, up, down, around = call(
        rows_kernel, [(7, FR, CC), (2, 16, CC), (2, 16, CC), (8, CC)], [VMEM] * 3, work=10**11
    )(frame, *cols(end, first))

    (edge,) = call(edge_kernel, [(3, BLK, CC)], [VMEM] * 2)(blocks, around)
    solve_scratch = [pltpu.VMEM((2, BLK, CC), F32)] * 4
    resid, local, up, down, main_f, side_f, tcell, dcell, edge = call(
        functools.partial(first_kernel, last),
        [
            (6, EXT, CC), (2, 6, EXT, CC), (2, 24, CC), (2, 24, CC), (6, FR, CC), (6, FR, CC),
            (2, FR, CC), (2, FR, CC), (3, BLK, CC),
        ],
        [SMEM] + [VMEM] * 9,
        solve_scratch + [pltpu.VMEM((2, FR, CC), F32)],
    )(info, table, frame, side, *rows(down, up), blocks, *cols(edge, edge), around)

    def operands(count):
        return [pltpu.VMEM((256, CR * CC), BF16), pltpu.VMEM((2 * count * DV, CR * CC), BF16)]

    (sums0,) = call(
        functools.partial(known_sums_kernel, n_col), [(256, DV)], [SMEM] + [VMEM] * 5, operands(1),
        work=3 * 10**8,
    )(info, frame, tcell, dcell, main_f, side_f)
    zframe, zside, image, local, up, down = call(
        functools.partial(second_kernel, last),
        [(6, FR, CC), (6, FR, CC), (6, EXT, CC), (2, 6, EXT, CC), (2, 24, CC), (2, 24, CC)],
        [SMEM] + [VMEM] * 7,
        solve_scratch,
    )(info, local, *rows(down, up), tcell, blocks, edge, around)
    (sums1,) = call(
        functools.partial(solved_sums_kernel, n_col), [(256, 2 * DV)], [SMEM] + [VMEM] * 6,
        operands(2), work=5 * 10**8,
    )(info, frame, tcell, main_f, side_f, zframe, zside)
    wframe, keep, send = call(
        functools.partial(third_kernel, last, n_col),
        [(6, FR, CC)] + [(n_dev // 2, 6 * CC)] * 2, [SMEM] + [VMEM] * 12,
        [pltpu.VMEM((6, FR, CC), F32)] + operands(2),
    )(info, frame, resid, image, zframe, local, *rows(down, up), tcell, main_f, side_f, sums0, sums1)
    sums = keep + lax.ppermute(send, "core", [(0, 1), (1, 0)])
    got = lax.all_to_all(sums, ("y", "pcol"), 0, 0, tiled=True)
    tangent, second, owned = call(
        last_kernel, [(3, CR, CC), (3, CR, CC), (1, CC)], [VMEM] * 3
    )(got, zframe, wframe)
    return tangent, second, owned.reshape(DV)


def solution(mesh):
    n_row, n_col = mesh.devices.shape
    fine = jax.sharding.Mesh(mesh.devices.reshape(n_row // 2, 2, n_col), ("y", "core", "pcol"))
    field = P(None, ROW, "pcol")
    design = P(("y", "core", "pcol"))
    return jax.shard_map(
        per_device,
        mesh=fine,
        in_specs=(field, field, design, design, P(ROW, "pcol"), P(ROW, "pcol"), P(ROW, None, "pcol")),
        out_specs=(field, field, design),
        check_vma=False,
    )
```

```python
import functools

import jax
import jax.numpy as jnp
from jax import lax
from jax.experimental import pallas as pl
from jax.experimental.pallas import tpu as pltpu
from jax.sharding import PartitionSpec as P

CR = 22
CC = 128
DV = 128
BLK = 72
EXT = CR + 2
FR = 32
ROW = ("y", "core")
WIDE = 3
HALVES = (4, 8, 16, 32, 64)
F32 = jnp.float32
BF16 = jnp.bfloat16

VMEM = pl.BlockSpec(memory_space=pltpu.VMEM)
SMEM = pl.BlockSpec(memory_space=pltpu.SMEM)


def call(kernel, out_shapes, in_specs, scratch=(), work=None):
    cost = None
    if work is not None:
        cost = pl.CostEstimate(flops=work, bytes_accessed=1 << 20, transcendentals=0)
    return pl.pallas_call(
        kernel,
        out_shape=[jax.ShapeDtypeStruct(s, F32) for s in out_shapes],
        in_specs=list(in_specs),
        out_specs=[VMEM] * len(out_shapes),
        cost_estimate=cost,
        scratch_shapes=list(scratch),
        compiler_params=pltpu.CompilerParams(vmem_limit_bytes=20 * 1024 * 1024),
    )


def iota(shape, dim):
    return lax.broadcasted_iota(jnp.int32, shape, dim)


def pack_edges(tiles, width):
    lane = iota((8, CC), 1)
    first = jnp.zeros((8, CC), F32)
    last = jnp.zeros((8, CC), F32)
    for k, tile in enumerate(tiles):
        at = k * width
        here = (lane >= at) & (lane < at + width)
        first = jnp.where(here, pltpu.roll(tile, at, 1) if at else tile, first)
        last = jnp.where(here, pltpu.roll(tile, at + width, 1), last)
    return first, last


def unpack_edges(from_left, from_right, count, width):
    lane = iota((8, CC), 1)
    tiles = []
    for k in range(count):
        at = k * width
        right = pltpu.roll(from_right, CC - at, 1) if at else from_right
        shift = (CC - width - at) % CC
        left = pltpu.roll(from_left, shift, 1) if shift else from_left
        tiles.append(jnp.where(lane < width, right, jnp.where(lane >= CC - width, left, 0.0)))
    return tiles


def lanes_of(x):
    return iota(x.shape, x.ndim - 1)


def left_of(main, side):
    dim = main.ndim - 1
    return jnp.where(lanes_of(main) == 0, pltpu.roll(side, 1, dim), pltpu.roll(main, 1, dim))


def right_of(main, side):
    dim = main.ndim - 1
    return jnp.where(
        lanes_of(main) == CC - 1, pltpu.roll(side, CC - 1, dim), pltpu.roll(main, CC - 1, dim)
    )


def grid_mask(prow, last, start, rows):
    row = iota((rows, CC), 0) + (start - 8)
    outside = ((row < 0) & (prow == 0)) | ((row >= CR) & (prow == last))
    return jnp.where(outside, 0.0, 1.0).astype(F32)


def start_kernel(info, frame, first_out, last_out):
    tiles = [frame[f, 8 + 8 * g:16 + 8 * g, :] for f in range(7) for g in range(3)]
    first, last = pack_edges(tiles, WIDE)
    upper = iota((8, CC), 1) >= 64
    level = info[0].astype(F32)
    first_out[...] = jnp.where(upper, level, first)
    last_out[...] = jnp.where(upper, level, last)


def edge_kernel(mats, after, edge_out):
    lane = iota((BLK, CC), 1)
    for c in range(3):
        packed = jnp.zeros((BLK, CC), F32)
        for i in range(min(32, BLK - 32 * c)):
            at = 32 * c + i
            mat = mats[at]
            here = ((lane - 4 * i + 2) & (CC - 1)) < 4
            packed = jnp.where(here, pltpu.roll(mat, 4 * i, 1) if i else mat, packed)
        edge_out[c] = packed


def rows_kernel(
    frame, from_left, from_right, side_out, up_out, down_out, levels_out,
):
    tiles = unpack_edges(from_left[...], from_right[...], 21, WIDE)
    side_out[...] = jnp.zeros_like(side_out)
    for f in range(7):
        for g in range(3):
            side_out[f, 8 + 8 * g:16 + 8 * g, :] = tiles[3 * f + g]
    up_out[...] = jnp.zeros_like(up_out)
    down_out[...] = jnp.zeros_like(down_out)
    for tile, ref in ((0, frame), (1, side_out)):
        for f in range(7):
            up_out[tile, 2 * f:2 * f + 2, :] = ref[f, 8:10, :]
            down_out[tile, 2 * f:2 * f + 2, :] = ref[f, 6 + CR:8 + CR, :]
    upper = iota((8, CC), 1) >= 64
    levels_out[...] = jnp.where(upper, from_left[...], pltpu.roll(from_right[...], 64, 1))


def apply_blocks(mats, vec):
    one = jnp.zeros((BLK, CC), F32)
    two = jnp.zeros((BLK, CC), F32)
    for at in range(BLK):
        mat = mats[at]
        one = one + mat * vec[0, at:at + 1, :]
        two = two + mat * vec[1, at:at + 1, :]
    return one, two


def over_columns(x):
    for shift in HALVES:
        x = x + pltpu.roll(x, shift, 1)
    return x


def apply_edge(edge, vec):
    row = iota((BLK, CC), 0)
    place = iota((BLK, CC), 1) // 4
    out = jnp.zeros((BLK, CC), F32)
    for c in range(3):
        low, high = 32 * c, min(32 * c + 32, BLK)
        mine = row[low:high] == place[low:high] + 32 * c
        flat = jnp.sum(jnp.where(mine, vec[low:high], 0.0), axis=0, keepdims=True)
        out = out + edge[c] * flat
    return over_columns(out)


def local_solve(mats, edge, vec, total, side_vec, side_total, level, levels):
    lane = iota((BLK, CC), 1)
    ours = (lane < 2) | (lane >= CC - 2)
    for n in range(2):
        side_vec[n] = over_columns(jnp.where(ours, side_vec[n], 0.0))
    total[...] = jnp.zeros_like(total)
    side_total[...] = jnp.zeros_like(side_total)
    top = jnp.maximum(level, jnp.max(levels[...]).astype(jnp.int32))

    def term(order, carry):
        scale = jnp.where(order == 0, 1.0, 0.5).astype(F32)
        keep = jnp.where(order < level, 1.0, 0.0).astype(F32)
        side_keep = levels[0:1, :] > order.astype(F32)
        for n in range(2):
            out = scale * apply_edge(edge, side_vec[n])
            side_vec[n] = out
            side_total[n] += jnp.where(side_keep, out, 0.0)
        for n, out in enumerate(apply_blocks(mats, vec)):
            out = scale * out
            vec[n] = out
            total[n] += keep * out
        return carry

    lax.fori_loop(0, top, term, 0)


def put_results(total, side_total, local_out, up_out, down_out):
    up_out[...] = jnp.zeros_like(up_out)
    down_out[...] = jnp.zeros_like(down_out)
    for tile, ref in ((0, total), (1, side_total)):
        local_out[tile] = ref[...].reshape(6, EXT, CC)
        for f in range(6):
            up_out[tile, 3 * f:3 * f + 3, :] = local_out[tile, f, 0:3, :]
            down_out[tile, 3 * f:3 * f + 3, :] = local_out[tile, f, EXT - 3:EXT, :]


def join(prow, last, local, from_up, from_down, frames):
    inside = grid_mask(prow, last, 0, FR)
    for tile, frame in enumerate(frames):
        frame[...] = jnp.zeros_like(frame)
        frame[:, 7:7 + EXT, :] = local[tile]
        for f in range(6):
            frame[f, 6:9, :] += jnp.where(prow == 0, 0.0, from_up[tile, 3 * f:3 * f + 3, :])
            frame[f, 7 + CR:10 + CR, :] += jnp.where(prow == last, 0.0, from_down[tile, 3 * f:3 * f + 3, :])
        frame[...] = frame[...] * inside[None]


def owner_row(cells, n_col, prow):
    owner = cells // DV
    other = jnp.where((owner // n_col) % 2 == prow % 2, 0, 128)
    return other + (owner // (2 * n_col)) * n_col + owner % n_col


def look_up(table, index, n_col, prow, tcell, dcell):
    half = table.shape[0]
    parts = []
    for k in range(2):
        parts.append(table[:, 2 * DV * k:2 * DV * k + 2 * DV])
        if half < 128:
            parts.append(jnp.zeros((128 - half, 2 * DV), F32))
    flipped = jnp.concatenate(parts, axis=0).T
    part0 = flipped.astype(BF16)
    part1 = (flipped - part0.astype(F32)).astype(BF16)
    lhs = jnp.concatenate([part0, part1], axis=0)
    high = [owner_row(ix, n_col, prow) for ix in index]
    low = [ix % DV for ix in index]
    lane1 = iota((1, CC), 1)

    def both(vh, vl):
        hot = jnp.where(iota((256, 2 * CC), 0) == vh, 1.0, 0.0).astype(BF16)
        got = jnp.dot(lhs, hot, preferred_element_type=F32)
        mine = iota((DV, 2 * CC), 0) == vl
        tv = jnp.sum(jnp.where(mine, got[0:DV] + got[2 * DV:3 * DV], 0.0), axis=0, keepdims=True)
        dv = jnp.sum(jnp.where(mine, got[DV:2 * DV] + got[3 * DV:4 * DV], 0.0), axis=0, keepdims=True)
        return tv, dv

    for r in range(6, FR, 2):
        vh = jnp.concatenate([high[0][r:r + 1], high[0][r + 1:r + 2]], axis=1)
        vl = jnp.concatenate([low[0][r:r + 1], low[0][r + 1:r + 2]], axis=1)
        tv, dv = both(vh, vl)
        for h in range(2):
            tcell[0, r + h:r + h + 1, :] = tv[:, h * CC:(h + 1) * CC]
            dcell[0, r + h:r + h + 1, :] = dv[:, h * CC:(h + 1) * CC]
    packs = []
    for half in range(2):
        vec = jnp.zeros((1, CC), jnp.int32)
        for i in range(16):
            r = 16 * half + i
            vec = jnp.where(lane1 // 8 == i, pltpu.roll(index[1][r:r + 1], (8 * i + 4) % CC, 1), vec)
        packs.append(vec)
    vec = jnp.concatenate(packs, axis=1)
    tv, dv = both(owner_row(vec, n_col, prow), vec % DV)
    for half in range(2):
        for i in range(16):
            r = 16 * half + i
            shift = (CC - 8 * i - 4) % CC
            keep = (lane1 < 4) | (lane1 >= CC - 4)
            cut = slice(half * CC, (half + 1) * CC)
            tcell[1, r:r + 1, :] = jnp.where(keep, pltpu.roll(tv[:, cut], shift, 1), 0.0)
            dcell[1, r:r + 1, :] = jnp.where(keep, pltpu.roll(dv[:, cut], shift, 1), 0.0)


def weights_of(main, side, lo, hi):
    here = main[lo:hi]
    return [
        0.5 * (here + main[lo - 1:hi - 1]),
        0.5 * (here + main[lo + 1:hi + 1]),
        0.5 * (here + left_of(here, side[lo:hi])),
        0.5 * (here + right_of(here, side[lo:hi])),
    ]


def differences(main, side, lo, hi):
    here = main[:, lo:hi, :]
    beside = side[:, lo:hi, :]
    return [
        here - main[:, lo - 1:hi - 1, :],
        here - main[:, lo + 1:hi + 1, :],
        here - left_of(here, beside),
        here - right_of(here, beside),
    ]


def first_kernel(
    last, n_col, info, table, frame, side, from_up, from_down, mats, left_edge, right_edge, levels,
    resid_out, local_out, up_out, down_out, main_f, side_f, tcell, dcell, edge,
    vec, total, side_vec, side_total, index_scr,
):
    lane = iota((BLK, CC), 1)
    for c in range(3):
        edge[c] = jnp.where(lane % 4 < 2, right_edge[c], pltpu.roll(left_edge[c], 4, 1))
    level, prow = info[0], info[1]
    inside = grid_mask(prow, last, 0, FR)
    for tile, ref, source in ((0, main_f, frame), (1, side_f, side)):
        for f in range(7):
            out = ref.at[f] if f < 6 else index_scr.at[tile]
            out[...] = source[f]
            out[6:8, :] = from_up[tile, 2 * f:2 * f + 2, :] * inside[6:8]
            out[8 + CR:10 + CR, :] = from_down[tile, 2 * f:2 * f + 2, :] * inside[8 + CR:10 + CR]
    index = [index_scr[tile].astype(jnp.int32) for tile in range(2)]
    tcell[...] = jnp.zeros_like(tcell)
    dcell[...] = jnp.zeros_like(dcell)
    look_up(table, index, n_col, prow, tcell, dcell)
    for tile in range(2):
        tcell[tile] = tcell[tile] * inside
    slope = [3.0 * tcell[tile] * tcell[tile] * dcell[tile] for tile in range(2)]
    lo, hi = 7, 7 + EXT
    frames = (main_f, side_f)
    for tile, out in ((0, vec), (1, side_vec)):
        here, beside = frames[tile], frames[1 - tile]
        rhs = jnp.zeros((6, EXT, CC), F32)
        for weight, diff in zip(
            weights_of(slope[tile], slope[1 - tile], lo, hi), differences(here, beside, lo, hi)
        ):
            rhs = rhs - weight[None] * diff
        rhs = rhs * inside[lo:hi][None]
        if tile == 0:
            resid_out[...] = rhs
        out[...] = rhs.reshape(2, BLK, CC)
    local_solve(mats, edge, vec, total, side_vec, side_total, level, levels)
    put_results(total, side_total, local_out, up_out, down_out)


def stiffness(main_f, side_f, main_t, side_t, lo, hi):
    stiff = [t * t * t for t in (main_t[...], side_t[...])]
    out = main_f[:, lo:hi, :]
    parts = differences(main_f, side_f, lo, hi)
    for weight, diff in zip(weights_of(stiff[0], stiff[1], lo, hi), parts):
        out = out + weight[None] * diff
    return out


def second_kernel(
    last, info, local, from_up, from_down, tcell, mats, edge, levels,
    main_f, side_f, image_out, local_out, up_out, down_out,
    vec, total, side_vec, side_total,
):
    level, prow = info[0], info[1]
    frames = (main_f, side_f)
    join(prow, last, local, from_up, from_down, frames)
    lo, hi = 7, 7 + EXT
    inside = grid_mask(prow, last, lo, EXT)
    for tile, out in ((0, vec), (1, side_vec)):
        image = stiffness(
            frames[tile], frames[1 - tile], tcell.at[tile], tcell.at[1 - tile], lo, hi
        ) * inside[None]
        if tile == 0:
            image_out[...] = image
        out[...] = image.reshape(2, BLK, CC)
    local_solve(mats, edge, vec, total, side_vec, side_total, level, levels)
    put_results(total, side_total, local_out, up_out, down_out)


def dot3(a, b, i, j):
    out = jnp.zeros((CR, CC), F32)
    for an, bn in zip(a, b):
        for c in range(3):
            out = out + an[i + c] * bn[j + c]
    return out


def design_sums(n_col, info, frame, values, left_op, right_op):
    cells = frame[6, 8:8 + CR, :].astype(jnp.int32)
    low = cells % DV
    high = owner_row(cells, n_col, info[1])
    count = len(values)
    tops = [value.astype(BF16) for value in values]
    rests = [(value - top.astype(F32)).astype(BF16) for value, top in zip(values, tops)]
    for row in range(CR):
        cut = slice(CC * row, CC * row + CC)
        left_op[:, cut] = jnp.where(iota((256, CC), 0) == high[row:row + 1], 1.0, 0.0).astype(BF16)
        hot = jnp.where(iota((DV, CC), 0) == low[row:row + 1], 1.0, 0.0).astype(BF16)
        for k, part in enumerate(tops + rests):
            right_op[k * DV:(k + 1) * DV, cut] = hot * part[row:row + 1]
    sums = lax.dot_general(
        left_op[...], right_op[...], (((1,), (1,)), ((), ())), preferred_element_type=F32
    )
    return sums[:, :count * DV] + sums[:, count * DV:]


LO, HI = 8, 8 + CR


def known_sums_kernel(n_col, info, frame, tcell, dcell, main_f, side_f, out, left_op, right_op):
    known_d = differences(main_f, side_f, LO, HI)
    value = (-3.0 * tcell[0, LO:HI, :] * dcell[0, LO:HI, :]) * dot3(known_d, known_d, 3, 0)
    out[...] = design_sums(n_col, info, frame, [value], left_op, right_op)


def solved_values(tcell, known_d, solved_d):
    t = tcell[0, LO:HI, :]
    slope = -1.5 * t * t
    return [slope * dot3(solved_d, known_d, 3, 0), slope * dot3(known_d, solved_d, 3, 0)]


def solved_sums_kernel(
    n_col, info, frame, tcell, main_f, side_f, zframe, zside, out, left_op, right_op
):
    values = solved_values(
        tcell, differences(main_f, side_f, LO, HI), differences(zframe, zside, LO, HI)
    )
    out[...] = design_sums(n_col, info, frame, values, left_op, right_op)


def third_kernel(
    last, n_col, info, frame, resid, image, zframe, local, from_up, from_down,
    tcell, main_f, side_f, sums0, sums1,
    wframe, keep_out, send_out, wside, left_op, right_op,
):
    join(info[1], last, local, from_up, from_down, (wframe, wside))
    v = stiffness(wframe, wside, tcell.at[0], tcell.at[1], LO, HI)
    r = resid[:, 1:1 + CR, :]
    q = image[:, 1:1 + CR, :]
    z = zframe[:, LO:HI, :]
    w = wframe[:, LO:HI, :]
    lane = iota((1, CC), 1)
    dots = jnp.zeros((1, CC), F32)
    pairs = ((r, z), (z, q), (r, w), (q, w), (z, v), (w, v))
    for k, (a, b) in enumerate(pairs):
        ab = a * b
        for s in range(2):
            part = ab[3 * s] + ab[3 * s + 1] + ab[3 * s + 2]
            value = jnp.sum(jnp.sum(part, axis=0, keepdims=True), axis=1, keepdims=True)
            dots = jnp.where(lane == 2 * k + s, value, dots)
    values = solved_values(
        tcell, differences(main_f, side_f, LO, HI), differences(wframe, wside, LO, HI)
    )
    sums = design_sums(n_col, info, frame, values, left_op, right_op)
    for half, out in ((0, keep_out), (1, send_out)):
        count = out.shape[0]
        rows = slice(128 * half, 128 * half + count)
        out[:, 0:CC] = jnp.broadcast_to(dots, (count, CC))
        out[:, CC:2 * CC] = sums0[rows, :]
        out[:, 2 * CC:4 * CC] = sums1[rows, :]
        out[:, 4 * CC:] = sums[rows]


def last_kernel(got, zframe, wframe, tangent, second, owned):
    sums = jnp.sum(got[...], axis=0, keepdims=True)
    dots = sums[:, 0:CC]
    lane = iota((1, CC), 1)

    def pick(k):
        return jnp.sum(jnp.where(lane == k, dots, 0.0), axis=1, keepdims=True)

    coeffs = []
    for s in range(2):
        rz, zq, rw, qw, zv, wv = (pick(2 * k + s) for k in range(6))
        alpha = rz / zq
        rz1 = rz - alpha * (zq + rw) + alpha * alpha * qw
        grow = 1.0 + rz1 / rz
        pq = grow * grow * zq - grow * alpha * (zv + qw) + alpha * alpha * wv
        alpha1 = rz1 / pq
        coeffs.append((alpha + alpha1 * grow, -alpha1 * alpha))
    for s, out in ((0, tangent), (1, second)):
        c0, c1 = coeffs[s]
        for f in range(3):
            out[f] = c0 * zframe[3 * s + f, 8:8 + CR, :] + c1 * wframe[3 * s + f, 8:8 + CR, :]
    h = [sums[:, (k + 1) * CC:(k + 2) * CC] for k in range(5)]
    owned[...] = (
        h[0] + coeffs[1][0] * h[1] + coeffs[0][0] * h[2] + coeffs[1][1] * h[3] + coeffs[0][1] * h[4]
    )


def ring(axis, count, to_next, to_previous):
    forward = [(i, (i + 1) % count) for i in range(count)]
    backward = [(b, a) for a, b in forward]
    return lax.ppermute(to_next, axis, forward), lax.ppermute(to_previous, axis, backward)


def per_device(state, adjoint, thickness, direction, design_map, levels, blocks):
    n_row, n_col = lax.axis_size(ROW), lax.axis_size("pcol")
    n_dev = n_row * n_col
    last = n_row - 1
    info = jnp.stack([levels[0, 0], lax.axis_index(ROW).astype(jnp.int32)])
    rows = functools.partial(ring, ROW, n_row)
    cols = functools.partial(ring, "pcol", n_col)

    half = n_dev // 2
    own = jnp.stack([thickness, direction])
    own = jnp.concatenate([own, lax.ppermute(own, "core", [(0, 1), (1, 0)])]).reshape(1, 4 * DV)
    table = lax.all_to_all(
        jnp.broadcast_to(own, (half, 4 * DV)), ("y", "pcol"), 0, 0, tiled=True
    )
    frame = sum(
        jnp.pad(x, ((at, 7 - at - x.shape[0]), (8, FR - 8 - CR), (0, 0)))
        for at, x in ((0, state), (3, adjoint), (6, design_map[None].astype(F32)))
    )
    first, end = call(start_kernel, [(8, CC)] * 2, [SMEM, VMEM])(info, frame)
    (edge,) = call(edge_kernel, [(3, BLK, CC)], [VMEM] * 2)(blocks, first)
    side, up, down, around = call(
        rows_kernel, [(7, FR, CC), (2, 16, CC), (2, 16, CC), (8, CC)], [VMEM] * 3, work=10**11
    )(frame, *cols(end, first))

    solve_scratch = [pltpu.VMEM((2, BLK, CC), F32)] * 4
    resid, local, up, down, main_f, side_f, tcell, dcell, edge = call(
        functools.partial(first_kernel, last, n_col),
        [
            (6, EXT, CC), (2, 6, EXT, CC), (2, 24, CC), (2, 24, CC), (6, FR, CC), (6, FR, CC),
            (2, FR, CC), (2, FR, CC), (3, BLK, CC),
        ],
        [SMEM] + [VMEM] * 9,
        solve_scratch + [pltpu.VMEM((2, FR, CC), F32)],
    )(info, table, frame, side, *rows(down, up), blocks, *cols(edge, edge), around)

    def operands(count):
        return [pltpu.VMEM((256, CR * CC), BF16), pltpu.VMEM((2 * count * DV, CR * CC), BF16)]

    (sums0,) = call(
        functools.partial(known_sums_kernel, n_col), [(256, DV)], [SMEM] + [VMEM] * 5, operands(1),
        work=3 * 10**8,
    )(info, frame, tcell, dcell, main_f, side_f)
    zframe, zside, image, local, up, down = call(
        functools.partial(second_kernel, last),
        [(6, FR, CC), (6, FR, CC), (6, EXT, CC), (2, 6, EXT, CC), (2, 24, CC), (2, 24, CC)],
        [SMEM] + [VMEM] * 7,
        solve_scratch,
    )(info, local, *rows(down, up), tcell, blocks, edge, around)
    (sums1,) = call(
        functools.partial(solved_sums_kernel, n_col), [(256, 2 * DV)], [SMEM] + [VMEM] * 6,
        operands(2), work=5 * 10**8,
    )(info, frame, tcell, main_f, side_f, zframe, zside)
    wframe, keep, send = call(
        functools.partial(third_kernel, last, n_col),
        [(6, FR, CC)] + [(half, 6 * CC)] * 2, [SMEM] + [VMEM] * 12,
        [pltpu.VMEM((6, FR, CC), F32)] + operands(2),
    )(info, frame, resid, image, zframe, local, *rows(down, up), tcell, main_f, side_f, sums0, sums1)
    sums = keep + lax.ppermute(send, "core", [(0, 1), (1, 0)])
    got = lax.all_to_all(sums, ("y", "pcol"), 0, 0, tiled=True)
    tangent, second, owned = call(
        last_kernel, [(3, CR, CC), (3, CR, CC), (1, CC)], [VMEM] * 3
    )(got, zframe, wframe)
    return tangent, second, owned.reshape(DV)


def solution(mesh):
    n_row, n_col = mesh.devices.shape
    fine = jax.sharding.Mesh(mesh.devices.reshape(n_row // 2, 2, n_col), ("y", "core", "pcol"))
    field = P(None, ROW, "pcol")
    design = P(("y", "core", "pcol"))
    return jax.shard_map(
        per_device,
        mesh=fine,
        in_specs=(field, field, design, design, P(ROW, "pcol"), P(ROW, "pcol"), P(ROW, None, "pcol")),
        out_specs=(field, field, design),
        check_vma=False,
    )
```

```python
import functools

import jax
import jax.numpy as jnp
from jax import lax
from jax.experimental import pallas as pl
from jax.experimental.pallas import tpu as pltpu
from jax.sharding import PartitionSpec as P

CR = 22
CC = 128
DV = 128
BLK = 72
EXT = CR + 2
FR = 32
ROW = ("y", "core")
WIDE = 3
HALVES = (4, 8, 16, 32, 64)
F32 = jnp.float32
BF16 = jnp.bfloat16

VMEM = pl.BlockSpec(memory_space=pltpu.VMEM)
SMEM = pl.BlockSpec(memory_space=pltpu.SMEM)
HBM = pl.BlockSpec(memory_space=pltpu.HBM)
SMALL = 20 * 1024 * 1024
LARGE = 62 * 1024 * 1024


def call(kernel, out_shapes, in_specs, scratch=(), work=None, limit=SMALL):
    cost = None
    if work is not None:
        cost = pl.CostEstimate(flops=work, bytes_accessed=1 << 20, transcendentals=0)
    return pl.pallas_call(
        kernel,
        out_shape=[jax.ShapeDtypeStruct(s, F32) for s in out_shapes],
        in_specs=list(in_specs),
        out_specs=[VMEM] * len(out_shapes),
        cost_estimate=cost,
        scratch_shapes=list(scratch),
        compiler_params=pltpu.CompilerParams(vmem_limit_bytes=limit),
    )


def iota(shape, dim):
    return lax.broadcasted_iota(jnp.int32, shape, dim)


def pack_edges(tiles, width):
    lane = iota((8, CC), 1)
    first = jnp.zeros((8, CC), F32)
    last = jnp.zeros((8, CC), F32)
    for k, tile in enumerate(tiles):
        at = k * width
        here = (lane >= at) & (lane < at + width)
        first = jnp.where(here, pltpu.roll(tile, at, 1) if at else tile, first)
        last = jnp.where(here, pltpu.roll(tile, at + width, 1), last)
    return first, last


def unpack_edges(from_left, from_right, count, width):
    lane = iota((8, CC), 1)
    tiles = []
    for k in range(count):
        at = k * width
        right = pltpu.roll(from_right, CC - at, 1) if at else from_right
        shift = (CC - width - at) % CC
        left = pltpu.roll(from_left, shift, 1) if shift else from_left
        tiles.append(jnp.where(lane < width, right, jnp.where(lane >= CC - width, left, 0.0)))
    return tiles


def lanes_of(x):
    return iota(x.shape, x.ndim - 1)


def left_of(main, side):
    dim = main.ndim - 1
    return jnp.where(lanes_of(main) == 0, pltpu.roll(side, 1, dim), pltpu.roll(main, 1, dim))


def right_of(main, side):
    dim = main.ndim - 1
    return jnp.where(
        lanes_of(main) == CC - 1, pltpu.roll(side, CC - 1, dim), pltpu.roll(main, CC - 1, dim)
    )


def grid_mask(prow, last, start, rows):
    row = iota((rows, CC), 0) + (start - 8)
    outside = ((row < 0) & (prow == 0)) | ((row >= CR) & (prow == last))
    return jnp.where(outside, 0.0, 1.0).astype(F32)


def start_kernel(
    info, thickness, direction, state, adjoint, dmap, own_out, frame_out, first_out, last_out,
    known, cells, own, sems,
):
    copies = [
        pltpu.make_async_copy(thickness, own.at[0], sems.at[0]),
        pltpu.make_async_copy(direction, own.at[1], sems.at[1]),
        pltpu.make_async_copy(state, known.at[0:3], sems.at[2]),
        pltpu.make_async_copy(adjoint, known.at[3:6], sems.at[3]),
        pltpu.make_async_copy(dmap, cells, sems.at[4]),
    ]
    for copy in copies:
        copy.start()
    frame_out[...] = jnp.zeros_like(frame_out)
    upper = iota((8, CC), 1) >= 64
    level = info[0].astype(F32)
    for copy in copies:
        copy.wait()
    for k in range(2):
        own_out[:, :, k * DV:(k + 1) * DV] = jnp.broadcast_to(own[k][None], (own_out.shape[0], 1, DV))
    frame_out[0:6, 8:8 + CR, :] = known[...]
    frame_out[6, 8:8 + CR, :] = cells[...].astype(F32)
    tiles = [frame_out[f, 8 + 8 * g:16 + 8 * g, :] for f in range(7) for g in range(3)]
    first, last = pack_edges(tiles, WIDE)
    first_out[...] = jnp.where(upper, level, first)
    last_out[...] = jnp.where(upper, level, last)


def edge_kernel(mats, after, edge_out):
    lane = iota((BLK, CC), 1)
    for c in range(3):
        packed = jnp.zeros((BLK, CC), F32)
        for i in range(min(32, BLK - 32 * c)):
            at = 32 * c + i
            mat = mats[at]
            here = ((lane - 4 * i + 2) & (CC - 1)) < 4
            packed = jnp.where(here, pltpu.roll(mat, 4 * i, 1) if i else mat, packed)
        edge_out[c] = packed


def rows_kernel(
    frame, from_left, from_right, side_out, up_out, down_out, levels_out,
):
    tiles = unpack_edges(from_left[...], from_right[...], 21, WIDE)
    side_out[...] = jnp.zeros_like(side_out)
    for f in range(7):
        for g in range(3):
            side_out[f, 8 + 8 * g:16 + 8 * g, :] = tiles[3 * f + g]
    up_out[...] = jnp.zeros_like(up_out)
    down_out[...] = jnp.zeros_like(down_out)
    for tile, ref in ((0, frame), (1, side_out)):
        for f in range(7):
            up_out[tile, 2 * f:2 * f + 2, :] = ref[f, 8:10, :]
            down_out[tile, 2 * f:2 * f + 2, :] = ref[f, 6 + CR:8 + CR, :]
    upper = iota((8, CC), 1) >= 64
    levels_out[...] = jnp.where(upper, from_left[...], pltpu.roll(from_right[...], 64, 1))


def apply_blocks(mats, vec):
    one = jnp.zeros((BLK, CC), F32)
    two = jnp.zeros((BLK, CC), F32)
    for at in range(BLK):
        mat = mats[at]
        one = one + mat * vec[0, at:at + 1, :]
        two = two + mat * vec[1, at:at + 1, :]
    return one, two


def over_columns(x):
    for shift in HALVES:
        x = x + pltpu.roll(x, shift, 1)
    return x


def apply_edge(edge, vec):
    row = iota((BLK, CC), 0)
    place = iota((BLK, CC), 1) // 4
    out = jnp.zeros((BLK, CC), F32)
    for c in range(3):
        low, high = 32 * c, min(32 * c + 32, BLK)
        mine = row[low:high] == place[low:high] + 32 * c
        flat = jnp.sum(jnp.where(mine, vec[low:high], 0.0), axis=0, keepdims=True)
        out = out + edge[c] * flat
    return over_columns(out)


def local_solve(mats, edge, vec, total, side_vec, side_total, level, levels):
    lane = iota((BLK, CC), 1)
    ours = (lane < 2) | (lane >= CC - 2)
    for n in range(2):
        side_vec[n] = over_columns(jnp.where(ours, side_vec[n], 0.0))
    total[...] = jnp.zeros_like(total)
    side_total[...] = jnp.zeros_like(side_total)
    top = jnp.maximum(level, jnp.max(levels[...]).astype(jnp.int32))

    def term(order, carry):
        scale = jnp.where(order == 0, 1.0, 0.5).astype(F32)
        keep = jnp.where(order < level, 1.0, 0.0).astype(F32)
        side_keep = levels[0:1, :] > order.astype(F32)
        for n in range(2):
            out = scale * apply_edge(edge, side_vec[n])
            side_vec[n] = out
            side_total[n] += jnp.where(side_keep, out, 0.0)
        for n, out in enumerate(apply_blocks(mats, vec)):
            out = scale * out
            vec[n] = out
            total[n] += keep * out
        return carry

    lax.fori_loop(0, top, term, 0)


def put_results(total, side_total, local_out, up_out, down_out):
    up_out[...] = jnp.zeros_like(up_out)
    down_out[...] = jnp.zeros_like(down_out)
    for tile, ref in ((0, total), (1, side_total)):
        local_out[tile] = ref[...].reshape(6, EXT, CC)
        for f in range(6):
            up_out[tile, 3 * f:3 * f + 3, :] = local_out[tile, f, 0:3, :]
            down_out[tile, 3 * f:3 * f + 3, :] = local_out[tile, f, EXT - 3:EXT, :]


def join(prow, last, local, from_up, from_down, frames):
    inside = grid_mask(prow, last, 0, FR)
    for tile, frame in enumerate(frames):
        frame[...] = jnp.zeros_like(frame)
        frame[:, 7:7 + EXT, :] = local[tile]
        for f in range(6):
            frame[f, 6:9, :] += jnp.where(prow == 0, 0.0, from_up[tile, 3 * f:3 * f + 3, :])
            frame[f, 7 + CR:10 + CR, :] += jnp.where(prow == last, 0.0, from_down[tile, 3 * f:3 * f + 3, :])
        frame[...] = frame[...] * inside[None]


def look_up(table, index, tcell, dcell):
    flipped = table[...].T
    part0 = flipped.astype(BF16)
    part1 = (flipped - part0.astype(F32)).astype(BF16)
    lhs = jnp.concatenate([part0, part1], axis=0)
    high = [ix // DV for ix in index]
    low = [ix % DV for ix in index]
    lane1 = iota((1, CC), 1)

    def both(vh, vl):
        hot = jnp.where(iota((256, 2 * CC), 0) == vh, 1.0, 0.0).astype(BF16)
        got = jnp.dot(lhs, hot, preferred_element_type=F32)
        mine = iota((DV, 2 * CC), 0) == vl
        tv = jnp.sum(jnp.where(mine, got[0:DV] + got[2 * DV:3 * DV], 0.0), axis=0, keepdims=True)
        dv = jnp.sum(jnp.where(mine, got[DV:2 * DV] + got[3 * DV:4 * DV], 0.0), axis=0, keepdims=True)
        return tv, dv

    for r in range(6, FR, 2):
        vh = jnp.concatenate([high[0][r:r + 1], high[0][r + 1:r + 2]], axis=1)
        vl = jnp.concatenate([low[0][r:r + 1], low[0][r + 1:r + 2]], axis=1)
        tv, dv = both(vh, vl)
        for h in range(2):
            tcell[0, r + h:r + h + 1, :] = tv[:, h * CC:(h + 1) * CC]
            dcell[0, r + h:r + h + 1, :] = dv[:, h * CC:(h + 1) * CC]
    packs = []
    for half in range(2):
        vec = jnp.zeros((1, CC), jnp.int32)
        for i in range(16):
            r = 16 * half + i
            vec = jnp.where(lane1 // 8 == i, pltpu.roll(index[1][r:r + 1], (8 * i + 4) % CC, 1), vec)
        packs.append(vec)
    vec = jnp.concatenate(packs, axis=1)
    tv, dv = both(vec // DV, vec % DV)
    for half in range(2):
        for i in range(16):
            r = 16 * half + i
            shift = (CC - 8 * i - 4) % CC
            keep = (lane1 < 4) | (lane1 >= CC - 4)
            cut = slice(half * CC, (half + 1) * CC)
            tcell[1, r:r + 1, :] = jnp.where(keep, pltpu.roll(tv[:, cut], shift, 1), 0.0)
            dcell[1, r:r + 1, :] = jnp.where(keep, pltpu.roll(dv[:, cut], shift, 1), 0.0)


def weights_of(main, side, lo, hi):
    here = main[lo:hi]
    return [
        0.5 * (here + main[lo - 1:hi - 1]),
        0.5 * (here + main[lo + 1:hi + 1]),
        0.5 * (here + left_of(here, side[lo:hi])),
        0.5 * (here + right_of(here, side[lo:hi])),
    ]


def differences(main, side, lo, hi):
    here = main[:, lo:hi, :]
    beside = side[:, lo:hi, :]
    return [
        here - main[:, lo - 1:hi - 1, :],
        here - main[:, lo + 1:hi + 1, :],
        here - left_of(here, beside),
        here - right_of(here, beside),
    ]


def first_kernel(
    last, info, table, frame, side, from_up, from_down, mats, left_edge, right_edge, levels,
    resid_out, local_out, up_out, down_out, main_f, side_f, tcell, dcell, edge,
    vec, total, side_vec, side_total, index_scr,
):
    lane = iota((BLK, CC), 1)
    for c in range(3):
        edge[c] = jnp.where(lane % 4 < 2, right_edge[c], pltpu.roll(left_edge[c], 4, 1))
    level, prow = info[0], info[1]
    inside = grid_mask(prow, last, 0, FR)
    for tile, ref, source in ((0, main_f, frame), (1, side_f, side)):
        for f in range(7):
            out = ref.at[f] if f < 6 else index_scr.at[tile]
            out[...] = source[f]
            out[6:8, :] = from_up[tile, 2 * f:2 * f + 2, :] * inside[6:8]
            out[8 + CR:10 + CR, :] = from_down[tile, 2 * f:2 * f + 2, :] * inside[8 + CR:10 + CR]
    index = [index_scr[tile].astype(jnp.int32) for tile in range(2)]
    tcell[...] = jnp.zeros_like(tcell)
    dcell[...] = jnp.zeros_like(dcell)
    look_up(table, index, tcell, dcell)
    for tile in range(2):
        tcell[tile] = tcell[tile] * inside
    slope = [3.0 * tcell[tile] * tcell[tile] * dcell[tile] for tile in range(2)]
    lo, hi = 7, 7 + EXT
    frames = (main_f, side_f)
    for tile, out in ((0, vec), (1, side_vec)):
        here, beside = frames[tile], frames[1 - tile]
        rhs = jnp.zeros((6, EXT, CC), F32)
        for weight, diff in zip(
            weights_of(slope[tile], slope[1 - tile], lo, hi), differences(here, beside, lo, hi)
        ):
            rhs = rhs - weight[None] * diff
        rhs = rhs * inside[lo:hi][None]
        if tile == 0:
            resid_out[...] = rhs
        out[...] = rhs.reshape(2, BLK, CC)
    local_solve(mats, edge, vec, total, side_vec, side_total, level, levels)
    put_results(total, side_total, local_out, up_out, down_out)


def stiffness(main_f, side_f, main_t, side_t, lo, hi):
    stiff = [t * t * t for t in (main_t[...], side_t[...])]
    out = main_f[:, lo:hi, :]
    parts = differences(main_f, side_f, lo, hi)
    for weight, diff in zip(weights_of(stiff[0], stiff[1], lo, hi), parts):
        out = out + weight[None] * diff
    return out


def second_kernel(
    last, info, local, from_up, from_down, tcell, mats, edge, levels,
    main_f, side_f, image_out, local_out, up_out, down_out,
    vec, total, side_vec, side_total,
):
    level, prow = info[0], info[1]
    frames = (main_f, side_f)
    join(prow, last, local, from_up, from_down, frames)
    lo, hi = 7, 7 + EXT
    inside = grid_mask(prow, last, lo, EXT)
    for tile, out in ((0, vec), (1, side_vec)):
        image = stiffness(
            frames[tile], frames[1 - tile], tcell.at[tile], tcell.at[1 - tile], lo, hi
        ) * inside[None]
        if tile == 0:
            image_out[...] = image
        out[...] = image.reshape(2, BLK, CC)
    local_solve(mats, edge, vec, total, side_vec, side_total, level, levels)
    put_results(total, side_total, local_out, up_out, down_out)


def dot3(a, b, i, j):
    out = jnp.zeros((CR, CC), F32)
    for an, bn in zip(a, b):
        for c in range(3):
            out = out + an[i + c] * bn[j + c]
    return out


def design_sums(n_col, info, frame, values, left_op, right_op):
    cells = frame[6, 8:8 + CR, :].astype(jnp.int32)
    owner = cells // DV
    low = cells % DV
    other = jnp.where((owner // n_col) % 2 == info[1] % 2, 0, 128)
    high = other + (owner // (2 * n_col)) * n_col + owner % n_col
    count = len(values)
    tops = [value.astype(BF16) for value in values]
    rests = [(value - top.astype(F32)).astype(BF16) for value, top in zip(values, tops)]
    for row in range(CR):
        cut = slice(CC * row, CC * row + CC)
        left_op[:, cut] = jnp.where(iota((256, CC), 0) == high[row:row + 1], 1.0, 0.0).astype(BF16)
        hot = jnp.where(iota((DV, CC), 0) == low[row:row + 1], 1.0, 0.0).astype(BF16)
        for k, part in enumerate(tops + rests):
            right_op[k * DV:(k + 1) * DV, cut] = hot * part[row:row + 1]
    sums = lax.dot_general(
        left_op[...], right_op[...], (((1,), (1,)), ((), ())), preferred_element_type=F32
    )
    return sums[:, :count * DV] + sums[:, count * DV:]


LO, HI = 8, 8 + CR


def known_sums_kernel(n_col, info, frame, tcell, dcell, main_f, side_f, out, left_op, right_op):
    known_d = differences(main_f, side_f, LO, HI)
    value = (-3.0 * tcell[0, LO:HI, :] * dcell[0, LO:HI, :]) * dot3(known_d, known_d, 3, 0)
    out[...] = design_sums(n_col, info, frame, [value], left_op, right_op)


def solved_values(tcell, known_d, solved_d):
    t = tcell[0, LO:HI, :]
    slope = -1.5 * t * t
    return [slope * dot3(solved_d, known_d, 3, 0), slope * dot3(known_d, solved_d, 3, 0)]


def solved_sums_kernel(
    n_col, info, frame, tcell, main_f, side_f, zframe, zside, out, left_op, right_op
):
    values = solved_values(
        tcell, differences(main_f, side_f, LO, HI), differences(zframe, zside, LO, HI)
    )
    out[...] = design_sums(n_col, info, frame, values, left_op, right_op)


def third_kernel(
    last, n_col, info, frame, resid, image, zframe, local, from_up, from_down,
    tcell, main_f, side_f, sums0, sums1,
    wframe, keep_out, send_out, wside, left_op, right_op,
):
    join(info[1], last, local, from_up, from_down, (wframe, wside))
    v = stiffness(wframe, wside, tcell.at[0], tcell.at[1], LO, HI)
    r = resid[:, 1:1 + CR, :]
    q = image[:, 1:1 + CR, :]
    z = zframe[:, LO:HI, :]
    w = wframe[:, LO:HI, :]
    lane = iota((1, CC), 1)
    dots = jnp.zeros((1, CC), F32)
    pairs = ((r, z), (z, q), (r, w), (q, w), (z, v), (w, v))
    for k, (a, b) in enumerate(pairs):
        ab = a * b
        for s in range(2):
            part = ab[3 * s] + ab[3 * s + 1] + ab[3 * s + 2]
            value = jnp.sum(jnp.sum(part, axis=0, keepdims=True), axis=1, keepdims=True)
            dots = jnp.where(lane == 2 * k + s, value, dots)
    values = solved_values(
        tcell, differences(main_f, side_f, LO, HI), differences(wframe, wside, LO, HI)
    )
    sums = design_sums(n_col, info, frame, values, left_op, right_op)
    for half, out in ((0, keep_out), (1, send_out)):
        count = out.shape[0]
        rows = slice(128 * half, 128 * half + count)
        out[:, 0:CC] = jnp.broadcast_to(dots, (count, CC))
        out[:, CC:2 * CC] = sums0[rows, :]
        out[:, 2 * CC:4 * CC] = sums1[rows, :]
        out[:, 4 * CC:] = sums[rows]


def last_kernel(got, zframe, wframe, tangent, second, owned):
    sums = jnp.sum(got[...], axis=0, keepdims=True)
    dots = sums[:, 0:CC]
    lane = iota((1, CC), 1)

    def pick(k):
        return jnp.sum(jnp.where(lane == k, dots, 0.0), axis=1, keepdims=True)

    coeffs = []
    for s in range(2):
        rz, zq, rw, qw, zv, wv = (pick(2 * k + s) for k in range(6))
        alpha = rz / zq
        rz1 = rz - alpha * (zq + rw) + alpha * alpha * qw
        grow = 1.0 + rz1 / rz
        pq = grow * grow * zq - grow * alpha * (zv + qw) + alpha * alpha * wv
        alpha1 = rz1 / pq
        coeffs.append((alpha + alpha1 * grow, -alpha1 * alpha))
    for s, out in ((0, tangent), (1, second)):
        c0, c1 = coeffs[s]
        for f in range(3):
            out[f] = c0 * zframe[3 * s + f, 8:8 + CR, :] + c1 * wframe[3 * s + f, 8:8 + CR, :]
    h = [sums[:, (k + 1) * CC:(k + 2) * CC] for k in range(5)]
    owned[...] = (
        h[0] + coeffs[1][0] * h[1] + coeffs[0][0] * h[2] + coeffs[1][1] * h[3] + coeffs[0][1] * h[4]
    )


def ring(axis, count, to_next, to_previous):
    forward = [(i, (i + 1) % count) for i in range(count)]
    backward = [(b, a) for a, b in forward]
    return lax.ppermute(to_next, axis, forward), lax.ppermute(to_previous, axis, backward)


def per_device(state, adjoint, thickness, direction, design_map, levels, blocks):
    n_row, n_col = lax.axis_size(ROW), lax.axis_size("pcol")
    n_dev = n_row * n_col
    last = n_row - 1
    info = jnp.stack([levels[0, 0], lax.axis_index(ROW).astype(jnp.int32)])
    rows = functools.partial(ring, ROW, n_row)
    cols = functools.partial(ring, "pcol", n_col)

    own, frame, first, end = call(
        start_kernel, [(n_dev, 1, 2 * DV), (7, FR, CC), (8, CC), (8, CC)], [SMEM] + [HBM] * 5,
        [
            pltpu.VMEM((6, CR, CC), F32), pltpu.VMEM((CR, CC), jnp.int32),
            pltpu.VMEM((2, 1, DV), F32), pltpu.SemaphoreType.DMA((5,)),
        ],
        work=10**9, limit=LARGE,
    )(info, thickness.reshape(1, DV), direction.reshape(1, DV), state, adjoint, design_map)
    table = lax.all_to_all(own, ROW + ("pcol",), 0, 0, tiled=True).reshape(n_dev, 2 * DV)
    if n_dev < 256:
        table = jnp.concatenate([table, jnp.zeros((256 - n_dev, 2 * DV), F32)], axis=0)
    from_left, from_right = cols(end, first)
    (edge,) = call(edge_kernel, [(3, BLK, CC)], [VMEM] * 2)(blocks, from_left)
    side, up, down, around = call(
        rows_kernel, [(7, FR, CC), (2, 16, CC), (2, 16, CC), (8, CC)], [VMEM] * 3, work=10**11
    )(frame, from_left, from_right)

    solve_scratch = [pltpu.VMEM((2, BLK, CC), F32)] * 4
    resid, local, up, down, main_f, side_f, tcell, dcell, edge = call(
        functools.partial(first_kernel, last),
        [
            (6, EXT, CC), (2, 6, EXT, CC), (2, 24, CC), (2, 24, CC), (6, FR, CC), (6, FR, CC),
            (2, FR, CC), (2, FR, CC), (3, BLK, CC),
        ],
        [SMEM] + [VMEM] * 9,
        solve_scratch + [pltpu.VMEM((2, FR, CC), F32)],
    )(info, table, frame, side, *rows(down, up), blocks, *cols(edge, edge), around)

    def operands(count):
        return [pltpu.VMEM((256, CR * CC), BF16), pltpu.VMEM((2 * count * DV, CR * CC), BF16)]

    (sums0,) = call(
        functools.partial(known_sums_kernel, n_col), [(256, DV)], [SMEM] + [VMEM] * 5, operands(1),
        work=3 * 10**8,
    )(info, frame, tcell, dcell, main_f, side_f)
    zframe, zside, image, local, up, down = call(
        functools.partial(second_kernel, last),
        [(6, FR, CC), (6, FR, CC), (6, EXT, CC), (2, 6, EXT, CC), (2, 24, CC), (2, 24, CC)],
        [SMEM] + [VMEM] * 7,
        solve_scratch,
    )(info, local, *rows(down, up), tcell, blocks, edge, around)
    (sums1,) = call(
        functools.partial(solved_sums_kernel, n_col), [(256, 2 * DV)], [SMEM] + [VMEM] * 6,
        operands(2), work=5 * 10**8,
    )(info, frame, tcell, main_f, side_f, zframe, zside)
    wframe, keep, send = call(
        functools.partial(third_kernel, last, n_col),
        [(6, FR, CC)] + [(n_dev // 2, 6 * CC)] * 2, [SMEM] + [VMEM] * 12,
        [pltpu.VMEM((6, FR, CC), F32)] + operands(2),
    )(info, frame, resid, image, zframe, local, *rows(down, up), tcell, main_f, side_f, sums0, sums1)
    sums = keep + lax.ppermute(send, "core", [(0, 1), (1, 0)])
    got = lax.all_to_all(sums, ("y", "pcol"), 0, 0, tiled=True)
    tangent, second, owned = call(
        last_kernel, [(3, CR, CC), (3, CR, CC), (1, CC)], [VMEM] * 3
    )(got, zframe, wframe)
    return tangent, second, owned.reshape(DV)


def solution(mesh):
    n_row, n_col = mesh.devices.shape
    fine = jax.sharding.Mesh(mesh.devices.reshape(n_row // 2, 2, n_col), ("y", "core", "pcol"))
    field = P(None, ROW, "pcol")
    design = P(("y", "core", "pcol"))
    return jax.shard_map(
        per_device,
        mesh=fine,
        in_specs=(field, field, design, design, P(ROW, "pcol"), P(ROW, "pcol"), P(ROW, None, "pcol")),
        out_specs=(field, field, design),
        check_vma=False,
    )
```

```python
import functools

import jax
import jax.numpy as jnp
from jax import lax
from jax.experimental import pallas as pl
from jax.experimental.pallas import tpu as pltpu
from jax.sharding import PartitionSpec as P

CR = 22
CC = 128
DV = 128
BLK = 72
EXT = CR + 2
FR = 32
ROW = ("y", "core")
WIDE = 3
HALVES = (4, 8, 16, 32, 64)
F32 = jnp.float32
BF16 = jnp.bfloat16

VMEM = pl.BlockSpec(memory_space=pltpu.VMEM)
SMEM = pl.BlockSpec(memory_space=pltpu.SMEM)
HBM = pl.BlockSpec(memory_space=pltpu.HBM)
SMALL = 20 * 1024 * 1024
LARGE = 62 * 1024 * 1024


def call(kernel, out_shapes, in_specs, scratch=(), work=None, limit=SMALL):
    cost = None
    if work is not None:
        cost = pl.CostEstimate(flops=work, bytes_accessed=1 << 20, transcendentals=0)
    return pl.pallas_call(
        kernel,
        out_shape=[jax.ShapeDtypeStruct(s, F32) for s in out_shapes],
        in_specs=list(in_specs),
        out_specs=[VMEM] * len(out_shapes),
        cost_estimate=cost,
        scratch_shapes=list(scratch),
        compiler_params=pltpu.CompilerParams(vmem_limit_bytes=limit),
    )


def iota(shape, dim):
    return lax.broadcasted_iota(jnp.int32, shape, dim)


def pack_edges(tiles, width):
    lane = iota((8, CC), 1)
    first = jnp.zeros((8, CC), F32)
    last = jnp.zeros((8, CC), F32)
    for k, tile in enumerate(tiles):
        at = k * width
        here = (lane >= at) & (lane < at + width)
        first = jnp.where(here, pltpu.roll(tile, at, 1) if at else tile, first)
        last = jnp.where(here, pltpu.roll(tile, at + width, 1), last)
    return first, last


def unpack_edges(from_left, from_right, count, width):
    lane = iota((8, CC), 1)
    tiles = []
    for k in range(count):
        at = k * width
        right = pltpu.roll(from_right, CC - at, 1) if at else from_right
        shift = (CC - width - at) % CC
        left = pltpu.roll(from_left, shift, 1) if shift else from_left
        tiles.append(jnp.where(lane < width, right, jnp.where(lane >= CC - width, left, 0.0)))
    return tiles


def lanes_of(x):
    return iota(x.shape, x.ndim - 1)


def left_of(main, side):
    dim = main.ndim - 1
    return jnp.where(lanes_of(main) == 0, pltpu.roll(side, 1, dim), pltpu.roll(main, 1, dim))


def right_of(main, side):
    dim = main.ndim - 1
    return jnp.where(
        lanes_of(main) == CC - 1, pltpu.roll(side, CC - 1, dim), pltpu.roll(main, CC - 1, dim)
    )


def grid_mask(prow, last, start, rows):
    row = iota((rows, CC), 0) + (start - 8)
    outside = ((row < 0) & (prow == 0)) | ((row >= CR) & (prow == last))
    return jnp.where(outside, 0.0, 1.0).astype(F32)


PIECE = 24
EDGE = 3 * BLK


def start_kernel(
    levels, thickness, direction, state, adjoint, dmap, blocks,
    own_out, frame_out, first_out, last_out,
    level, known, cells, own, mats, sems, block_sems,
):
    copies = [
        pltpu.make_async_copy(thickness, own.at[0], sems.at[0]),
        pltpu.make_async_copy(direction, own.at[1], sems.at[1]),
        pltpu.make_async_copy(state, known.at[0:3], sems.at[2]),
        pltpu.make_async_copy(adjoint, known.at[3:6], sems.at[3]),
        pltpu.make_async_copy(dmap, cells, sems.at[4]),
        pltpu.make_async_copy(levels, level, sems.at[5]),
    ]
    pieces = []
    for k in range(BLK // PIECE):
        cut = pl.ds(k * PIECE, PIECE)
        pieces.append(pltpu.make_async_copy(blocks.at[cut], mats.at[cut], block_sems.at[k]))
    for copy in copies + pieces:
        copy.start()
    frame_out[...] = jnp.zeros_like(frame_out)
    upper = iota((8, CC), 1) >= 64
    for copy in copies:
        copy.wait()
    for k in range(2):
        own_out[:, :, k * DV:(k + 1) * DV] = jnp.broadcast_to(own[k][None], (own_out.shape[0], 1, DV))
    frame_out[0:6, 8:8 + CR, :] = known[...]
    frame_out[6, 8:8 + CR, :] = cells[...].astype(F32)
    tiles = [frame_out[f, 8 + 8 * g:16 + 8 * g, :] for f in range(7) for g in range(3)]
    first, last = pack_edges(tiles, WIDE)
    depth = jnp.broadcast_to(level[...].astype(F32), (8, CC))
    first_out[EDGE:, :] = jnp.where(upper, depth, first)
    last_out[EDGE:, :] = jnp.where(upper, depth, last)
    lane = iota((BLK, CC), 1)
    for c in range(3):
        packed = jnp.zeros((BLK, CC), F32)
        for i in range(min(32, BLK - 32 * c)):
            at = 32 * c + i
            if at % PIECE == 0:
                pieces[at // PIECE].wait()
            mat = mats[at]
            here = ((lane - 4 * i + 2) & (CC - 1)) < 4
            packed = jnp.where(here, pltpu.roll(mat, 4 * i, 1) if i else mat, packed)
        first_out[c * BLK:(c + 1) * BLK, :] = packed
        last_out[c * BLK:(c + 1) * BLK, :] = packed


def rows_kernel(
    frame, from_left, from_right, side_out, up_out, down_out, levels_out, edge_out,
):
    left_end, right_end = from_left[EDGE:, :], from_right[EDGE:, :]
    tiles = unpack_edges(left_end, right_end, 21, WIDE)
    side_out[...] = jnp.zeros_like(side_out)
    for f in range(7):
        for g in range(3):
            side_out[f, 8 + 8 * g:16 + 8 * g, :] = tiles[3 * f + g]
    up_out[...] = jnp.zeros_like(up_out)
    down_out[...] = jnp.zeros_like(down_out)
    for tile, ref in ((0, frame), (1, side_out)):
        for f in range(7):
            up_out[tile, 2 * f:2 * f + 2, :] = ref[f, 8:10, :]
            down_out[tile, 2 * f:2 * f + 2, :] = ref[f, 6 + CR:8 + CR, :]
    upper = iota((8, CC), 1) >= 64
    levels_out[...] = jnp.where(upper, left_end, pltpu.roll(right_end, 64, 1))
    lane = iota((BLK, CC), 1)
    for c in range(3):
        cut = slice(c * BLK, (c + 1) * BLK)
        edge_out[c] = jnp.where(lane % 4 < 2, from_right[cut, :], pltpu.roll(from_left[cut, :], 4, 1))


def apply_blocks(mats, vec):
    one = jnp.zeros((BLK, CC), F32)
    two = jnp.zeros((BLK, CC), F32)
    for at in range(BLK):
        mat = mats[at]
        one = one + mat * vec[0, at:at + 1, :]
        two = two + mat * vec[1, at:at + 1, :]
    return one, two


def over_columns(x):
    for shift in HALVES:
        x = x + pltpu.roll(x, shift, 1)
    return x


def apply_edge(edge, vec):
    row = iota((BLK, CC), 0)
    place = iota((BLK, CC), 1) // 4
    out = jnp.zeros((BLK, CC), F32)
    for c in range(3):
        low, high = 32 * c, min(32 * c + 32, BLK)
        mine = row[low:high] == place[low:high] + 32 * c
        flat = jnp.sum(jnp.where(mine, vec[low:high], 0.0), axis=0, keepdims=True)
        out = out + edge[c] * flat
    return over_columns(out)


def local_solve(mats, edge, vec, total, side_vec, side_total, level, levels):
    lane = iota((BLK, CC), 1)
    ours = (lane < 2) | (lane >= CC - 2)
    for n in range(2):
        side_vec[n] = over_columns(jnp.where(ours, side_vec[n], 0.0))
    total[...] = jnp.zeros_like(total)
    side_total[...] = jnp.zeros_like(side_total)
    top = jnp.maximum(level, jnp.max(levels[...]).astype(jnp.int32))

    def term(order, carry):
        scale = jnp.where(order == 0, 1.0, 0.5).astype(F32)
        keep = jnp.where(order < level, 1.0, 0.0).astype(F32)
        side_keep = levels[0:1, :] > order.astype(F32)
        for n in range(2):
            out = scale * apply_edge(edge, side_vec[n])
            side_vec[n] = out
            side_total[n] += jnp.where(side_keep, out, 0.0)
        for n, out in enumerate(apply_blocks(mats, vec)):
            out = scale * out
            vec[n] = out
            total[n] += keep * out
        return carry

    lax.fori_loop(0, top, term, 0)


def put_results(total, side_total, local_out, up_out, down_out):
    up_out[...] = jnp.zeros_like(up_out)
    down_out[...] = jnp.zeros_like(down_out)
    for tile, ref in ((0, total), (1, side_total)):
        local_out[tile] = ref[...].reshape(6, EXT, CC)
        for f in range(6):
            up_out[tile, 3 * f:3 * f + 3, :] = local_out[tile, f, 0:3, :]
            down_out[tile, 3 * f:3 * f + 3, :] = local_out[tile, f, EXT - 3:EXT, :]


def join(prow, last, local, from_up, from_down, frames):
    inside = grid_mask(prow, last, 0, FR)
    for tile, frame in enumerate(frames):
        frame[...] = jnp.zeros_like(frame)
        frame[:, 7:7 + EXT, :] = local[tile]
        for f in range(6):
            frame[f, 6:9, :] += jnp.where(prow == 0, 0.0, from_up[tile, 3 * f:3 * f + 3, :])
            frame[f, 7 + CR:10 + CR, :] += jnp.where(prow == last, 0.0, from_down[tile, 3 * f:3 * f + 3, :])
        frame[...] = frame[...] * inside[None]


def look_up(table, index, tcell, dcell):
    flipped = table[...].T
    part0 = flipped.astype(BF16)
    part1 = (flipped - part0.astype(F32)).astype(BF16)
    lhs = jnp.concatenate([part0, part1], axis=0)
    high = [ix // DV for ix in index]
    low = [ix % DV for ix in index]
    lane1 = iota((1, CC), 1)

    def both(vh, vl):
        hot = jnp.where(iota((256, 2 * CC), 0) == vh, 1.0, 0.0).astype(BF16)
        got = jnp.dot(lhs, hot, preferred_element_type=F32)
        mine = iota((DV, 2 * CC), 0) == vl
        tv = jnp.sum(jnp.where(mine, got[0:DV] + got[2 * DV:3 * DV], 0.0), axis=0, keepdims=True)
        dv = jnp.sum(jnp.where(mine, got[DV:2 * DV] + got[3 * DV:4 * DV], 0.0), axis=0, keepdims=True)
        return tv, dv

    for r in range(6, FR, 2):
        vh = jnp.concatenate([high[0][r:r + 1], high[0][r + 1:r + 2]], axis=1)
        vl = jnp.concatenate([low[0][r:r + 1], low[0][r + 1:r + 2]], axis=1)
        tv, dv = both(vh, vl)
        for h in range(2):
            tcell[0, r + h:r + h + 1, :] = tv[:, h * CC:(h + 1) * CC]
            dcell[0, r + h:r + h + 1, :] = dv[:, h * CC:(h + 1) * CC]
    packs = []
    for half in range(2):
        vec = jnp.zeros((1, CC), jnp.int32)
        for i in range(16):
            r = 16 * half + i
            vec = jnp.where(lane1 // 8 == i, pltpu.roll(index[1][r:r + 1], (8 * i + 4) % CC, 1), vec)
        packs.append(vec)
    vec = jnp.concatenate(packs, axis=1)
    tv, dv = both(vec // DV, vec % DV)
    for half in range(2):
        for i in range(16):
            r = 16 * half + i
            shift = (CC - 8 * i - 4) % CC
            keep = (lane1 < 4) | (lane1 >= CC - 4)
            cut = slice(half * CC, (half + 1) * CC)
            tcell[1, r:r + 1, :] = jnp.where(keep, pltpu.roll(tv[:, cut], shift, 1), 0.0)
            dcell[1, r:r + 1, :] = jnp.where(keep, pltpu.roll(dv[:, cut], shift, 1), 0.0)


def weights_of(main, side, lo, hi):
    here = main[lo:hi]
    return [
        0.5 * (here + main[lo - 1:hi - 1]),
        0.5 * (here + main[lo + 1:hi + 1]),
        0.5 * (here + left_of(here, side[lo:hi])),
        0.5 * (here + right_of(here, side[lo:hi])),
    ]


def differences(main, side, lo, hi):
    here = main[:, lo:hi, :]
    beside = side[:, lo:hi, :]
    return [
        here - main[:, lo - 1:hi - 1, :],
        here - main[:, lo + 1:hi + 1, :],
        here - left_of(here, beside),
        here - right_of(here, beside),
    ]


def first_kernel(
    last, info, table, frame, side, from_up, from_down, mats, edge, levels,
    resid_out, local_out, up_out, down_out, main_f, side_f, tcell, dcell,
    vec, total, side_vec, side_total, index_scr,
):
    level, prow = info[0], info[1]
    inside = grid_mask(prow, last, 0, FR)
    for tile, ref, source in ((0, main_f, frame), (1, side_f, side)):
        for f in range(7):
            out = ref.at[f] if f < 6 else index_scr.at[tile]
            out[...] = source[f]
            out[6:8, :] = from_up[tile, 2 * f:2 * f + 2, :] * inside[6:8]
            out[8 + CR:10 + CR, :] = from_down[tile, 2 * f:2 * f + 2, :] * inside[8 + CR:10 + CR]
    index = [index_scr[tile].astype(jnp.int32) for tile in range(2)]
    tcell[...] = jnp.zeros_like(tcell)
    dcell[...] = jnp.zeros_like(dcell)
    look_up(table, index, tcell, dcell)
    for tile in range(2):
        tcell[tile] = tcell[tile] * inside
    slope = [3.0 * tcell[tile] * tcell[tile] * dcell[tile] for tile in range(2)]
    lo, hi = 7, 7 + EXT
    frames = (main_f, side_f)
    for tile, out in ((0, vec), (1, side_vec)):
        here, beside = frames[tile], frames[1 - tile]
        rhs = jnp.zeros((6, EXT, CC), F32)
        for weight, diff in zip(
            weights_of(slope[tile], slope[1 - tile], lo, hi), differences(here, beside, lo, hi)
        ):
            rhs = rhs - weight[None] * diff
        rhs = rhs * inside[lo:hi][None]
        if tile == 0:
            resid_out[...] = rhs
        out[...] = rhs.reshape(2, BLK, CC)
    local_solve(mats, edge, vec, total, side_vec, side_total, level, levels)
    put_results(total, side_total, local_out, up_out, down_out)


def stiffness(main_f, side_f, main_t, side_t, lo, hi):
    stiff = [t * t * t for t in (main_t[...], side_t[...])]
    out = main_f[:, lo:hi, :]
    parts = differences(main_f, side_f, lo, hi)
    for weight, diff in zip(weights_of(stiff[0], stiff[1], lo, hi), parts):
        out = out + weight[None] * diff
    return out


def second_kernel(
    last, info, local, from_up, from_down, tcell, mats, edge, levels,
    main_f, side_f, image_out, local_out, up_out, down_out,
    vec, total, side_vec, side_total,
):
    level, prow = info[0], info[1]
    frames = (main_f, side_f)
    join(prow, last, local, from_up, from_down, frames)
    lo, hi = 7, 7 + EXT
    inside = grid_mask(prow, last, lo, EXT)
    for tile, out in ((0, vec), (1, side_vec)):
        image = stiffness(
            frames[tile], frames[1 - tile], tcell.at[tile], tcell.at[1 - tile], lo, hi
        ) * inside[None]
        if tile == 0:
            image_out[...] = image
        out[...] = image.reshape(2, BLK, CC)
    local_solve(mats, edge, vec, total, side_vec, side_total, level, levels)
    put_results(total, side_total, local_out, up_out, down_out)


def dot3(a, b, i, j):
    out = jnp.zeros((CR, CC), F32)
    for an, bn in zip(a, b):
        for c in range(3):
            out = out + an[i + c] * bn[j + c]
    return out


def design_sums(n_col, info, frame, values, left_op, right_op):
    cells = frame[6, 8:8 + CR, :].astype(jnp.int32)
    owner = cells // DV
    low = cells % DV
    other = jnp.where((owner // n_col) % 2 == info[1] % 2, 0, 128)
    high = other + (owner // (2 * n_col)) * n_col + owner % n_col
    count = len(values)
    tops = [value.astype(BF16) for value in values]
    rests = [(value - top.astype(F32)).astype(BF16) for value, top in zip(values, tops)]
    for row in range(CR):
        cut = slice(CC * row, CC * row + CC)
        left_op[:, cut] = jnp.where(iota((256, CC), 0) == high[row:row + 1], 1.0, 0.0).astype(BF16)
        hot = jnp.where(iota((DV, CC), 0) == low[row:row + 1], 1.0, 0.0).astype(BF16)
        for k, part in enumerate(tops + rests):
            right_op[k * DV:(k + 1) * DV, cut] = hot * part[row:row + 1]
    sums = lax.dot_general(
        left_op[...], right_op[...], (((1,), (1,)), ((), ())), preferred_element_type=F32
    )
    return sums[:, :count * DV] + sums[:, count * DV:]


LO, HI = 8, 8 + CR


def known_sums_kernel(n_col, info, frame, tcell, dcell, main_f, side_f, out, left_op, right_op):
    known_d = differences(main_f, side_f, LO, HI)
    value = (-3.0 * tcell[0, LO:HI, :] * dcell[0, LO:HI, :]) * dot3(known_d, known_d, 3, 0)
    out[...] = design_sums(n_col, info, frame, [value], left_op, right_op)


def solved_values(tcell, known_d, solved_d):
    t = tcell[0, LO:HI, :]
    slope = -1.5 * t * t
    return [slope * dot3(solved_d, known_d, 3, 0), slope * dot3(known_d, solved_d, 3, 0)]


def solved_sums_kernel(
    n_col, info, frame, tcell, main_f, side_f, zframe, zside, out, left_op, right_op
):
    values = solved_values(
        tcell, differences(main_f, side_f, LO, HI), differences(zframe, zside, LO, HI)
    )
    out[...] = design_sums(n_col, info, frame, values, left_op, right_op)


def third_kernel(
    last, n_col, info, frame, resid, image, zframe, local, from_up, from_down,
    tcell, main_f, side_f, sums0, sums1,
    wframe, keep_out, send_out, wside, left_op, right_op,
):
    join(info[1], last, local, from_up, from_down, (wframe, wside))
    v = stiffness(wframe, wside, tcell.at[0], tcell.at[1], LO, HI)
    r = resid[:, 1:1 + CR, :]
    q = image[:, 1:1 + CR, :]
    z = zframe[:, LO:HI, :]
    w = wframe[:, LO:HI, :]
    lane = iota((1, CC), 1)
    dots = jnp.zeros((1, CC), F32)
    pairs = ((r, z), (z, q), (r, w), (q, w), (z, v), (w, v))
    for k, (a, b) in enumerate(pairs):
        ab = a * b
        for s in range(2):
            part = ab[3 * s] + ab[3 * s + 1] + ab[3 * s + 2]
            value = jnp.sum(jnp.sum(part, axis=0, keepdims=True), axis=1, keepdims=True)
            dots = jnp.where(lane == 2 * k + s, value, dots)
    values = solved_values(
        tcell, differences(main_f, side_f, LO, HI), differences(wframe, wside, LO, HI)
    )
    sums = design_sums(n_col, info, frame, values, left_op, right_op)
    for half, out in ((0, keep_out), (1, send_out)):
        count = out.shape[0]
        rows = slice(128 * half, 128 * half + count)
        out[:, 0:CC] = jnp.broadcast_to(dots, (count, CC))
        out[:, CC:2 * CC] = sums0[rows, :]
        out[:, 2 * CC:4 * CC] = sums1[rows, :]
        out[:, 4 * CC:] = sums[rows]


def last_kernel(got, zframe, wframe, tangent, second, owned):
    sums = jnp.sum(got[...], axis=0, keepdims=True)
    dots = sums[:, 0:CC]
    lane = iota((1, CC), 1)

    def pick(k):
        return jnp.sum(jnp.where(lane == k, dots, 0.0), axis=1, keepdims=True)

    coeffs = []
    for s in range(2):
        rz, zq, rw, qw, zv, wv = (pick(2 * k + s) for k in range(6))
        alpha = rz / zq
        rz1 = rz - alpha * (zq + rw) + alpha * alpha * qw
        grow = 1.0 + rz1 / rz
        pq = grow * grow * zq - grow * alpha * (zv + qw) + alpha * alpha * wv
        alpha1 = rz1 / pq
        coeffs.append((alpha + alpha1 * grow, -alpha1 * alpha))
    for s, out in ((0, tangent), (1, second)):
        c0, c1 = coeffs[s]
        for f in range(3):
            out[f] = c0 * zframe[3 * s + f, 8:8 + CR, :] + c1 * wframe[3 * s + f, 8:8 + CR, :]
    h = [sums[:, (k + 1) * CC:(k + 2) * CC] for k in range(5)]
    owned[...] = (
        h[0] + coeffs[1][0] * h[1] + coeffs[0][0] * h[2] + coeffs[1][1] * h[3] + coeffs[0][1] * h[4]
    )


def ring(axis, count, to_next, to_previous):
    forward = [(i, (i + 1) % count) for i in range(count)]
    backward = [(b, a) for a, b in forward]
    return lax.ppermute(to_next, axis, forward), lax.ppermute(to_previous, axis, backward)


def per_device(state, adjoint, thickness, direction, design_map, levels, blocks):
    n_row, n_col = lax.axis_size(ROW), lax.axis_size("pcol")
    n_dev = n_row * n_col
    last = n_row - 1
    info = jnp.stack([levels[0, 0], lax.axis_index(ROW).astype(jnp.int32)])
    rows = functools.partial(ring, ROW, n_row)
    cols = functools.partial(ring, "pcol", n_col)

    own, frame, first, end = call(
        start_kernel, [(n_dev, 1, 2 * DV), (7, FR, CC), (EDGE + 8, CC), (EDGE + 8, CC)], [HBM] * 7,
        [
            pltpu.VMEM((1, 1), jnp.int32), pltpu.VMEM((6, CR, CC), F32),
            pltpu.VMEM((CR, CC), jnp.int32), pltpu.VMEM((2, 1, DV), F32),
            pltpu.VMEM((BLK, BLK, CC), F32), pltpu.SemaphoreType.DMA((6,)),
            pltpu.SemaphoreType.DMA((BLK // PIECE,)),
        ],
        work=10**9, limit=LARGE,
    )(levels, thickness.reshape(1, DV), direction.reshape(1, DV), state, adjoint, design_map, blocks)
    table = lax.all_to_all(own, ROW + ("pcol",), 0, 0, tiled=True).reshape(n_dev, 2 * DV)
    if n_dev < 256:
        table = jnp.concatenate([table, jnp.zeros((256 - n_dev, 2 * DV), F32)], axis=0)
    from_left, from_right = cols(end, first)
    side, up, down, around, edge = call(
        rows_kernel, [(7, FR, CC), (2, 16, CC), (2, 16, CC), (8, CC), (3, BLK, CC)], [VMEM] * 3,
        work=10**11,
    )(frame, from_left, from_right)

    solve_scratch = [pltpu.VMEM((2, BLK, CC), F32)] * 4
    resid, local, up, down, main_f, side_f, tcell, dcell = call(
        functools.partial(first_kernel, last),
        [
            (6, EXT, CC), (2, 6, EXT, CC), (2, 24, CC), (2, 24, CC), (6, FR, CC), (6, FR, CC),
            (2, FR, CC), (2, FR, CC),
        ],
        [SMEM] + [VMEM] * 8,
        solve_scratch + [pltpu.VMEM((2, FR, CC), F32)],
    )(info, table, frame, side, *rows(down, up), blocks, edge, around)

    def operands(count):
        return [pltpu.VMEM((256, CR * CC), BF16), pltpu.VMEM((2 * count * DV, CR * CC), BF16)]

    (sums0,) = call(
        functools.partial(known_sums_kernel, n_col), [(256, DV)], [SMEM] + [VMEM] * 5, operands(1),
        work=3 * 10**8,
    )(info, frame, tcell, dcell, main_f, side_f)
    zframe, zside, image, local, up, down = call(
        functools.partial(second_kernel, last),
        [(6, FR, CC), (6, FR, CC), (6, EXT, CC), (2, 6, EXT, CC), (2, 24, CC), (2, 24, CC)],
        [SMEM] + [VMEM] * 7,
        solve_scratch,
    )(info, local, *rows(down, up), tcell, blocks, edge, around)
    (sums1,) = call(
        functools.partial(solved_sums_kernel, n_col), [(256, 2 * DV)], [SMEM] + [VMEM] * 6,
        operands(2), work=5 * 10**8,
    )(info, frame, tcell, main_f, side_f, zframe, zside)
    wframe, keep, send = call(
        functools.partial(third_kernel, last, n_col),
        [(6, FR, CC)] + [(n_dev // 2, 6 * CC)] * 2, [SMEM] + [VMEM] * 12,
        [pltpu.VMEM((6, FR, CC), F32)] + operands(2),
    )(info, frame, resid, image, zframe, local, *rows(down, up), tcell, main_f, side_f, sums0, sums1)
    sums = keep + lax.ppermute(send, "core", [(0, 1), (1, 0)])
    got = lax.all_to_all(sums, ("y", "pcol"), 0, 0, tiled=True)
    tangent, second, owned = call(
        last_kernel, [(3, CR, CC), (3, CR, CC), (1, CC)], [VMEM] * 3
    )(got, zframe, wframe)
    return tangent, second, owned.reshape(DV)


def solution(mesh):
    n_row, n_col = mesh.devices.shape
    fine = jax.sharding.Mesh(mesh.devices.reshape(n_row // 2, 2, n_col), ("y", "core", "pcol"))
    field = P(None, ROW, "pcol")
    design = P(("y", "core", "pcol"))
    return jax.shard_map(
        per_device,
        mesh=fine,
        in_specs=(field, field, design, design, P(ROW, "pcol"), P(ROW, "pcol"), P(ROW, None, "pcol")),
        out_specs=(field, field, design),
        check_vma=False,
    )
```

```python
import functools

import jax
import jax.numpy as jnp
from jax import lax
from jax.experimental import pallas as pl
from jax.experimental.pallas import tpu as pltpu
from jax.sharding import PartitionSpec as P

CR = 22
CC = 128
DV = 128
BLK = 72
EXT = CR + 2
FR = 32
ROW = ("y", "core")
WIDE = 3
HALVES = (4, 8, 16, 32, 64)
F32 = jnp.float32
BF16 = jnp.bfloat16

VMEM = pl.BlockSpec(memory_space=pltpu.VMEM)
SMEM = pl.BlockSpec(memory_space=pltpu.SMEM)
HBM = pl.BlockSpec(memory_space=pltpu.HBM)
SMALL = 20 * 1024 * 1024
LARGE = 62 * 1024 * 1024


def call(kernel, out_shapes, in_specs, scratch=(), work=None, limit=SMALL, outs=None):
    cost = None
    if work is not None:
        cost = pl.CostEstimate(flops=work, bytes_accessed=1 << 20, transcendentals=0)
    return pl.pallas_call(
        kernel,
        out_shape=[
            s if isinstance(s, jax.ShapeDtypeStruct) else jax.ShapeDtypeStruct(s, F32)
            for s in out_shapes
        ],
        in_specs=list(in_specs),
        out_specs=[VMEM] * len(out_shapes) if outs is None else outs,
        cost_estimate=cost,
        scratch_shapes=list(scratch),
        compiler_params=pltpu.CompilerParams(vmem_limit_bytes=limit),
    )


def iota(shape, dim):
    return lax.broadcasted_iota(jnp.int32, shape, dim)


def pack_edges(tiles, width):
    lane = iota((8, CC), 1)
    first = jnp.zeros((8, CC), F32)
    last = jnp.zeros((8, CC), F32)
    for k, tile in enumerate(tiles):
        at = k * width
        here = (lane >= at) & (lane < at + width)
        first = jnp.where(here, pltpu.roll(tile, at, 1) if at else tile, first)
        last = jnp.where(here, pltpu.roll(tile, at + width, 1), last)
    return first, last


def unpack_edges(from_left, from_right, count, width):
    lane = iota((8, CC), 1)
    tiles = []
    for k in range(count):
        at = k * width
        right = pltpu.roll(from_right, CC - at, 1) if at else from_right
        shift = (CC - width - at) % CC
        left = pltpu.roll(from_left, shift, 1) if shift else from_left
        tiles.append(jnp.where(lane < width, right, jnp.where(lane >= CC - width, left, 0.0)))
    return tiles


def lanes_of(x):
    return iota(x.shape, x.ndim - 1)


def left_of(main, side):
    dim = main.ndim - 1
    return jnp.where(lanes_of(main) == 0, pltpu.roll(side, 1, dim), pltpu.roll(main, 1, dim))


def right_of(main, side):
    dim = main.ndim - 1
    return jnp.where(
        lanes_of(main) == CC - 1, pltpu.roll(side, CC - 1, dim), pltpu.roll(main, CC - 1, dim)
    )


def grid_mask(prow, last, start, rows):
    row = iota((rows, CC), 0) + (start - 8)
    outside = ((row < 0) & (prow == 0)) | ((row >= CR) & (prow == last))
    return jnp.where(outside, 0.0, 1.0).astype(F32)


PIECE = 24
EDGE = 3 * BLK


def start_kernel(
    levels, thickness, direction, state, adjoint, dmap, blocks,
    own_out, frame_out, first_out, last_out,
    level, known, cells, own, many, mats, sems, block_sems,
):
    copies = [
        pltpu.make_async_copy(thickness, own.at[0], sems.at[0]),
        pltpu.make_async_copy(direction, own.at[1], sems.at[1]),
        pltpu.make_async_copy(state, known.at[0:3], sems.at[2]),
        pltpu.make_async_copy(adjoint, known.at[3:6], sems.at[3]),
        pltpu.make_async_copy(dmap, cells, sems.at[4]),
        pltpu.make_async_copy(levels, level, sems.at[5]),
    ]
    pieces = []
    for k in range(BLK // PIECE):
        cut = pl.ds(k * PIECE, PIECE)
        pieces.append(pltpu.make_async_copy(blocks.at[cut], mats.at[cut], block_sems.at[k]))
    for copy in copies + pieces:
        copy.start()
    frame_out[...] = jnp.zeros_like(frame_out)
    upper = iota((8, CC), 1) >= 64
    for copy in copies:
        copy.wait()
    for k in range(2):
        many[:, :, k * DV:(k + 1) * DV] = jnp.broadcast_to(own[k][None], (many.shape[0], 1, DV))
    written = pltpu.make_async_copy(many, own_out, sems.at[6])
    written.start()
    frame_out[0:6, 8:8 + CR, :] = known[...]
    frame_out[6, 8:8 + CR, :] = cells[...].astype(F32)
    tiles = [frame_out[f, 8 + 8 * g:16 + 8 * g, :] for f in range(7) for g in range(3)]
    first, last = pack_edges(tiles, WIDE)
    depth = jnp.broadcast_to(level[...].astype(F32), (8, CC))
    first_out[EDGE:, :] = jnp.where(upper, depth, first)
    last_out[EDGE:, :] = jnp.where(upper, depth, last)
    lane = iota((BLK, CC), 1)
    for c in range(3):
        packed = jnp.zeros((BLK, CC), F32)
        for i in range(min(32, BLK - 32 * c)):
            at = 32 * c + i
            if at % PIECE == 0:
                pieces[at // PIECE].wait()
            mat = mats[at]
            here = ((lane - 4 * i + 2) & (CC - 1)) < 4
            packed = jnp.where(here, pltpu.roll(mat, 4 * i, 1) if i else mat, packed)
        first_out[c * BLK:(c + 1) * BLK, :] = packed
        last_out[c * BLK:(c + 1) * BLK, :] = packed
    written.wait()


def rows_kernel(
    frame, from_left, from_right, side_out, up_out, down_out, levels_out, edge_out,
):
    left_end, right_end = from_left[EDGE:, :], from_right[EDGE:, :]
    tiles = unpack_edges(left_end, right_end, 21, WIDE)
    side_out[...] = jnp.zeros_like(side_out)
    for f in range(7):
        for g in range(3):
            side_out[f, 8 + 8 * g:16 + 8 * g, :] = tiles[3 * f + g]
    up_out[...] = jnp.zeros_like(up_out)
    down_out[...] = jnp.zeros_like(down_out)
    for tile, ref in ((0, frame), (1, side_out)):
        for f in range(7):
            up_out[tile, 2 * f:2 * f + 2, :] = ref[f, 8:10, :]
            down_out[tile, 2 * f:2 * f + 2, :] = ref[f, 6 + CR:8 + CR, :]
    upper = iota((8, CC), 1) >= 64
    levels_out[...] = jnp.where(upper, left_end, pltpu.roll(right_end, 64, 1))
    lane = iota((BLK, CC), 1)
    for c in range(3):
        cut = slice(c * BLK, (c + 1) * BLK)
        edge_out[c] = jnp.where(lane % 4 < 2, from_right[cut, :], pltpu.roll(from_left[cut, :], 4, 1))


def apply_blocks(mats, vec):
    one = jnp.zeros((BLK, CC), F32)
    two = jnp.zeros((BLK, CC), F32)
    for at in range(BLK):
        mat = mats[at]
        one = one + mat * vec[0, at:at + 1, :]
        two = two + mat * vec[1, at:at + 1, :]
    return one, two


def over_columns(x):
    for shift in HALVES:
        x = x + pltpu.roll(x, shift, 1)
    return x


def apply_edge(edge, vec):
    row = iota((BLK, CC), 0)
    place = iota((BLK, CC), 1) // 4
    out = jnp.zeros((BLK, CC), F32)
    for c in range(3):
        low, high = 32 * c, min(32 * c + 32, BLK)
        mine = row[low:high] == place[low:high] + 32 * c
        flat = jnp.sum(jnp.where(mine, vec[low:high], 0.0), axis=0, keepdims=True)
        out = out + edge[c] * flat
    return over_columns(out)


def local_solve(mats, edge, vec, total, side_vec, side_total, level, levels):
    lane = iota((BLK, CC), 1)
    ours = (lane < 2) | (lane >= CC - 2)
    for n in range(2):
        side_vec[n] = over_columns(jnp.where(ours, side_vec[n], 0.0))
    total[...] = jnp.zeros_like(total)
    side_total[...] = jnp.zeros_like(side_total)
    top = jnp.maximum(level, jnp.max(levels[...]).astype(jnp.int32))

    def term(order, carry):
        scale = jnp.where(order == 0, 1.0, 0.5).astype(F32)
        keep = jnp.where(order < level, 1.0, 0.0).astype(F32)
        side_keep = levels[0:1, :] > order.astype(F32)
        for n in range(2):
            out = scale * apply_edge(edge, side_vec[n])
            side_vec[n] = out
            side_total[n] += jnp.where(side_keep, out, 0.0)
        for n, out in enumerate(apply_blocks(mats, vec)):
            out = scale * out
            vec[n] = out
            total[n] += keep * out
        return carry

    lax.fori_loop(0, top, term, 0)


def put_results(total, side_total, local_out, up_out, down_out):
    up_out[...] = jnp.zeros_like(up_out)
    down_out[...] = jnp.zeros_like(down_out)
    for tile, ref in ((0, total), (1, side_total)):
        local_out[tile] = ref[...].reshape(6, EXT, CC)
        for f in range(6):
            up_out[tile, 3 * f:3 * f + 3, :] = local_out[tile, f, 0:3, :]
            down_out[tile, 3 * f:3 * f + 3, :] = local_out[tile, f, EXT - 3:EXT, :]


def join(prow, last, local, from_up, from_down, frames):
    inside = grid_mask(prow, last, 0, FR)
    for tile, frame in enumerate(frames):
        frame[...] = jnp.zeros_like(frame)
        frame[:, 7:7 + EXT, :] = local[tile]
        for f in range(6):
            frame[f, 6:9, :] += jnp.where(prow == 0, 0.0, from_up[tile, 3 * f:3 * f + 3, :])
            frame[f, 7 + CR:10 + CR, :] += jnp.where(prow == last, 0.0, from_down[tile, 3 * f:3 * f + 3, :])
        frame[...] = frame[...] * inside[None]


PAIRS = range(6, FR, 2)


def place_cells(index, cells):
    lane1 = iota((1, CC), 1)
    vecs = [jnp.concatenate([index[0][r:r + 1], index[0][r + 1:r + 2]], axis=1) for r in PAIRS]
    packs = []
    for half in range(2):
        vec = jnp.zeros((1, CC), jnp.int32)
        for i in range(16):
            r = 16 * half + i
            vec = jnp.where(lane1 // 8 == i, pltpu.roll(index[1][r:r + 1], (8 * i + 4) % CC, 1), vec)
        packs.append(vec)
    vecs.append(jnp.concatenate(packs, axis=1))
    for k, vec in enumerate(vecs):
        cells[k:k + 1, :] = vec


def look_up(table, cells, tcell, dcell):
    flipped = table[...].T
    part0 = flipped.astype(BF16)
    part1 = (flipped - part0.astype(F32)).astype(BF16)
    lhs = jnp.concatenate([part0, part1], axis=0)
    lane1 = iota((1, CC), 1)

    def both(k):
        vec = cells[k:k + 1, :]
        hot = jnp.where(iota((256, 2 * CC), 0) == vec // DV, 1.0, 0.0).astype(BF16)
        got = jnp.dot(lhs, hot, preferred_element_type=F32)
        mine = iota((DV, 2 * CC), 0) == vec % DV
        tv = jnp.sum(jnp.where(mine, got[0:DV] + got[2 * DV:3 * DV], 0.0), axis=0, keepdims=True)
        dv = jnp.sum(jnp.where(mine, got[DV:2 * DV] + got[3 * DV:4 * DV], 0.0), axis=0, keepdims=True)
        return tv, dv

    for k, r in enumerate(PAIRS):
        tv, dv = both(k)
        for h in range(2):
            tcell[0, r + h:r + h + 1, :] = tv[:, h * CC:(h + 1) * CC]
            dcell[0, r + h:r + h + 1, :] = dv[:, h * CC:(h + 1) * CC]
    tv, dv = both(len(PAIRS))
    for half in range(2):
        for i in range(16):
            r = 16 * half + i
            shift = (CC - 8 * i - 4) % CC
            keep = (lane1 < 4) | (lane1 >= CC - 4)
            cut = slice(half * CC, (half + 1) * CC)
            tcell[1, r:r + 1, :] = jnp.where(keep, pltpu.roll(tv[:, cut], shift, 1), 0.0)
            dcell[1, r:r + 1, :] = jnp.where(keep, pltpu.roll(dv[:, cut], shift, 1), 0.0)


def weights_of(main, side, lo, hi):
    here = main[lo:hi]
    return [
        0.5 * (here + main[lo - 1:hi - 1]),
        0.5 * (here + main[lo + 1:hi + 1]),
        0.5 * (here + left_of(here, side[lo:hi])),
        0.5 * (here + right_of(here, side[lo:hi])),
    ]


def differences(main, side, lo, hi):
    here = main[:, lo:hi, :]
    beside = side[:, lo:hi, :]
    return [
        here - main[:, lo - 1:hi - 1, :],
        here - main[:, lo + 1:hi + 1, :],
        here - left_of(here, beside),
        here - right_of(here, beside),
    ]


def place_kernel(last, info, frame, side, from_up, from_down, main_f, side_f, cells, index_scr):
    inside = grid_mask(info[1], last, 0, FR)
    for tile, ref, source in ((0, main_f, frame), (1, side_f, side)):
        for f in range(7):
            out = ref.at[f] if f < 6 else index_scr.at[tile]
            out[...] = source[f]
            out[6:8, :] = from_up[tile, 2 * f:2 * f + 2, :] * inside[6:8]
            out[8 + CR:10 + CR, :] = from_down[tile, 2 * f:2 * f + 2, :] * inside[8 + CR:10 + CR]
    place_cells([index_scr[tile].astype(jnp.int32) for tile in range(2)], cells)


def first_kernel(
    last, info, table, main_f, side_f, cells, mats, edge, levels,
    resid_out, local_out, up_out, down_out, tcell, dcell,
    vec, total, side_vec, side_total,
):
    level, prow = info[0], info[1]
    inside = grid_mask(prow, last, 0, FR)
    tcell[...] = jnp.zeros_like(tcell)
    dcell[...] = jnp.zeros_like(dcell)
    look_up(table, cells, tcell, dcell)
    for tile in range(2):
        tcell[tile] = tcell[tile] * inside
    slope = [3.0 * tcell[tile] * tcell[tile] * dcell[tile] for tile in range(2)]
    lo, hi = 7, 7 + EXT
    frames = (main_f, side_f)
    for tile, out in ((0, vec), (1, side_vec)):
        here, beside = frames[tile], frames[1 - tile]
        rhs = jnp.zeros((6, EXT, CC), F32)
        for weight, diff in zip(
            weights_of(slope[tile], slope[1 - tile], lo, hi), differences(here, beside, lo, hi)
        ):
            rhs = rhs - weight[None] * diff
        rhs = rhs * inside[lo:hi][None]
        if tile == 0:
            resid_out[...] = rhs
        out[...] = rhs.reshape(2, BLK, CC)
    local_solve(mats, edge, vec, total, side_vec, side_total, level, levels)
    put_results(total, side_total, local_out, up_out, down_out)


def stiffness(main_f, side_f, main_t, side_t, lo, hi):
    stiff = [t * t * t for t in (main_t[...], side_t[...])]
    out = main_f[:, lo:hi, :]
    parts = differences(main_f, side_f, lo, hi)
    for weight, diff in zip(weights_of(stiff[0], stiff[1], lo, hi), parts):
        out = out + weight[None] * diff
    return out


def second_kernel(
    last, info, local, from_up, from_down, tcell, mats, edge, levels,
    main_f, side_f, image_out, local_out, up_out, down_out,
    vec, total, side_vec, side_total,
):
    level, prow = info[0], info[1]
    frames = (main_f, side_f)
    join(prow, last, local, from_up, from_down, frames)
    lo, hi = 7, 7 + EXT
    inside = grid_mask(prow, last, lo, EXT)
    for tile, out in ((0, vec), (1, side_vec)):
        image = stiffness(
            frames[tile], frames[1 - tile], tcell.at[tile], tcell.at[1 - tile], lo, hi
        ) * inside[None]
        if tile == 0:
            image_out[...] = image
        out[...] = image.reshape(2, BLK, CC)
    local_solve(mats, edge, vec, total, side_vec, side_total, level, levels)
    put_results(total, side_total, local_out, up_out, down_out)


def dot3(a, b, i, j):
    out = jnp.zeros((CR, CC), F32)
    for an, bn in zip(a, b):
        for c in range(3):
            out = out + an[i + c] * bn[j + c]
    return out


def design_sums(n_col, info, frame, values, left_op, right_op):
    cells = frame[6, 8:8 + CR, :].astype(jnp.int32)
    owner = cells // DV
    low = cells % DV
    other = jnp.where((owner // n_col) % 2 == info[1] % 2, 0, 128)
    high = other + (owner // (2 * n_col)) * n_col + owner % n_col
    count = len(values)
    tops = [value.astype(BF16) for value in values]
    rests = [(value - top.astype(F32)).astype(BF16) for value, top in zip(values, tops)]
    for row in range(CR):
        cut = slice(CC * row, CC * row + CC)
        left_op[:, cut] = jnp.where(iota((256, CC), 0) == high[row:row + 1], 1.0, 0.0).astype(BF16)
        hot = jnp.where(iota((DV, CC), 0) == low[row:row + 1], 1.0, 0.0).astype(BF16)
        for k, part in enumerate(tops + rests):
            right_op[k * DV:(k + 1) * DV, cut] = hot * part[row:row + 1]
    sums = lax.dot_general(
        left_op[...], right_op[...], (((1,), (1,)), ((), ())), preferred_element_type=F32
    )
    return sums[:, :count * DV] + sums[:, count * DV:]


LO, HI = 8, 8 + CR


def known_sums_kernel(n_col, info, frame, tcell, dcell, main_f, side_f, out, left_op, right_op):
    known_d = differences(main_f, side_f, LO, HI)
    value = (-3.0 * tcell[0, LO:HI, :] * dcell[0, LO:HI, :]) * dot3(known_d, known_d, 3, 0)
    out[...] = design_sums(n_col, info, frame, [value], left_op, right_op)


def solved_values(tcell, known_d, solved_d):
    t = tcell[0, LO:HI, :]
    slope = -1.5 * t * t
    return [slope * dot3(solved_d, known_d, 3, 0), slope * dot3(known_d, solved_d, 3, 0)]


def solved_sums_kernel(
    n_col, info, frame, tcell, main_f, side_f, zframe, zside, out, left_op, right_op
):
    values = solved_values(
        tcell, differences(main_f, side_f, LO, HI), differences(zframe, zside, LO, HI)
    )
    out[...] = design_sums(n_col, info, frame, values, left_op, right_op)


def third_kernel(
    last, n_col, info, frame, resid, image, zframe, local, from_up, from_down,
    tcell, main_f, side_f, sums0, sums1,
    wframe, keep_out, send_out, wside, left_op, right_op,
):
    join(info[1], last, local, from_up, from_down, (wframe, wside))
    v = stiffness(wframe, wside, tcell.at[0], tcell.at[1], LO, HI)
    r = resid[:, 1:1 + CR, :]
    q = image[:, 1:1 + CR, :]
    z = zframe[:, LO:HI, :]
    w = wframe[:, LO:HI, :]
    lane = iota((1, CC), 1)
    dots = jnp.zeros((1, CC), F32)
    pairs = ((r, z), (z, q), (r, w), (q, w), (z, v), (w, v))
    for k, (a, b) in enumerate(pairs):
        ab = a * b
        for s in range(2):
            part = ab[3 * s] + ab[3 * s + 1] + ab[3 * s + 2]
            value = jnp.sum(jnp.sum(part, axis=0, keepdims=True), axis=1, keepdims=True)
            dots = jnp.where(lane == 2 * k + s, value, dots)
    values = solved_values(
        tcell, differences(main_f, side_f, LO, HI), differences(wframe, wside, LO, HI)
    )
    sums = design_sums(n_col, info, frame, values, left_op, right_op)
    for half, out in ((0, keep_out), (1, send_out)):
        count = out.shape[0]
        rows = slice(128 * half, 128 * half + count)
        out[:, 0:CC] = jnp.broadcast_to(dots, (count, CC))
        out[:, CC:2 * CC] = sums0[rows, :]
        out[:, 2 * CC:4 * CC] = sums1[rows, :]
        out[:, 4 * CC:] = sums[rows]


def last_kernel(got, zframe, wframe, tangent, second, owned):
    sums = jnp.sum(got[...], axis=0, keepdims=True)
    dots = sums[:, 0:CC]
    lane = iota((1, CC), 1)

    def pick(k):
        return jnp.sum(jnp.where(lane == k, dots, 0.0), axis=1, keepdims=True)

    coeffs = []
    for s in range(2):
        rz, zq, rw, qw, zv, wv = (pick(2 * k + s) for k in range(6))
        alpha = rz / zq
        rz1 = rz - alpha * (zq + rw) + alpha * alpha * qw
        grow = 1.0 + rz1 / rz
        pq = grow * grow * zq - grow * alpha * (zv + qw) + alpha * alpha * wv
        alpha1 = rz1 / pq
        coeffs.append((alpha + alpha1 * grow, -alpha1 * alpha))
    for s, out in ((0, tangent), (1, second)):
        c0, c1 = coeffs[s]
        for f in range(3):
            out[f] = c0 * zframe[3 * s + f, 8:8 + CR, :] + c1 * wframe[3 * s + f, 8:8 + CR, :]
    h = [sums[:, (k + 1) * CC:(k + 2) * CC] for k in range(5)]
    owned[...] = (
        h[0] + coeffs[1][0] * h[1] + coeffs[0][0] * h[2] + coeffs[1][1] * h[3] + coeffs[0][1] * h[4]
    )


def ring(axis, count, to_next, to_previous):
    forward = [(i, (i + 1) % count) for i in range(count)]
    backward = [(b, a) for a, b in forward]
    return lax.ppermute(to_next, axis, forward), lax.ppermute(to_previous, axis, backward)


def per_device(state, adjoint, thickness, direction, design_map, levels, blocks):
    n_row, n_col = lax.axis_size(ROW), lax.axis_size("pcol")
    n_dev = n_row * n_col
    last = n_row - 1
    info = jnp.stack([levels[0, 0], lax.axis_index(ROW).astype(jnp.int32)])
    rows = functools.partial(ring, ROW, n_row)
    cols = functools.partial(ring, "pcol", n_col)

    own, frame, first, end = call(
        start_kernel, [(n_dev, 1, 2 * DV), (7, FR, CC), (EDGE + 8, CC), (EDGE + 8, CC)], [HBM] * 7,
        [
            pltpu.VMEM((1, 1), jnp.int32), pltpu.VMEM((6, CR, CC), F32),
            pltpu.VMEM((CR, CC), jnp.int32), pltpu.VMEM((2, 1, DV), F32),
            pltpu.VMEM((n_dev, 1, 2 * DV), F32), pltpu.VMEM((BLK, BLK, CC), F32),
            pltpu.SemaphoreType.DMA((7,)),
            pltpu.SemaphoreType.DMA((BLK // PIECE,)),
        ],
        work=10**9, limit=LARGE, outs=[HBM] + [VMEM] * 3,
    )(levels, thickness.reshape(1, DV), direction.reshape(1, DV), state, adjoint, design_map, blocks)
    table = lax.all_to_all(own, ROW + ("pcol",), 0, 0, tiled=True).reshape(n_dev, 2 * DV)
    if n_dev < 256:
        table = jnp.concatenate([table, jnp.zeros((256 - n_dev, 2 * DV), F32)], axis=0)
    from_left, from_right = cols(end, first)
    side, up, down, around, edge = call(
        rows_kernel, [(7, FR, CC), (2, 16, CC), (2, 16, CC), (8, CC), (3, BLK, CC)], [VMEM] * 3,
        work=10**11,
    )(frame, from_left, from_right)

    solve_scratch = [pltpu.VMEM((2, BLK, CC), F32)] * 4
    pairs = len(PAIRS) + 1
    main_f, side_f, cells = call(
        functools.partial(place_kernel, last),
        [
            (6, FR, CC), (6, FR, CC), jax.ShapeDtypeStruct((pairs, 2 * CC), jnp.int32),
        ],
        [SMEM] + [VMEM] * 4, [pltpu.VMEM((2, FR, CC), F32)], work=3 * 10**9,
    )(info, frame, side, *rows(down, up))
    resid, local, up, down, tcell, dcell = call(
        functools.partial(first_kernel, last),
        [
            (6, EXT, CC), (2, 6, EXT, CC), (2, 24, CC), (2, 24, CC), (2, FR, CC), (2, FR, CC),
        ],
        [SMEM] + [VMEM] * 7, solve_scratch,
    )(info, table, main_f, side_f, cells, blocks, edge, around)

    def operands(count):
        return [pltpu.VMEM((256, CR * CC), BF16), pltpu.VMEM((2 * count * DV, CR * CC), BF16)]

    (sums0,) = call(
        functools.partial(known_sums_kernel, n_col), [(256, DV)], [SMEM] + [VMEM] * 5, operands(1),
        work=3 * 10**8,
    )(info, frame, tcell, dcell, main_f, side_f)
    zframe, zside, image, local, up, down = call(
        functools.partial(second_kernel, last),
        [(6, FR, CC), (6, FR, CC), (6, EXT, CC), (2, 6, EXT, CC), (2, 24, CC), (2, 24, CC)],
        [SMEM] + [VMEM] * 7,
        solve_scratch,
    )(info, local, *rows(down, up), tcell, blocks, edge, around)
    (sums1,) = call(
        functools.partial(solved_sums_kernel, n_col), [(256, 2 * DV)], [SMEM] + [VMEM] * 6,
        operands(2), work=5 * 10**8,
    )(info, frame, tcell, main_f, side_f, zframe, zside)
    wframe, keep, send = call(
        functools.partial(third_kernel, last, n_col),
        [(6, FR, CC)] + [(n_dev // 2, 6 * CC)] * 2, [SMEM] + [VMEM] * 12,
        [pltpu.VMEM((6, FR, CC), F32)] + operands(2),
    )(info, frame, resid, image, zframe, local, *rows(down, up), tcell, main_f, side_f, sums0, sums1)
    sums = keep + lax.ppermute(send, "core", [(0, 1), (1, 0)])
    got = lax.all_to_all(sums, ("y", "pcol"), 0, 0, tiled=True)
    tangent, second, owned = call(
        last_kernel, [(3, CR, CC), (3, CR, CC), (1, CC)], [VMEM] * 3
    )(got, zframe, wframe)
    return tangent, second, owned.reshape(DV)


def solution(mesh):
    n_row, n_col = mesh.devices.shape
    fine = jax.sharding.Mesh(mesh.devices.reshape(n_row // 2, 2, n_col), ("y", "core", "pcol"))
    field = P(None, ROW, "pcol")
    design = P(("y", "core", "pcol"))
    return jax.shard_map(
        per_device,
        mesh=fine,
        in_specs=(field, field, design, design, P(ROW, "pcol"), P(ROW, "pcol"), P(ROW, None, "pcol")),
        out_specs=(field, field, design),
        check_vma=False,
    )
```

```python
import functools

import jax
import jax.numpy as jnp
from jax import lax
from jax.experimental import pallas as pl
from jax.experimental.pallas import tpu as pltpu
from jax.sharding import PartitionSpec as P

CR = 22
CC = 128
DV = 128
BLK = 72
EXT = CR + 2
FR = 32
ROW = ("y", "core")
WIDE = 3
F32 = jnp.float32
BF16 = jnp.bfloat16

VMEM = pl.BlockSpec(memory_space=pltpu.VMEM)
SMEM = pl.BlockSpec(memory_space=pltpu.SMEM)
HBM = pl.BlockSpec(memory_space=pltpu.HBM)
SMALL = 20 * 1024 * 1024
LARGE = 62 * 1024 * 1024


def call(kernel, out_shapes, in_specs, scratch=(), work=None, limit=SMALL, outs=None):
    cost = None
    if work is not None:
        cost = pl.CostEstimate(flops=work, bytes_accessed=1 << 20, transcendentals=0)
    return pl.pallas_call(
        kernel,
        out_shape=[
            s if isinstance(s, jax.ShapeDtypeStruct) else jax.ShapeDtypeStruct(s, F32)
            for s in out_shapes
        ],
        in_specs=list(in_specs),
        out_specs=[VMEM] * len(out_shapes) if outs is None else outs,
        cost_estimate=cost,
        scratch_shapes=list(scratch),
        compiler_params=pltpu.CompilerParams(vmem_limit_bytes=limit),
    )


def iota(shape, dim):
    return lax.broadcasted_iota(jnp.int32, shape, dim)


def pack_edges(tiles, width):
    lane = iota((8, CC), 1)
    first = jnp.zeros((8, CC), F32)
    last = jnp.zeros((8, CC), F32)
    for k, tile in enumerate(tiles):
        at = k * width
        here = (lane >= at) & (lane < at + width)
        first = jnp.where(here, pltpu.roll(tile, at, 1) if at else tile, first)
        last = jnp.where(here, pltpu.roll(tile, at + width, 1), last)
    return first, last


def unpack_edges(from_left, from_right, count, width):
    lane = iota((8, CC), 1)
    tiles = []
    for k in range(count):
        at = k * width
        right = pltpu.roll(from_right, CC - at, 1) if at else from_right
        shift = (CC - width - at) % CC
        left = pltpu.roll(from_left, shift, 1) if shift else from_left
        tiles.append(jnp.where(lane < width, right, jnp.where(lane >= CC - width, left, 0.0)))
    return tiles


def lanes_of(x):
    return iota(x.shape, x.ndim - 1)


def left_of(main, side):
    dim = main.ndim - 1
    return jnp.where(lanes_of(main) == 0, pltpu.roll(side, 1, dim), pltpu.roll(main, 1, dim))


def right_of(main, side):
    dim = main.ndim - 1
    return jnp.where(
        lanes_of(main) == CC - 1, pltpu.roll(side, CC - 1, dim), pltpu.roll(main, CC - 1, dim)
    )


def grid_mask(prow, last, start, rows):
    row = iota((rows, CC), 0) + (start - 8)
    outside = ((row < 0) & (prow == 0)) | ((row >= CR) & (prow == last))
    return jnp.where(outside, 0.0, 1.0).astype(F32)


PIECE = 24
EDGE = 3 * BLK


def start_kernel(
    levels, thickness, direction, state, adjoint, dmap, blocks,
    own_out, frame_out, first_out, last_out,
    level, known, cells, own, many, mats, sems, block_sems,
):
    copies = [
        pltpu.make_async_copy(thickness, own.at[0], sems.at[0]),
        pltpu.make_async_copy(direction, own.at[1], sems.at[1]),
        pltpu.make_async_copy(state, known.at[0:3], sems.at[2]),
        pltpu.make_async_copy(adjoint, known.at[3:6], sems.at[3]),
        pltpu.make_async_copy(dmap, cells, sems.at[4]),
        pltpu.make_async_copy(levels, level, sems.at[5]),
    ]
    pieces = []
    for k in range(BLK // PIECE):
        cut = pl.ds(k * PIECE, PIECE)
        pieces.append(pltpu.make_async_copy(blocks.at[cut], mats.at[cut], block_sems.at[k]))
    for copy in copies + pieces:
        copy.start()
    frame_out[...] = jnp.zeros_like(frame_out)
    upper = iota((8, CC), 1) >= 64
    for copy in copies:
        copy.wait()
    for k in range(2):
        many[:, :, k * DV:(k + 1) * DV] = jnp.broadcast_to(own[k][None], (many.shape[0], 1, DV))
    written = pltpu.make_async_copy(many, own_out, sems.at[6])
    written.start()
    frame_out[0:6, 8:8 + CR, :] = known[...]
    frame_out[6, 8:8 + CR, :] = cells[...].astype(F32)
    tiles = [frame_out[f, 8 + 8 * g:16 + 8 * g, :] for f in range(7) for g in range(3)]
    first, last = pack_edges(tiles, WIDE)
    depth = level[0].astype(F32)
    first_out[EDGE:, :] = jnp.where(upper, depth, first)
    last_out[EDGE:, :] = jnp.where(upper, depth, last)
    lane = iota((BLK, CC), 1)
    for c in range(3):
        packed = jnp.zeros((BLK, CC), F32)
        for i in range(min(32, BLK - 32 * c)):
            at = 32 * c + i
            if at % PIECE == 0:
                pieces[at // PIECE].wait()
            mat = mats[at]
            here = ((lane - 4 * i + 2) & (CC - 1)) < 4
            packed = jnp.where(here, pltpu.roll(mat, 4 * i, 1) if i else mat, packed)
        first_out[c * BLK:(c + 1) * BLK, :] = packed
        last_out[c * BLK:(c + 1) * BLK, :] = packed
    written.wait()


def rows_kernel(
    frame, from_left, from_right, side_out, up_out, down_out, levels_out, edge_out,
):
    left_end, right_end = from_left[EDGE:, :], from_right[EDGE:, :]
    tiles = unpack_edges(left_end, right_end, 21, WIDE)
    side_out[...] = jnp.zeros_like(side_out)
    for f in range(7):
        for g in range(3):
            side_out[f, 8 + 8 * g:16 + 8 * g, :] = tiles[3 * f + g]
    up_out[...] = jnp.zeros_like(up_out)
    down_out[...] = jnp.zeros_like(down_out)
    for tile, ref in ((0, frame), (1, side_out)):
        for f in range(7):
            up_out[tile, 2 * f:2 * f + 2, :] = ref[f, 8:10, :]
            down_out[tile, 2 * f:2 * f + 2, :] = ref[f, 6 + CR:8 + CR, :]
    upper = iota((8, CC), 1) >= 64
    levels_out[...] = jnp.where(upper, left_end, pltpu.roll(right_end, 64, 1))
    lane = iota((BLK, CC), 1)
    for c in range(3):
        cut = slice(c * BLK, (c + 1) * BLK)
        edge_out[c] = jnp.where(lane % 4 < 2, from_right[cut, :], pltpu.roll(from_left[cut, :], 4, 1))


def apply_blocks(mats, vec):
    one = jnp.zeros((BLK, CC), F32)
    two = jnp.zeros((BLK, CC), F32)
    for at in range(BLK):
        mat = mats[at]
        one = one + mat * vec[0, at:at + 1, :]
        two = two + mat * vec[1, at:at + 1, :]
    return one, two


def over_columns(x):
    same = (iota((2 * CC, CC), 0) - iota((2 * CC, CC), 1)) % 4 == 0
    top = x.astype(BF16)
    rest = (x - top.astype(F32)).astype(BF16)
    return jnp.dot(
        jnp.concatenate([top, rest], axis=1), jnp.where(same, 1.0, 0.0).astype(BF16),
        preferred_element_type=F32,
    )


def apply_edge(edge, vec):
    row = iota((BLK, CC), 0)
    place = iota((BLK, CC), 1) // 4
    out = jnp.zeros((BLK, CC), F32)
    for c in range(3):
        low, high = 32 * c, min(32 * c + 32, BLK)
        mine = row[low:high] == place[low:high] + 32 * c
        flat = jnp.sum(jnp.where(mine, vec[low:high], 0.0), axis=0, keepdims=True)
        out = out + edge[c] * flat
    return out


def local_solve(mats, edge, vec, total, side_vec, side_total, level, levels):
    lane = iota((BLK, CC), 1)
    ours = (lane < 2) | (lane >= CC - 2)
    kept = [jnp.where(ours, side_vec[n], 0.0) for n in range(2)]
    spread = over_columns(jnp.concatenate(kept, axis=0))
    side_vec[0] = spread[:BLK]
    side_vec[1] = spread[BLK:]
    total[...] = jnp.zeros_like(total)
    side_total[...] = jnp.zeros_like(side_total)
    top = jnp.maximum(level, jnp.max(levels[...]).astype(jnp.int32))

    def term(order, carry):
        scale = jnp.where(order == 0, 1.0, 0.5).astype(F32)
        keep = jnp.where(order < level, 1.0, 0.0).astype(F32)
        side_keep = levels[0:1, :] > order.astype(F32)
        parts = [apply_edge(edge, side_vec[n]) for n in range(2)]
        outs = scale * over_columns(jnp.concatenate(parts, axis=0))
        for n in range(2):
            out = outs[n * BLK:(n + 1) * BLK]
            side_vec[n] = out
            side_total[n] += jnp.where(side_keep, out, 0.0)
        for n, out in enumerate(apply_blocks(mats, vec)):
            out = scale * out
            vec[n] = out
            total[n] += keep * out
        return carry

    lax.fori_loop(0, top, term, 0)


def put_results(total, side_total, local_out, up_out, down_out):
    up_out[...] = jnp.zeros_like(up_out)
    down_out[...] = jnp.zeros_like(down_out)
    for tile, ref in ((0, total), (1, side_total)):
        local_out[tile] = ref[...].reshape(6, EXT, CC)
        for f in range(6):
            up_out[tile, 3 * f:3 * f + 3, :] = local_out[tile, f, 0:3, :]
            down_out[tile, 3 * f:3 * f + 3, :] = local_out[tile, f, EXT - 3:EXT, :]


def join(prow, last, local, from_up, from_down, frames):
    inside = grid_mask(prow, last, 0, FR)
    for tile, frame in enumerate(frames):
        frame[...] = jnp.zeros_like(frame)
        frame[:, 7:7 + EXT, :] = local[tile]
        for f in range(6):
            frame[f, 6:9, :] += jnp.where(prow == 0, 0.0, from_up[tile, 3 * f:3 * f + 3, :])
            frame[f, 7 + CR:10 + CR, :] += jnp.where(prow == last, 0.0, from_down[tile, 3 * f:3 * f + 3, :])
        frame[...] = frame[...] * inside[None]


PAIRS = range(6, FR, 2)


def place_cells(index, cells):
    lane1 = iota((1, CC), 1)
    vecs = [jnp.concatenate([index[0][r:r + 1], index[0][r + 1:r + 2]], axis=1) for r in PAIRS]
    packs = []
    for half in range(2):
        vec = jnp.zeros((1, CC), jnp.int32)
        for i in range(16):
            r = 16 * half + i
            vec = jnp.where(lane1 // 8 == i, pltpu.roll(index[1][r:r + 1], (8 * i + 4) % CC, 1), vec)
        packs.append(vec)
    vecs.append(jnp.concatenate(packs, axis=1))
    for k, vec in enumerate(vecs):
        cells[k:k + 1, :] = vec


def look_up(table, cells, tcell, dcell):
    flipped = table[...].T
    part0 = flipped.astype(BF16)
    part1 = (flipped - part0.astype(F32)).astype(BF16)
    lhs = jnp.concatenate([part0, part1], axis=0)
    lane1 = iota((1, CC), 1)

    def both(k):
        vec = cells[k:k + 1, :]
        hot = jnp.where(iota((256, 2 * CC), 0) == vec // DV, 1.0, 0.0).astype(BF16)
        got = jnp.dot(lhs, hot, preferred_element_type=F32)
        mine = iota((DV, 2 * CC), 0) == vec % DV
        tv = jnp.sum(jnp.where(mine, got[0:DV] + got[2 * DV:3 * DV], 0.0), axis=0, keepdims=True)
        dv = jnp.sum(jnp.where(mine, got[DV:2 * DV] + got[3 * DV:4 * DV], 0.0), axis=0, keepdims=True)
        return tv, dv

    for k, r in enumerate(PAIRS):
        tv, dv = both(k)
        for h in range(2):
            tcell[0, r + h:r + h + 1, :] = tv[:, h * CC:(h + 1) * CC]
            dcell[0, r + h:r + h + 1, :] = dv[:, h * CC:(h + 1) * CC]
    tv, dv = both(len(PAIRS))
    for half in range(2):
        for i in range(16):
            r = 16 * half + i
            shift = (CC - 8 * i - 4) % CC
            keep = (lane1 < 4) | (lane1 >= CC - 4)
            cut = slice(half * CC, (half + 1) * CC)
            tcell[1, r:r + 1, :] = jnp.where(keep, pltpu.roll(tv[:, cut], shift, 1), 0.0)
            dcell[1, r:r + 1, :] = jnp.where(keep, pltpu.roll(dv[:, cut], shift, 1), 0.0)


def weights_of(main, side, lo, hi):
    here = main[lo:hi]
    return [
        0.5 * (here + main[lo - 1:hi - 1]),
        0.5 * (here + main[lo + 1:hi + 1]),
        0.5 * (here + left_of(here, side[lo:hi])),
        0.5 * (here + right_of(here, side[lo:hi])),
    ]


def differences(main, side, lo, hi):
    here = main[:, lo:hi, :]
    beside = side[:, lo:hi, :]
    return [
        here - main[:, lo - 1:hi - 1, :],
        here - main[:, lo + 1:hi + 1, :],
        here - left_of(here, beside),
        here - right_of(here, beside),
    ]


def place_kernel(last, info, frame, side, from_up, from_down, main_f, side_f, cells, index_scr):
    inside = grid_mask(info[1], last, 0, FR)
    for tile, ref, source in ((0, main_f, frame), (1, side_f, side)):
        for f in range(7):
            out = ref.at[f] if f < 6 else index_scr.at[tile]
            out[...] = source[f]
            out[6:8, :] = from_up[tile, 2 * f:2 * f + 2, :] * inside[6:8]
            out[8 + CR:10 + CR, :] = from_down[tile, 2 * f:2 * f + 2, :] * inside[8 + CR:10 + CR]
    place_cells([index_scr[tile].astype(jnp.int32) for tile in range(2)], cells)


def first_kernel(
    last, info, table, main_f, side_f, cells, mats, edge, levels,
    resid_out, local_out, up_out, down_out, tcell, dcell,
    vec, total, side_vec, side_total,
):
    level, prow = info[0], info[1]
    inside = grid_mask(prow, last, 0, FR)
    tcell[...] = jnp.zeros_like(tcell)
    dcell[...] = jnp.zeros_like(dcell)
    look_up(table, cells, tcell, dcell)
    for tile in range(2):
        tcell[tile] = tcell[tile] * inside
    slope = [3.0 * tcell[tile] * tcell[tile] * dcell[tile] for tile in range(2)]
    lo, hi = 7, 7 + EXT
    frames = (main_f, side_f)
    for tile, out in ((0, vec), (1, side_vec)):
        here, beside = frames[tile], frames[1 - tile]
        rhs = jnp.zeros((6, EXT, CC), F32)
        for weight, diff in zip(
            weights_of(slope[tile], slope[1 - tile], lo, hi), differences(here, beside, lo, hi)
        ):
            rhs = rhs - weight[None] * diff
        rhs = rhs * inside[lo:hi][None]
        if tile == 0:
            resid_out[...] = rhs
        out[...] = rhs.reshape(2, BLK, CC)
    local_solve(mats, edge, vec, total, side_vec, side_total, level, levels)
    put_results(total, side_total, local_out, up_out, down_out)


def stiffness(main_f, side_f, main_t, side_t, lo, hi):
    stiff = [t * t * t for t in (main_t[...], side_t[...])]
    out = main_f[:, lo:hi, :]
    parts = differences(main_f, side_f, lo, hi)
    for weight, diff in zip(weights_of(stiff[0], stiff[1], lo, hi), parts):
        out = out + weight[None] * diff
    return out


def second_kernel(
    last, info, local, from_up, from_down, tcell, mats, edge, levels,
    main_f, side_f, image_out, local_out, up_out, down_out,
    vec, total, side_vec, side_total,
):
    level, prow = info[0], info[1]
    frames = (main_f, side_f)
    join(prow, last, local, from_up, from_down, frames)
    lo, hi = 7, 7 + EXT
    inside = grid_mask(prow, last, lo, EXT)
    for tile, out in ((0, vec), (1, side_vec)):
        image = stiffness(
            frames[tile], frames[1 - tile], tcell.at[tile], tcell.at[1 - tile], lo, hi
        ) * inside[None]
        if tile == 0:
            image_out[...] = image
        out[...] = image.reshape(2, BLK, CC)
    local_solve(mats, edge, vec, total, side_vec, side_total, level, levels)
    put_results(total, side_total, local_out, up_out, down_out)


def dot3(a, b, i, j):
    out = jnp.zeros((CR, CC), F32)
    for an, bn in zip(a, b):
        for c in range(3):
            out = out + an[i + c] * bn[j + c]
    return out


def design_sums(n_col, info, frame, values, left_op, right_op):
    cells = frame[6, 8:8 + CR, :].astype(jnp.int32)
    owner = cells // DV
    low = cells % DV
    other = jnp.where((owner // n_col) % 2 == info[1] % 2, 0, 128)
    high = other + (owner // (2 * n_col)) * n_col + owner % n_col
    count = len(values)
    tops = [value.astype(BF16) for value in values]
    rests = [(value - top.astype(F32)).astype(BF16) for value, top in zip(values, tops)]
    for row in range(CR):
        cut = slice(CC * row, CC * row + CC)
        left_op[:, cut] = jnp.where(iota((256, CC), 0) == high[row:row + 1], 1.0, 0.0).astype(BF16)
        hot = jnp.where(iota((DV, CC), 0) == low[row:row + 1], 1.0, 0.0).astype(BF16)
        for k, part in enumerate(tops + rests):
            right_op[k * DV:(k + 1) * DV, cut] = hot * part[row:row + 1]
    sums = lax.dot_general(
        left_op[...], right_op[...], (((1,), (1,)), ((), ())), preferred_element_type=F32
    )
    return sums[:, :count * DV] + sums[:, count * DV:]


LO, HI = 8, 8 + CR


def known_sums_kernel(n_col, info, frame, tcell, dcell, main_f, side_f, out, left_op, right_op):
    known_d = differences(main_f, side_f, LO, HI)
    value = (-3.0 * tcell[0, LO:HI, :] * dcell[0, LO:HI, :]) * dot3(known_d, known_d, 3, 0)
    out[...] = design_sums(n_col, info, frame, [value], left_op, right_op)


def solved_values(tcell, known_d, solved_d):
    t = tcell[0, LO:HI, :]
    slope = -1.5 * t * t
    return [slope * dot3(solved_d, known_d, 3, 0), slope * dot3(known_d, solved_d, 3, 0)]


def solved_sums_kernel(
    n_col, info, frame, tcell, main_f, side_f, zframe, zside, out, left_op, right_op
):
    values = solved_values(
        tcell, differences(main_f, side_f, LO, HI), differences(zframe, zside, LO, HI)
    )
    out[...] = design_sums(n_col, info, frame, values, left_op, right_op)


def third_kernel(
    last, n_col, info, frame, resid, image, zframe, local, from_up, from_down,
    tcell, main_f, side_f, sums0, sums1,
    wframe, keep_out, send_out, wside, left_op, right_op,
):
    join(info[1], last, local, from_up, from_down, (wframe, wside))
    v = stiffness(wframe, wside, tcell.at[0], tcell.at[1], LO, HI)
    r = resid[:, 1:1 + CR, :]
    q = image[:, 1:1 + CR, :]
    z = zframe[:, LO:HI, :]
    w = wframe[:, LO:HI, :]
    lane = iota((1, CC), 1)
    dots = jnp.zeros((1, CC), F32)
    pairs = ((r, z), (z, q), (r, w), (q, w), (z, v), (w, v))
    for k, (a, b) in enumerate(pairs):
        ab = a * b
        for s in range(2):
            part = ab[3 * s] + ab[3 * s + 1] + ab[3 * s + 2]
            value = jnp.sum(jnp.sum(part, axis=0, keepdims=True), axis=1, keepdims=True)
            dots = jnp.where(lane == 2 * k + s, value, dots)
    values = solved_values(
        tcell, differences(main_f, side_f, LO, HI), differences(wframe, wside, LO, HI)
    )
    sums = design_sums(n_col, info, frame, values, left_op, right_op)
    for half, out in ((0, keep_out), (1, send_out)):
        count = out.shape[0]
        rows = slice(128 * half, 128 * half + count)
        out[:, 0:CC] = jnp.broadcast_to(dots, (count, CC))
        out[:, CC:2 * CC] = sums0[rows, :]
        out[:, 2 * CC:4 * CC] = sums1[rows, :]
        out[:, 4 * CC:] = sums[rows]


def last_kernel(got, zframe, wframe, tangent, second, owned):
    sums = jnp.sum(got[...], axis=0, keepdims=True)
    dots = sums[:, 0:CC]
    lane = iota((1, CC), 1)

    def pick(k):
        return jnp.sum(jnp.where(lane == k, dots, 0.0), axis=1, keepdims=True)

    coeffs = []
    for s in range(2):
        rz, zq, rw, qw, zv, wv = (pick(2 * k + s) for k in range(6))
        alpha = rz / zq
        rz1 = rz - alpha * (zq + rw) + alpha * alpha * qw
        grow = 1.0 + rz1 / rz
        pq = grow * grow * zq - grow * alpha * (zv + qw) + alpha * alpha * wv
        alpha1 = rz1 / pq
        coeffs.append((alpha + alpha1 * grow, -alpha1 * alpha))
    for s, out in ((0, tangent), (1, second)):
        c0, c1 = coeffs[s]
        for f in range(3):
            out[f] = c0 * zframe[3 * s + f, 8:8 + CR, :] + c1 * wframe[3 * s + f, 8:8 + CR, :]
    h = [sums[:, (k + 1) * CC:(k + 2) * CC] for k in range(5)]
    owned[...] = (
        h[0] + coeffs[1][0] * h[1] + coeffs[0][0] * h[2] + coeffs[1][1] * h[3] + coeffs[0][1] * h[4]
    )


def ring(axis, count, to_next, to_previous):
    forward = [(i, (i + 1) % count) for i in range(count)]
    backward = [(b, a) for a, b in forward]
    return lax.ppermute(to_next, axis, forward), lax.ppermute(to_previous, axis, backward)


def per_device(state, adjoint, thickness, direction, design_map, levels, blocks):
    n_row, n_col = lax.axis_size(ROW), lax.axis_size("pcol")
    n_dev = n_row * n_col
    last = n_row - 1
    info = jnp.stack([levels[0, 0], lax.axis_index(ROW).astype(jnp.int32)])
    rows = functools.partial(ring, ROW, n_row)
    cols = functools.partial(ring, "pcol", n_col)

    own, frame, first, end = call(
        start_kernel, [(n_dev, 1, 2 * DV), (7, FR, CC), (EDGE + 8, CC), (EDGE + 8, CC)], [HBM] * 7,
        [
            pltpu.SMEM((1,), jnp.int32), pltpu.VMEM((6, CR, CC), F32),
            pltpu.VMEM((CR, CC), jnp.int32), pltpu.VMEM((2, 1, DV), F32),
            pltpu.VMEM((n_dev, 1, 2 * DV), F32), pltpu.VMEM((BLK, BLK, CC), F32),
            pltpu.SemaphoreType.DMA((7,)),
            pltpu.SemaphoreType.DMA((BLK // PIECE,)),
        ],
        work=10**9, limit=LARGE, outs=[HBM] + [VMEM] * 3,
    )(levels.reshape(1), thickness.reshape(1, DV), direction.reshape(1, DV), state, adjoint, design_map, blocks)
    table = lax.all_to_all(own, ROW + ("pcol",), 0, 0, tiled=True).reshape(n_dev, 2 * DV)
    if n_dev < 256:
        table = jnp.concatenate([table, jnp.zeros((256 - n_dev, 2 * DV), F32)], axis=0)
    from_left, from_right = cols(end, first)
    side, up, down, around, edge = call(
        rows_kernel, [(7, FR, CC), (2, 16, CC), (2, 16, CC), (8, CC), (3, BLK, CC)], [VMEM] * 3,
        work=10**11,
    )(frame, from_left, from_right)

    solve_scratch = [pltpu.VMEM((2, BLK, CC), F32)] * 4
    pairs = len(PAIRS) + 1
    main_f, side_f, cells = call(
        functools.partial(place_kernel, last),
        [
            (6, FR, CC), (6, FR, CC), jax.ShapeDtypeStruct((pairs, 2 * CC), jnp.int32),
        ],
        [SMEM] + [VMEM] * 4, [pltpu.VMEM((2, FR, CC), F32)], work=3 * 10**9,
    )(info, frame, side, *rows(down, up))
    resid, local, up, down, tcell, dcell = call(
        functools.partial(first_kernel, last),
        [
            (6, EXT, CC), (2, 6, EXT, CC), (2, 24, CC), (2, 24, CC), (2, FR, CC), (2, FR, CC),
        ],
        [SMEM] + [VMEM] * 7, solve_scratch,
    )(info, table, main_f, side_f, cells, blocks, edge, around)

    def operands(count):
        return [pltpu.VMEM((256, CR * CC), BF16), pltpu.VMEM((2 * count * DV, CR * CC), BF16)]

    (sums0,) = call(
        functools.partial(known_sums_kernel, n_col), [(256, DV)], [SMEM] + [VMEM] * 5, operands(1),
        work=3 * 10**8,
    )(info, frame, tcell, dcell, main_f, side_f)
    zframe, zside, image, local, up, down = call(
        functools.partial(second_kernel, last),
        [(6, FR, CC), (6, FR, CC), (6, EXT, CC), (2, 6, EXT, CC), (2, 24, CC), (2, 24, CC)],
        [SMEM] + [VMEM] * 7,
        solve_scratch,
    )(info, local, *rows(down, up), tcell, blocks, edge, around)
    (sums1,) = call(
        functools.partial(solved_sums_kernel, n_col), [(256, 2 * DV)], [SMEM] + [VMEM] * 6,
        operands(2), work=5 * 10**8,
    )(info, frame, tcell, main_f, side_f, zframe, zside)
    wframe, keep, send = call(
        functools.partial(third_kernel, last, n_col),
        [(6, FR, CC)] + [(n_dev // 2, 6 * CC)] * 2, [SMEM] + [VMEM] * 12,
        [pltpu.VMEM((6, FR, CC), F32)] + operands(2),
    )(info, frame, resid, image, zframe, local, *rows(down, up), tcell, main_f, side_f, sums0, sums1)
    sums = keep + lax.ppermute(send, "core", [(0, 1), (1, 0)])
    got = lax.all_to_all(sums, ("y", "pcol"), 0, 0, tiled=True)
    tangent, second, owned = call(
        last_kernel, [(3, CR, CC), (3, CR, CC), (1, CC)], [VMEM] * 3
    )(got, zframe, wframe)
    return tangent, second, owned.reshape(DV)


def solution(mesh):
    n_row, n_col = mesh.devices.shape
    fine = jax.sharding.Mesh(mesh.devices.reshape(n_row // 2, 2, n_col), ("y", "core", "pcol"))
    field = P(None, ROW, "pcol")
    design = P(("y", "core", "pcol"))
    return jax.shard_map(
        per_device,
        mesh=fine,
        in_specs=(field, field, design, design, P(ROW, "pcol"), P(ROW, "pcol"), P(ROW, None, "pcol")),
        out_specs=(field, field, design),
        check_vma=False,
    )
```

```python
import functools

import jax
import jax.numpy as jnp
from jax import lax
from jax.experimental import pallas as pl
from jax.experimental.pallas import tpu as pltpu
from jax.sharding import PartitionSpec as P

CR = 22
CC = 128
DV = 128
BLK = 72
EXT = CR + 2
FR = 32
ROW = ("y", "core")
WIDE = 3
F32 = jnp.float32
BF16 = jnp.bfloat16

VMEM = pl.BlockSpec(memory_space=pltpu.VMEM)
SMEM = pl.BlockSpec(memory_space=pltpu.SMEM)
HBM = pl.BlockSpec(memory_space=pltpu.HBM)
SMALL = 20 * 1024 * 1024
LARGE = 62 * 1024 * 1024


def call(kernel, out_shapes, in_specs, scratch=(), work=None, limit=SMALL, outs=None):
    cost = None
    if work is not None:
        cost = pl.CostEstimate(flops=work, bytes_accessed=1 << 20, transcendentals=0)
    return pl.pallas_call(
        kernel,
        out_shape=[
            s if isinstance(s, jax.ShapeDtypeStruct) else jax.ShapeDtypeStruct(s, F32)
            for s in out_shapes
        ],
        in_specs=list(in_specs),
        out_specs=[VMEM] * len(out_shapes) if outs is None else outs,
        cost_estimate=cost,
        scratch_shapes=list(scratch),
        compiler_params=pltpu.CompilerParams(vmem_limit_bytes=limit),
    )


def iota(shape, dim):
    return lax.broadcasted_iota(jnp.int32, shape, dim)


def pack_edges(tiles, width):
    lane = iota((8, CC), 1)
    first = jnp.zeros((8, CC), F32)
    last = jnp.zeros((8, CC), F32)
    for k, tile in enumerate(tiles):
        at = k * width
        here = (lane >= at) & (lane < at + width)
        first = jnp.where(here, pltpu.roll(tile, at, 1) if at else tile, first)
        last = jnp.where(here, pltpu.roll(tile, at + width, 1), last)
    return first, last


def unpack_edges(from_left, from_right, count, width):
    lane = iota((8, CC), 1)
    tiles = []
    for k in range(count):
        at = k * width
        right = pltpu.roll(from_right, CC - at, 1) if at else from_right
        shift = (CC - width - at) % CC
        left = pltpu.roll(from_left, shift, 1) if shift else from_left
        tiles.append(jnp.where(lane < width, right, jnp.where(lane >= CC - width, left, 0.0)))
    return tiles


def lanes_of(x):
    return iota(x.shape, x.ndim - 1)


def left_of(main, side):
    dim = main.ndim - 1
    return jnp.where(lanes_of(main) == 0, pltpu.roll(side, 1, dim), pltpu.roll(main, 1, dim))


def right_of(main, side):
    dim = main.ndim - 1
    return jnp.where(
        lanes_of(main) == CC - 1, pltpu.roll(side, CC - 1, dim), pltpu.roll(main, CC - 1, dim)
    )


def grid_mask(prow, last, start, rows):
    row = iota((rows, CC), 0) + (start - 8)
    outside = ((row < 0) & (prow == 0)) | ((row >= CR) & (prow == last))
    return jnp.where(outside, 0.0, 1.0).astype(F32)


PIECE = 24
EDGE = 3 * BLK


def start_kernel(
    levels, thickness, direction, state, adjoint, dmap, blocks,
    own_out, frame_out, first_out, last_out,
    level, known, cells, own, many, mats, sems, block_sems,
):
    copies = [
        pltpu.make_async_copy(thickness, own.at[0], sems.at[0]),
        pltpu.make_async_copy(direction, own.at[1], sems.at[1]),
        pltpu.make_async_copy(state, known.at[0:3], sems.at[2]),
        pltpu.make_async_copy(adjoint, known.at[3:6], sems.at[3]),
        pltpu.make_async_copy(dmap, cells, sems.at[4]),
        pltpu.make_async_copy(levels, level, sems.at[5]),
    ]
    pieces = []
    for k in range(BLK // PIECE):
        cut = pl.ds(k * PIECE, PIECE)
        pieces.append(pltpu.make_async_copy(blocks.at[cut], mats.at[cut], block_sems.at[k]))
    for copy in copies + pieces:
        copy.start()
    frame_out[...] = jnp.zeros_like(frame_out)
    upper = iota((8, CC), 1) >= 64
    for copy in copies:
        copy.wait()
    for k in range(2):
        many[:, :, k * DV:(k + 1) * DV] = jnp.broadcast_to(own[k][None], (many.shape[0], 1, DV))
    written = pltpu.make_async_copy(many, own_out, sems.at[6])
    written.start()
    frame_out[0:6, 8:8 + CR, :] = known[...]
    frame_out[6, 8:8 + CR, :] = cells[...].astype(F32)
    tiles = [frame_out[f, 8 + 8 * g:16 + 8 * g, :] for f in range(7) for g in range(3)]
    first, last = pack_edges(tiles, WIDE)
    depth = level[0].astype(F32)
    first_out[EDGE:, :] = jnp.where(upper, depth, first)
    last_out[EDGE:, :] = jnp.where(upper, depth, last)
    lane = iota((BLK, CC), 1)
    for c in range(3):
        packed = jnp.zeros((BLK, CC), F32)
        for i in range(min(32, BLK - 32 * c)):
            at = 32 * c + i
            if at % PIECE == 0:
                pieces[at // PIECE].wait()
            mat = mats[at]
            here = ((lane - 4 * i + 2) & (CC - 1)) < 4
            packed = jnp.where(here, pltpu.roll(mat, 4 * i, 1) if i else mat, packed)
        first_out[c * BLK:(c + 1) * BLK, :] = packed
        last_out[c * BLK:(c + 1) * BLK, :] = packed
    written.wait()


def by_turn(prow, up, down):
    even = prow % 2 == 0
    return jnp.where(even, down, up), jnp.where(even, up, down)


def rows_kernel(
    info, frame, from_left, from_right, side_out, one_out, two_out, levels_out, edge_out,
):
    left_end, right_end = from_left[EDGE:, :], from_right[EDGE:, :]
    tiles = unpack_edges(left_end, right_end, 21, WIDE)
    side_out[...] = jnp.zeros_like(side_out)
    for f in range(7):
        for g in range(3):
            side_out[f, 8 + 8 * g:16 + 8 * g, :] = tiles[3 * f + g]
    one_out[...] = jnp.zeros_like(one_out)
    two_out[...] = jnp.zeros_like(two_out)
    for tile, ref in ((0, frame), (1, side_out)):
        for f in range(7):
            one, two = by_turn(info[1], ref[f, 8:10, :], ref[f, 6 + CR:8 + CR, :])
            one_out[tile, 2 * f:2 * f + 2, :] = one
            two_out[tile, 2 * f:2 * f + 2, :] = two
    upper = iota((8, CC), 1) >= 64
    levels_out[...] = jnp.where(upper, left_end, pltpu.roll(right_end, 64, 1))
    lane = iota((BLK, CC), 1)
    for c in range(3):
        cut = slice(c * BLK, (c + 1) * BLK)
        edge_out[c] = jnp.where(lane % 4 < 2, from_right[cut, :], pltpu.roll(from_left[cut, :], 4, 1))


def apply_blocks(mats, vec):
    one = jnp.zeros((BLK, CC), F32)
    two = jnp.zeros((BLK, CC), F32)
    for at in range(BLK):
        mat = mats[at]
        one = one + mat * vec[0, at:at + 1, :]
        two = two + mat * vec[1, at:at + 1, :]
    return one, two


def over_columns(x):
    same = (iota((2 * CC, CC), 0) - iota((2 * CC, CC), 1)) % 4 == 0
    top = x.astype(BF16)
    rest = (x - top.astype(F32)).astype(BF16)
    return jnp.dot(
        jnp.concatenate([top, rest], axis=1), jnp.where(same, 1.0, 0.0).astype(BF16),
        preferred_element_type=F32,
    )


def apply_edge(edge, vec):
    row = iota((BLK, CC), 0)
    place = iota((BLK, CC), 1) // 4
    out = jnp.zeros((BLK, CC), F32)
    for c in range(3):
        low, high = 32 * c, min(32 * c + 32, BLK)
        mine = row[low:high] == place[low:high] + 32 * c
        flat = jnp.sum(jnp.where(mine, vec[low:high], 0.0), axis=0, keepdims=True)
        out = out + edge[c] * flat
    return out


def local_solve(mats, edge, vec, total, side_vec, side_total, level, levels):
    lane = iota((BLK, CC), 1)
    ours = (lane < 2) | (lane >= CC - 2)
    kept = [jnp.where(ours, side_vec[n], 0.0) for n in range(2)]
    spread = over_columns(jnp.concatenate(kept, axis=0))
    side_vec[0] = spread[:BLK]
    side_vec[1] = spread[BLK:]
    total[...] = jnp.zeros_like(total)
    side_total[...] = jnp.zeros_like(side_total)
    top = jnp.maximum(level, jnp.max(levels[...]).astype(jnp.int32))

    def term(order, carry):
        scale = jnp.where(order == 0, 1.0, 0.5).astype(F32)
        keep = jnp.where(order < level, 1.0, 0.0).astype(F32)
        side_keep = levels[0:1, :] > order.astype(F32)
        parts = [apply_edge(edge, side_vec[n]) for n in range(2)]
        outs = scale * over_columns(jnp.concatenate(parts, axis=0))
        for n in range(2):
            out = outs[n * BLK:(n + 1) * BLK]
            side_vec[n] = out
            side_total[n] += jnp.where(side_keep, out, 0.0)
        for n, out in enumerate(apply_blocks(mats, vec)):
            out = scale * out
            vec[n] = out
            total[n] += keep * out
        return carry

    lax.fori_loop(0, top, term, 0)


def put_results(prow, total, side_total, local_out, one_out, two_out):
    one_out[...] = jnp.zeros_like(one_out)
    two_out[...] = jnp.zeros_like(two_out)
    for tile, ref in ((0, total), (1, side_total)):
        local_out[tile] = ref[...].reshape(6, EXT, CC)
        for f in range(6):
            one, two = by_turn(prow, local_out[tile, f, 0:3, :], local_out[tile, f, EXT - 3:EXT, :])
            one_out[tile, 3 * f:3 * f + 3, :] = one
            two_out[tile, 3 * f:3 * f + 3, :] = two


def join(prow, last, local, got_one, got_two, frames):
    inside = grid_mask(prow, last, 0, FR)
    for tile, frame in enumerate(frames):
        frame[...] = jnp.zeros_like(frame)
        frame[:, 7:7 + EXT, :] = local[tile]
        for f in range(6):
            cut = slice(3 * f, 3 * f + 3)
            above, below = by_turn(prow, got_one[tile, cut, :], got_two[tile, cut, :])
            frame[f, 6:9, :] += jnp.where(prow == 0, 0.0, above)
            frame[f, 7 + CR:10 + CR, :] += jnp.where(prow == last, 0.0, below)
        frame[...] = frame[...] * inside[None]


PAIRS = range(6, FR, 2)


def place_cells(index, cells):
    lane1 = iota((1, CC), 1)
    vecs = [jnp.concatenate([index[0][r:r + 1], index[0][r + 1:r + 2]], axis=1) for r in PAIRS]
    packs = []
    for half in range(2):
        vec = jnp.zeros((1, CC), jnp.int32)
        for i in range(16):
            r = 16 * half + i
            vec = jnp.where(lane1 // 8 == i, pltpu.roll(index[1][r:r + 1], (8 * i + 4) % CC, 1), vec)
        packs.append(vec)
    vecs.append(jnp.concatenate(packs, axis=1))
    for k, vec in enumerate(vecs):
        cells[k:k + 1, :] = vec


def look_up(table, cells, tcell, dcell):
    flipped = table[...].T
    part0 = flipped.astype(BF16)
    part1 = (flipped - part0.astype(F32)).astype(BF16)
    lhs = jnp.concatenate([part0, part1], axis=0)
    lane1 = iota((1, CC), 1)

    def both(k):
        vec = cells[k:k + 1, :]
        hot = jnp.where(iota((256, 2 * CC), 0) == vec // DV, 1.0, 0.0).astype(BF16)
        got = jnp.dot(lhs, hot, preferred_element_type=F32)
        mine = iota((DV, 2 * CC), 0) == vec % DV
        tv = jnp.sum(jnp.where(mine, got[0:DV] + got[2 * DV:3 * DV], 0.0), axis=0, keepdims=True)
        dv = jnp.sum(jnp.where(mine, got[DV:2 * DV] + got[3 * DV:4 * DV], 0.0), axis=0, keepdims=True)
        return tv, dv

    for k, r in enumerate(PAIRS):
        tv, dv = both(k)
        for h in range(2):
            tcell[0, r + h:r + h + 1, :] = tv[:, h * CC:(h + 1) * CC]
            dcell[0, r + h:r + h + 1, :] = dv[:, h * CC:(h + 1) * CC]
    tv, dv = both(len(PAIRS))
    for half in range(2):
        for i in range(16):
            r = 16 * half + i
            shift = (CC - 8 * i - 4) % CC
            keep = (lane1 < 4) | (lane1 >= CC - 4)
            cut = slice(half * CC, (half + 1) * CC)
            tcell[1, r:r + 1, :] = jnp.where(keep, pltpu.roll(tv[:, cut], shift, 1), 0.0)
            dcell[1, r:r + 1, :] = jnp.where(keep, pltpu.roll(dv[:, cut], shift, 1), 0.0)


def weights_of(main, side, lo, hi):
    here = main[lo:hi]
    return [
        0.5 * (here + main[lo - 1:hi - 1]),
        0.5 * (here + main[lo + 1:hi + 1]),
        0.5 * (here + left_of(here, side[lo:hi])),
        0.5 * (here + right_of(here, side[lo:hi])),
    ]


def differences(main, side, lo, hi):
    here = main[:, lo:hi, :]
    beside = side[:, lo:hi, :]
    return [
        here - main[:, lo - 1:hi - 1, :],
        here - main[:, lo + 1:hi + 1, :],
        here - left_of(here, beside),
        here - right_of(here, beside),
    ]


def place_kernel(last, info, frame, side, got_one, got_two, main_f, side_f, cells, index_scr):
    inside = grid_mask(info[1], last, 0, FR)
    for tile, ref, source in ((0, main_f, frame), (1, side_f, side)):
        for f in range(7):
            out = ref.at[f] if f < 6 else index_scr.at[tile]
            out[...] = source[f]
            cut = slice(2 * f, 2 * f + 2)
            above, below = by_turn(info[1], got_one[tile, cut, :], got_two[tile, cut, :])
            out[6:8, :] = above * inside[6:8]
            out[8 + CR:10 + CR, :] = below * inside[8 + CR:10 + CR]
    place_cells([index_scr[tile].astype(jnp.int32) for tile in range(2)], cells)


def first_kernel(
    last, info, table, main_f, side_f, cells, mats, edge, levels,
    resid_out, local_out, one_out, two_out, tcell, dcell,
    vec, total, side_vec, side_total,
):
    level, prow = info[0], info[1]
    inside = grid_mask(prow, last, 0, FR)
    tcell[...] = jnp.zeros_like(tcell)
    dcell[...] = jnp.zeros_like(dcell)
    look_up(table, cells, tcell, dcell)
    for tile in range(2):
        tcell[tile] = tcell[tile] * inside
    slope = [3.0 * tcell[tile] * tcell[tile] * dcell[tile] for tile in range(2)]
    lo, hi = 7, 7 + EXT
    frames = (main_f, side_f)
    for tile, out in ((0, vec), (1, side_vec)):
        here, beside = frames[tile], frames[1 - tile]
        rhs = jnp.zeros((6, EXT, CC), F32)
        for weight, diff in zip(
            weights_of(slope[tile], slope[1 - tile], lo, hi), differences(here, beside, lo, hi)
        ):
            rhs = rhs - weight[None] * diff
        rhs = rhs * inside[lo:hi][None]
        if tile == 0:
            resid_out[...] = rhs
        out[...] = rhs.reshape(2, BLK, CC)
    local_solve(mats, edge, vec, total, side_vec, side_total, level, levels)
    put_results(prow, total, side_total, local_out, one_out, two_out)


def stiffness(main_f, side_f, main_t, side_t, lo, hi):
    stiff = [t * t * t for t in (main_t[...], side_t[...])]
    out = main_f[:, lo:hi, :]
    parts = differences(main_f, side_f, lo, hi)
    for weight, diff in zip(weights_of(stiff[0], stiff[1], lo, hi), parts):
        out = out + weight[None] * diff
    return out


def second_kernel(
    last, info, local, got_one, got_two, tcell, mats, edge, levels,
    main_f, side_f, image_out, local_out, one_out, two_out,
    vec, total, side_vec, side_total,
):
    level, prow = info[0], info[1]
    frames = (main_f, side_f)
    join(prow, last, local, got_one, got_two, frames)
    lo, hi = 7, 7 + EXT
    inside = grid_mask(prow, last, lo, EXT)
    for tile, out in ((0, vec), (1, side_vec)):
        image = stiffness(
            frames[tile], frames[1 - tile], tcell.at[tile], tcell.at[1 - tile], lo, hi
        ) * inside[None]
        if tile == 0:
            image_out[...] = image
        out[...] = image.reshape(2, BLK, CC)
    local_solve(mats, edge, vec, total, side_vec, side_total, level, levels)
    put_results(prow, total, side_total, local_out, one_out, two_out)


def dot3(a, b, i, j):
    out = jnp.zeros((CR, CC), F32)
    for an, bn in zip(a, b):
        for c in range(3):
            out = out + an[i + c] * bn[j + c]
    return out


def design_sums(n_col, info, frame, values, left_op, right_op):
    cells = frame[6, 8:8 + CR, :].astype(jnp.int32)
    owner = cells // DV
    low = cells % DV
    other = jnp.where((owner // n_col) % 2 == info[1] % 2, 0, 128)
    high = other + (owner // (2 * n_col)) * n_col + owner % n_col
    count = len(values)
    tops = [value.astype(BF16) for value in values]
    rests = [(value - top.astype(F32)).astype(BF16) for value, top in zip(values, tops)]
    for row in range(CR):
        cut = slice(CC * row, CC * row + CC)
        left_op[:, cut] = jnp.where(iota((256, CC), 0) == high[row:row + 1], 1.0, 0.0).astype(BF16)
        hot = jnp.where(iota((DV, CC), 0) == low[row:row + 1], 1.0, 0.0).astype(BF16)
        for k, part in enumerate(tops + rests):
            right_op[k * DV:(k + 1) * DV, cut] = hot * part[row:row + 1]
    sums = lax.dot_general(
        left_op[...], right_op[...], (((1,), (1,)), ((), ())), preferred_element_type=F32
    )
    return sums[:, :count * DV] + sums[:, count * DV:]


LO, HI = 8, 8 + CR


def known_sums_kernel(n_col, info, frame, tcell, dcell, main_f, side_f, out, left_op, right_op):
    known_d = differences(main_f, side_f, LO, HI)
    value = (-3.0 * tcell[0, LO:HI, :] * dcell[0, LO:HI, :]) * dot3(known_d, known_d, 3, 0)
    out[...] = design_sums(n_col, info, frame, [value], left_op, right_op)


def solved_values(tcell, known_d, solved_d):
    t = tcell[0, LO:HI, :]
    slope = -1.5 * t * t
    return [slope * dot3(solved_d, known_d, 3, 0), slope * dot3(known_d, solved_d, 3, 0)]


def solved_sums_kernel(
    n_col, info, frame, tcell, main_f, side_f, zframe, zside, out, left_op, right_op
):
    values = solved_values(
        tcell, differences(main_f, side_f, LO, HI), differences(zframe, zside, LO, HI)
    )
    out[...] = design_sums(n_col, info, frame, values, left_op, right_op)


def third_kernel(
    last, n_col, info, frame, resid, image, zframe, local, got_one, got_two,
    tcell, main_f, side_f, sums0, sums1,
    wframe, keep_out, send_out, wside, left_op, right_op,
):
    join(info[1], last, local, got_one, got_two, (wframe, wside))
    v = stiffness(wframe, wside, tcell.at[0], tcell.at[1], LO, HI)
    r = resid[:, 1:1 + CR, :]
    q = image[:, 1:1 + CR, :]
    z = zframe[:, LO:HI, :]
    w = wframe[:, LO:HI, :]
    lane = iota((1, CC), 1)
    dots = jnp.zeros((1, CC), F32)
    pairs = ((r, z), (z, q), (r, w), (q, w), (z, v), (w, v))
    for k, (a, b) in enumerate(pairs):
        ab = a * b
        for s in range(2):
            part = ab[3 * s] + ab[3 * s + 1] + ab[3 * s + 2]
            value = jnp.sum(jnp.sum(part, axis=0, keepdims=True), axis=1, keepdims=True)
            dots = jnp.where(lane == 2 * k + s, value, dots)
    values = solved_values(
        tcell, differences(main_f, side_f, LO, HI), differences(wframe, wside, LO, HI)
    )
    sums = design_sums(n_col, info, frame, values, left_op, right_op)
    for half, out in ((0, keep_out), (1, send_out)):
        count = out.shape[0]
        rows = slice(128 * half, 128 * half + count)
        out[:, 0, 0:CC] = jnp.broadcast_to(dots, (count, CC))
        out[:, 0, CC:2 * CC] = sums0[rows, :]
        out[:, 0, 2 * CC:4 * CC] = sums1[rows, :]
        out[:, 0, 4 * CC:] = sums[rows]


def last_kernel(got, zframe, wframe, tangent, second, owned):
    sums = jnp.sum(got[...], axis=0, keepdims=True)
    dots = sums[:, 0:CC]
    lane = iota((1, CC), 1)

    def pick(k):
        return jnp.sum(jnp.where(lane == k, dots, 0.0), axis=1, keepdims=True)

    coeffs = []
    for s in range(2):
        rz, zq, rw, qw, zv, wv = (pick(2 * k + s) for k in range(6))
        alpha = rz / zq
        rz1 = rz - alpha * (zq + rw) + alpha * alpha * qw
        grow = 1.0 + rz1 / rz
        pq = grow * grow * zq - grow * alpha * (zv + qw) + alpha * alpha * wv
        alpha1 = rz1 / pq
        coeffs.append((alpha + alpha1 * grow, -alpha1 * alpha))
    for s, out in ((0, tangent), (1, second)):
        c0, c1 = coeffs[s]
        for f in range(3):
            out[f] = c0 * zframe[3 * s + f, 8:8 + CR, :] + c1 * wframe[3 * s + f, 8:8 + CR, :]
    h = [sums[:, (k + 1) * CC:(k + 2) * CC] for k in range(5)]
    owned[...] = (
        h[0] + coeffs[1][0] * h[1] + coeffs[0][0] * h[2] + coeffs[1][1] * h[3] + coeffs[0][1] * h[4]
    )


def pairwise(count, one, two):
    first = [(i, i ^ 1) for i in range(count)]
    second = [(i, min(max(i + (1 if i % 2 else -1), 0), count - 1)) for i in range(count)]
    return lax.ppermute(one, ROW, first), lax.ppermute(two, ROW, second)


def ring(axis, count, to_next, to_previous):
    forward = [(i, (i + 1) % count) for i in range(count)]
    backward = [(b, a) for a, b in forward]
    return lax.ppermute(to_next, axis, forward), lax.ppermute(to_previous, axis, backward)


def per_device(state, adjoint, thickness, direction, design_map, levels, blocks):
    n_row, n_col = lax.axis_size(ROW), lax.axis_size("pcol")
    n_dev = n_row * n_col
    last = n_row - 1
    info = jnp.stack([levels[0, 0], lax.axis_index(ROW).astype(jnp.int32)])
    rows = functools.partial(pairwise, n_row)
    cols = functools.partial(ring, "pcol", n_col)

    own, frame, first, end = call(
        start_kernel, [(n_dev, 1, 2 * DV), (7, FR, CC), (EDGE + 8, CC), (EDGE + 8, CC)], [HBM] * 7,
        [
            pltpu.SMEM((1,), jnp.int32), pltpu.VMEM((6, CR, CC), F32),
            pltpu.VMEM((CR, CC), jnp.int32), pltpu.VMEM((2, 1, DV), F32),
            pltpu.VMEM((n_dev, 1, 2 * DV), F32), pltpu.VMEM((BLK, BLK, CC), F32),
            pltpu.SemaphoreType.DMA((7,)),
            pltpu.SemaphoreType.DMA((BLK // PIECE,)),
        ],
        work=10**9, limit=LARGE, outs=[HBM] + [VMEM] * 3,
    )(levels.reshape(1), thickness.reshape(1, DV), direction.reshape(1, DV), state, adjoint, design_map, blocks)
    table = lax.all_to_all(own, ROW + ("pcol",), 0, 0, tiled=True).reshape(n_dev, 2 * DV)
    if n_dev < 256:
        table = jnp.concatenate([table, jnp.zeros((256 - n_dev, 2 * DV), F32)], axis=0)
    from_left, from_right = cols(end, first)
    side, one, two, around, edge = call(
        rows_kernel, [(7, FR, CC), (2, 16, CC), (2, 16, CC), (8, CC), (3, BLK, CC)], [SMEM] + [VMEM] * 3,
        work=10**11,
    )(info, frame, from_left, from_right)

    solve_scratch = [pltpu.VMEM((2, BLK, CC), F32)] * 4
    pairs = len(PAIRS) + 1
    main_f, side_f, cells = call(
        functools.partial(place_kernel, last),
        [
            (6, FR, CC), (6, FR, CC), jax.ShapeDtypeStruct((pairs, 2 * CC), jnp.int32),
        ],
        [SMEM] + [VMEM] * 4, [pltpu.VMEM((2, FR, CC), F32)], work=3 * 10**9,
    )(info, frame, side, *rows(one, two))
    resid, local, one, two, tcell, dcell = call(
        functools.partial(first_kernel, last),
        [
            (6, EXT, CC), (2, 6, EXT, CC), (2, 24, CC), (2, 24, CC), (2, FR, CC), (2, FR, CC),
        ],
        [SMEM] + [VMEM] * 7, solve_scratch,
    )(info, table, main_f, side_f, cells, blocks, edge, around)

    def operands(count):
        return [pltpu.VMEM((256, CR * CC), BF16), pltpu.VMEM((2 * count * DV, CR * CC), BF16)]

    (sums0,) = call(
        functools.partial(known_sums_kernel, n_col), [(256, DV)], [SMEM] + [VMEM] * 5, operands(1),
        work=3 * 10**8,
    )(info, frame, tcell, dcell, main_f, side_f)
    zframe, zside, image, local, one, two = call(
        functools.partial(second_kernel, last),
        [(6, FR, CC), (6, FR, CC), (6, EXT, CC), (2, 6, EXT, CC), (2, 24, CC), (2, 24, CC)],
        [SMEM] + [VMEM] * 7,
        solve_scratch,
    )(info, local, *rows(one, two), tcell, blocks, edge, around)
    (sums1,) = call(
        functools.partial(solved_sums_kernel, n_col), [(256, 2 * DV)], [SMEM] + [VMEM] * 6,
        operands(2), work=5 * 10**8,
    )(info, frame, tcell, main_f, side_f, zframe, zside)
    wframe, keep, send = call(
        functools.partial(third_kernel, last, n_col),
        [(6, FR, CC)] + [(n_dev // 2, 1, 6 * CC)] * 2, [SMEM] + [VMEM] * 12,
        [pltpu.VMEM((6, FR, CC), F32)] + operands(2),
    )(info, frame, resid, image, zframe, local, *rows(one, two), tcell, main_f, side_f, sums0, sums1)
    sums = keep + lax.ppermute(send, "core", [(0, 1), (1, 0)])
    got = lax.all_to_all(sums, ("y", "pcol"), 0, 0, tiled=True).reshape(n_dev // 2, 6 * CC)
    tangent, second, owned = call(
        last_kernel, [(3, CR, CC), (3, CR, CC), (1, CC)], [VMEM] * 3
    )(got, zframe, wframe)
    return tangent, second, owned.reshape(DV)


def solution(mesh):
    n_row, n_col = mesh.devices.shape
    fine = jax.sharding.Mesh(mesh.devices.reshape(n_row // 2, 2, n_col), ("y", "core", "pcol"))
    field = P(None, ROW, "pcol")
    design = P(("y", "core", "pcol"))
    return jax.shard_map(
        per_device,
        mesh=fine,
        in_specs=(field, field, design, design, P(ROW, "pcol"), P(ROW, "pcol"), P(ROW, None, "pcol")),
        out_specs=(field, field, design),
        check_vma=False,
    )
```

```python
import functools

import jax
import jax.numpy as jnp
from jax import lax
from jax.experimental import pallas as pl
from jax.experimental.pallas import tpu as pltpu
from jax.sharding import PartitionSpec as P

CR = 22
CC = 128
DV = 128
BLK = 72
EXT = CR + 2
FR = 32
ROW = ("y", "core")
WIDE = 3
F32 = jnp.float32
BF16 = jnp.bfloat16

VMEM = pl.BlockSpec(memory_space=pltpu.VMEM)
SMEM = pl.BlockSpec(memory_space=pltpu.SMEM)
HBM = pl.BlockSpec(memory_space=pltpu.HBM)
SMALL = 20 * 1024 * 1024
LARGE = 62 * 1024 * 1024


def call(kernel, out_shapes, in_specs, scratch=(), work=None, limit=SMALL, outs=None):
    cost = None
    if work is not None:
        cost = pl.CostEstimate(flops=work, bytes_accessed=1 << 20, transcendentals=0)
    return pl.pallas_call(
        kernel,
        out_shape=[
            s if isinstance(s, jax.ShapeDtypeStruct) else jax.ShapeDtypeStruct(s, F32)
            for s in out_shapes
        ],
        in_specs=list(in_specs),
        out_specs=[VMEM] * len(out_shapes) if outs is None else outs,
        cost_estimate=cost,
        scratch_shapes=list(scratch),
        compiler_params=pltpu.CompilerParams(vmem_limit_bytes=limit),
    )


def iota(shape, dim):
    return lax.broadcasted_iota(jnp.int32, shape, dim)


def pack_edges(tiles, width):
    lane = iota((8, CC), 1)
    first = jnp.zeros((8, CC), F32)
    last = jnp.zeros((8, CC), F32)
    for k, tile in enumerate(tiles):
        at = k * width
        here = (lane >= at) & (lane < at + width)
        first = jnp.where(here, pltpu.roll(tile, at, 1) if at else tile, first)
        last = jnp.where(here, pltpu.roll(tile, at + width, 1), last)
    return first, last


def unpack_edges(from_left, from_right, count, width):
    lane = iota((8, CC), 1)
    tiles = []
    for k in range(count):
        at = k * width
        right = pltpu.roll(from_right, CC - at, 1) if at else from_right
        shift = (CC - width - at) % CC
        left = pltpu.roll(from_left, shift, 1) if shift else from_left
        tiles.append(jnp.where(lane < width, right, jnp.where(lane >= CC - width, left, 0.0)))
    return tiles


def lanes_of(x):
    return iota(x.shape, x.ndim - 1)


def left_of(main, side):
    dim = main.ndim - 1
    return jnp.where(lanes_of(main) == 0, pltpu.roll(side, 1, dim), pltpu.roll(main, 1, dim))


def right_of(main, side):
    dim = main.ndim - 1
    return jnp.where(
        lanes_of(main) == CC - 1, pltpu.roll(side, CC - 1, dim), pltpu.roll(main, CC - 1, dim)
    )


def grid_mask(prow, last, start, rows):
    row = iota((rows, CC), 0) + (start - 8)
    outside = ((row < 0) & (prow == 0)) | ((row >= CR) & (prow == last))
    return jnp.where(outside, 0.0, 1.0).astype(F32)


PIECE = 24
EDGE = 3 * BLK


def start_kernel(
    levels, thickness, direction, state, adjoint, dmap, blocks,
    own_out, frame_out, first_out, last_out,
    level, known, cells, own, many, mats, sems, block_sems,
):
    copies = [
        pltpu.make_async_copy(thickness, own.at[0], sems.at[0]),
        pltpu.make_async_copy(direction, own.at[1], sems.at[1]),
        pltpu.make_async_copy(state, known.at[0:3], sems.at[2]),
        pltpu.make_async_copy(adjoint, known.at[3:6], sems.at[3]),
        pltpu.make_async_copy(dmap, cells, sems.at[4]),
        pltpu.make_async_copy(levels, level, sems.at[5]),
    ]
    pieces = []
    for k in range(BLK // PIECE):
        cut = pl.ds(k * PIECE, PIECE)
        pieces.append(pltpu.make_async_copy(blocks.at[cut], mats.at[cut], block_sems.at[k]))
    for copy in copies + pieces:
        copy.start()
    frame_out[...] = jnp.zeros_like(frame_out)
    upper = iota((8, CC), 1) >= 64
    for copy in copies:
        copy.wait()
    for k in range(2):
        many[:, :, k * DV:(k + 1) * DV] = jnp.broadcast_to(own[k][None], (many.shape[0], 1, DV))
    written = pltpu.make_async_copy(many, own_out, sems.at[6])
    written.start()
    frame_out[0:6, 8:8 + CR, :] = known[...]
    frame_out[6, 8:8 + CR, :] = cells[...].astype(F32)
    tiles = [frame_out[f, 8 + 8 * g:16 + 8 * g, :] for f in range(7) for g in range(3)]
    first, last = pack_edges(tiles, WIDE)
    depth = level[0].astype(F32)
    first_out[EDGE:, :] = jnp.where(upper, depth, first)
    last_out[EDGE:, :] = jnp.where(upper, depth, last)
    lane = iota((BLK, CC), 1)
    for c in range(3):
        packed = jnp.zeros((BLK, CC), F32)
        for i in range(min(32, BLK - 32 * c)):
            at = 32 * c + i
            if at % PIECE == 0:
                pieces[at // PIECE].wait()
            mat = mats[at]
            here = ((lane - 4 * i + 2) & (CC - 1)) < 4
            packed = jnp.where(here, pltpu.roll(mat, 4 * i, 1) if i else mat, packed)
        first_out[c * BLK:(c + 1) * BLK, :] = packed
        last_out[c * BLK:(c + 1) * BLK, :] = packed
    written.wait()


def by_turn(prow, up, down):
    even = prow % 2 == 0
    return jnp.where(even, down, up), jnp.where(even, up, down)


def rows_kernel(
    info, frame, from_left, from_right, side_out, one_out, two_out, levels_out, edge_out,
):
    left_end, right_end = from_left[EDGE:, :], from_right[EDGE:, :]
    tiles = unpack_edges(left_end, right_end, 21, WIDE)
    side_out[...] = jnp.zeros_like(side_out)
    for f in range(7):
        for g in range(3):
            side_out[f, 8 + 8 * g:16 + 8 * g, :] = tiles[3 * f + g]
    one_out[...] = jnp.zeros_like(one_out)
    two_out[...] = jnp.zeros_like(two_out)
    for tile, ref in ((0, frame), (1, side_out)):
        for f in range(7):
            one, two = by_turn(info[1], ref[f, 8:10, :], ref[f, 6 + CR:8 + CR, :])
            one_out[tile, 2 * f:2 * f + 2, :] = one
            two_out[tile, 2 * f:2 * f + 2, :] = two
    upper = iota((8, CC), 1) >= 64
    levels_out[...] = jnp.where(upper, left_end, pltpu.roll(right_end, 64, 1))
    lane = iota((BLK, CC), 1)
    for c in range(3):
        cut = slice(c * BLK, (c + 1) * BLK)
        edge_out[c] = jnp.where(lane % 4 < 2, from_right[cut, :], pltpu.roll(from_left[cut, :], 4, 1))


def apply_blocks(mats, vec):
    one = jnp.zeros((BLK, CC), F32)
    two = jnp.zeros((BLK, CC), F32)
    for at in range(BLK):
        mat = mats[at]
        one = one + mat * vec[0, at:at + 1, :]
        two = two + mat * vec[1, at:at + 1, :]
    return one, two


def over_columns(x):
    same = (iota((2 * CC, CC), 0) - iota((2 * CC, CC), 1)) % 4 == 0
    top = x.astype(BF16)
    rest = (x - top.astype(F32)).astype(BF16)
    return jnp.dot(
        jnp.concatenate([top, rest], axis=1), jnp.where(same, 1.0, 0.0).astype(BF16),
        preferred_element_type=F32,
    )


def apply_edge(edge, vec):
    row = iota((BLK, CC), 0)
    place = iota((BLK, CC), 1) // 4
    out = jnp.zeros((BLK, CC), F32)
    for c in range(3):
        low, high = 32 * c, min(32 * c + 32, BLK)
        mine = row[low:high] == place[low:high] + 32 * c
        flat = jnp.sum(jnp.where(mine, vec[low:high], 0.0), axis=0, keepdims=True)
        out = out + edge[c] * flat
    return out


def local_solve(mats, edge, vec, total, side_vec, side_total, level, levels):
    lane = iota((BLK, CC), 1)
    ours = (lane < 2) | (lane >= CC - 2)
    kept = [jnp.where(ours, side_vec[n], 0.0) for n in range(2)]
    spread = over_columns(jnp.concatenate(kept, axis=0))
    side_vec[0] = spread[:BLK]
    side_vec[1] = spread[BLK:]
    total[...] = jnp.zeros_like(total)
    side_total[...] = jnp.zeros_like(side_total)
    top = jnp.maximum(level, jnp.max(levels[...]).astype(jnp.int32))

    def term(order, carry):
        scale = jnp.where(order == 0, 1.0, 0.5).astype(F32)
        keep = jnp.where(order < level, 1.0, 0.0).astype(F32)
        side_keep = levels[0:1, :] > order.astype(F32)
        parts = [apply_edge(edge, side_vec[n]) for n in range(2)]
        outs = scale * over_columns(jnp.concatenate(parts, axis=0))
        for n in range(2):
            out = outs[n * BLK:(n + 1) * BLK]
            side_vec[n] = out
            side_total[n] += jnp.where(side_keep, out, 0.0)
        for n, out in enumerate(apply_blocks(mats, vec)):
            out = scale * out
            vec[n] = out
            total[n] += keep * out
        return carry

    lax.fori_loop(0, top, term, 0)


def put_results(prow, total, side_total, local_out, one_out, two_out):
    one_out[...] = jnp.zeros_like(one_out)
    two_out[...] = jnp.zeros_like(two_out)
    for tile, ref in ((0, total), (1, side_total)):
        local_out[tile] = ref[...].reshape(6, EXT, CC)
        for f in range(6):
            one, two = by_turn(prow, local_out[tile, f, 0:3, :], local_out[tile, f, EXT - 3:EXT, :])
            one_out[tile, 3 * f:3 * f + 3, :] = one
            two_out[tile, 3 * f:3 * f + 3, :] = two


def join(prow, last, local, got_one, got_two, frames):
    inside = grid_mask(prow, last, 0, FR)
    for tile, frame in enumerate(frames):
        frame[...] = jnp.zeros_like(frame)
        frame[:, 7:7 + EXT, :] = local[tile]
        for f in range(6):
            cut = slice(3 * f, 3 * f + 3)
            above, below = by_turn(prow, got_one[tile, cut, :], got_two[tile, cut, :])
            frame[f, 6:9, :] += jnp.where(prow == 0, 0.0, above)
            frame[f, 7 + CR:10 + CR, :] += jnp.where(prow == last, 0.0, below)
        frame[...] = frame[...] * inside[None]


PAIRS = range(6, FR, 2)


def place_cells(index, cells):
    lane1 = iota((1, CC), 1)
    vecs = [jnp.concatenate([index[0][r:r + 1], index[0][r + 1:r + 2]], axis=1) for r in PAIRS]
    packs = []
    for half in range(2):
        vec = jnp.zeros((1, CC), jnp.int32)
        for i in range(16):
            r = 16 * half + i
            vec = jnp.where(lane1 // 8 == i, pltpu.roll(index[1][r:r + 1], (8 * i + 4) % CC, 1), vec)
        packs.append(vec)
    vecs.append(jnp.concatenate(packs, axis=1))
    for k, vec in enumerate(vecs):
        cells[k:k + 1, :] = vec


def look_up(table, cells, tcell, dcell):
    flipped = table[...].T
    part0 = flipped.astype(BF16)
    part1 = (flipped - part0.astype(F32)).astype(BF16)
    lhs = jnp.concatenate([part0, part1], axis=0)
    lane1 = iota((1, CC), 1)

    def both(k):
        vec = cells[k:k + 1, :]
        hot = jnp.where(iota((256, 2 * CC), 0) == vec // DV, 1.0, 0.0).astype(BF16)
        got = jnp.dot(lhs, hot, preferred_element_type=F32)
        mine = iota((DV, 2 * CC), 0) == vec % DV
        tv = jnp.sum(jnp.where(mine, got[0:DV] + got[2 * DV:3 * DV], 0.0), axis=0, keepdims=True)
        dv = jnp.sum(jnp.where(mine, got[DV:2 * DV] + got[3 * DV:4 * DV], 0.0), axis=0, keepdims=True)
        return tv, dv

    for k, r in enumerate(PAIRS):
        tv, dv = both(k)
        for h in range(2):
            tcell[0, r + h:r + h + 1, :] = tv[:, h * CC:(h + 1) * CC]
            dcell[0, r + h:r + h + 1, :] = dv[:, h * CC:(h + 1) * CC]
    tv, dv = both(len(PAIRS))
    for half in range(2):
        for i in range(16):
            r = 16 * half + i
            shift = (CC - 8 * i - 4) % CC
            keep = (lane1 < 4) | (lane1 >= CC - 4)
            cut = slice(half * CC, (half + 1) * CC)
            tcell[1, r:r + 1, :] = jnp.where(keep, pltpu.roll(tv[:, cut], shift, 1), 0.0)
            dcell[1, r:r + 1, :] = jnp.where(keep, pltpu.roll(dv[:, cut], shift, 1), 0.0)


def weights_of(main, side, lo, hi):
    here = main[lo:hi]
    return [
        0.5 * (here + main[lo - 1:hi - 1]),
        0.5 * (here + main[lo + 1:hi + 1]),
        0.5 * (here + left_of(here, side[lo:hi])),
        0.5 * (here + right_of(here, side[lo:hi])),
    ]


def differences(main, side, lo, hi):
    here = main[:, lo:hi, :]
    beside = side[:, lo:hi, :]
    return [
        here - main[:, lo - 1:hi - 1, :],
        here - main[:, lo + 1:hi + 1, :],
        here - left_of(here, beside),
        here - right_of(here, beside),
    ]


def place_kernel(last, info, frame, side, got_one, got_two, main_f, side_f, cells, index_scr):
    inside = grid_mask(info[1], last, 0, FR)
    for tile, ref, source in ((0, main_f, frame), (1, side_f, side)):
        for f in range(7):
            out = ref.at[f] if f < 6 else index_scr.at[tile]
            out[...] = source[f]
            cut = slice(2 * f, 2 * f + 2)
            above, below = by_turn(info[1], got_one[tile, cut, :], got_two[tile, cut, :])
            out[6:8, :] = above * inside[6:8]
            out[8 + CR:10 + CR, :] = below * inside[8 + CR:10 + CR]
    place_cells([index_scr[tile].astype(jnp.int32) for tile in range(2)], cells)


def first_kernel(
    last, info, table, main_f, side_f, cells, mats, edge, levels,
    resid_out, local_out, one_out, two_out, tcell, dcell,
    vec, total, side_vec, side_total,
):
    level, prow = info[0], info[1]
    inside = grid_mask(prow, last, 0, FR)
    tcell[...] = jnp.zeros_like(tcell)
    dcell[...] = jnp.zeros_like(dcell)
    look_up(table, cells, tcell, dcell)
    for tile in range(2):
        tcell[tile] = tcell[tile] * inside
    slope = [3.0 * tcell[tile] * tcell[tile] * dcell[tile] for tile in range(2)]
    lo, hi = 7, 7 + EXT
    frames = (main_f, side_f)
    for tile, out in ((0, vec), (1, side_vec)):
        here, beside = frames[tile], frames[1 - tile]
        rhs = jnp.zeros((6, EXT, CC), F32)
        for weight, diff in zip(
            weights_of(slope[tile], slope[1 - tile], lo, hi), differences(here, beside, lo, hi)
        ):
            rhs = rhs - weight[None] * diff
        rhs = rhs * inside[lo:hi][None]
        if tile == 0:
            resid_out[...] = rhs
        out[...] = rhs.reshape(2, BLK, CC)
    local_solve(mats, edge, vec, total, side_vec, side_total, level, levels)
    put_results(prow, total, side_total, local_out, one_out, two_out)


def stiffness(main_f, side_f, main_t, side_t, lo, hi):
    stiff = [t * t * t for t in (main_t[...], side_t[...])]
    out = main_f[:, lo:hi, :]
    parts = differences(main_f, side_f, lo, hi)
    for weight, diff in zip(weights_of(stiff[0], stiff[1], lo, hi), parts):
        out = out + weight[None] * diff
    return out


def second_kernel(
    last, info, local, got_one, got_two, tcell, mats, edge, levels,
    main_f, side_f, image_out, local_out, one_out, two_out,
    vec, total, side_vec, side_total,
):
    level, prow = info[0], info[1]
    frames = (main_f, side_f)
    join(prow, last, local, got_one, got_two, frames)
    lo, hi = 7, 7 + EXT
    inside = grid_mask(prow, last, lo, EXT)
    for tile, out in ((0, vec), (1, side_vec)):
        image = stiffness(
            frames[tile], frames[1 - tile], tcell.at[tile], tcell.at[1 - tile], lo, hi
        ) * inside[None]
        if tile == 0:
            image_out[...] = image
        out[...] = image.reshape(2, BLK, CC)
    local_solve(mats, edge, vec, total, side_vec, side_total, level, levels)
    put_results(prow, total, side_total, local_out, one_out, two_out)


def dot3(a, b, i, j):
    out = jnp.zeros((CR, CC), F32)
    for an, bn in zip(a, b):
        for c in range(3):
            out = out + an[i + c] * bn[j + c]
    return out


def design_sums(n_col, info, frame, values, left_op, right_op):
    cells = frame[6, 8:8 + CR, :].astype(jnp.int32)
    owner = cells // DV
    low = cells % DV
    other = jnp.where((owner // n_col) % 2 == info[1] % 2, 0, 128)
    high = other + (owner // (2 * n_col)) * n_col + owner % n_col
    count = len(values)
    tops = [value.astype(BF16) for value in values]
    rests = [(value - top.astype(F32)).astype(BF16) for value, top in zip(values, tops)]
    for row in range(CR):
        cut = slice(CC * row, CC * row + CC)
        left_op[:, cut] = jnp.where(iota((256, CC), 0) == high[row:row + 1], 1.0, 0.0).astype(BF16)
        hot = jnp.where(iota((DV, CC), 0) == low[row:row + 1], 1.0, 0.0).astype(BF16)
        for k, part in enumerate(tops + rests):
            right_op[k * DV:(k + 1) * DV, cut] = hot * part[row:row + 1]
    sums = lax.dot_general(
        left_op[...], right_op[...], (((1,), (1,)), ((), ())), preferred_element_type=F32
    )
    return sums[:, :count * DV] + sums[:, count * DV:]


LO, HI = 8, 8 + CR


def known_sums_kernel(n_col, info, frame, tcell, dcell, main_f, side_f, out, left_op, right_op):
    known_d = differences(main_f, side_f, LO, HI)
    value = (-3.0 * tcell[0, LO:HI, :] * dcell[0, LO:HI, :]) * dot3(known_d, known_d, 3, 0)
    out[...] = design_sums(n_col, info, frame, [value], left_op, right_op)


def solved_values(tcell, known_d, solved_d):
    t = tcell[0, LO:HI, :]
    slope = -1.5 * t * t
    return [slope * dot3(solved_d, known_d, 3, 0), slope * dot3(known_d, solved_d, 3, 0)]


def solved_sums_kernel(
    n_col, info, frame, tcell, main_f, side_f, zframe, zside, out, left_op, right_op
):
    values = solved_values(
        tcell, differences(main_f, side_f, LO, HI), differences(zframe, zside, LO, HI)
    )
    out[...] = design_sums(n_col, info, frame, values, left_op, right_op)


def third_kernel(
    last, n_col, info, frame, resid, image, zframe, local, got_one, got_two,
    tcell, main_f, side_f, sums0, sums1,
    wframe, keep_out, send_out, wside, left_op, right_op,
):
    join(info[1], last, local, got_one, got_two, (wframe, wside))
    v = stiffness(wframe, wside, tcell.at[0], tcell.at[1], LO, HI)
    r = resid[:, 1:1 + CR, :]
    q = image[:, 1:1 + CR, :]
    z = zframe[:, LO:HI, :]
    w = wframe[:, LO:HI, :]
    lane = iota((1, CC), 1)
    dots = jnp.zeros((1, CC), F32)
    pairs = ((r, z), (z, q), (r, w), (q, w), (z, v), (w, v))
    for k, (a, b) in enumerate(pairs):
        ab = a * b
        for s in range(2):
            part = ab[3 * s] + ab[3 * s + 1] + ab[3 * s + 2]
            value = jnp.sum(jnp.sum(part, axis=0, keepdims=True), axis=1, keepdims=True)
            dots = jnp.where(lane == 2 * k + s, value, dots)
    values = solved_values(
        tcell, differences(main_f, side_f, LO, HI), differences(wframe, wside, LO, HI)
    )
    sums = design_sums(n_col, info, frame, values, left_op, right_op)
    for half, out in ((0, keep_out), (1, send_out)):
        count = out.shape[0]
        rows = slice(128 * half, 128 * half + count)
        out[:, 0:CC] = jnp.broadcast_to(dots, (count, CC))
        out[:, CC:2 * CC] = sums0[rows, :]
        out[:, 2 * CC:4 * CC] = sums1[rows, :]
        out[:, 4 * CC:] = sums[rows]


def last_kernel(got, zframe, wframe, tangent, second, owned):
    sums = jnp.sum(got[...], axis=0, keepdims=True)
    dots = sums[:, 0:CC]
    lane = iota((1, CC), 1)

    def pick(k):
        return jnp.sum(jnp.where(lane == k, dots, 0.0), axis=1, keepdims=True)

    coeffs = []
    for s in range(2):
        rz, zq, rw, qw, zv, wv = (pick(2 * k + s) for k in range(6))
        alpha = rz / zq
        rz1 = rz - alpha * (zq + rw) + alpha * alpha * qw
        grow = 1.0 + rz1 / rz
        pq = grow * grow * zq - grow * alpha * (zv + qw) + alpha * alpha * wv
        alpha1 = rz1 / pq
        coeffs.append((alpha + alpha1 * grow, -alpha1 * alpha))
    for s, out in ((0, tangent), (1, second)):
        c0, c1 = coeffs[s]
        for f in range(3):
            out[f] = c0 * zframe[3 * s + f, 8:8 + CR, :] + c1 * wframe[3 * s + f, 8:8 + CR, :]
    h = [sums[:, (k + 1) * CC:(k + 2) * CC] for k in range(5)]
    owned[...] = (
        h[0] + coeffs[1][0] * h[1] + coeffs[0][0] * h[2] + coeffs[1][1] * h[3] + coeffs[0][1] * h[4]
    )


def pairwise(count, one, two):
    first = [(i, i ^ 1) for i in range(count)]
    second = [(i, (i + (1 if i % 2 else -1)) % count) for i in range(count)]
    return lax.ppermute(one, ROW, first), lax.ppermute(two, ROW, second)


def ring(axis, count, to_next, to_previous):
    forward = [(i, (i + 1) % count) for i in range(count)]
    backward = [(b, a) for a, b in forward]
    return lax.ppermute(to_next, axis, forward), lax.ppermute(to_previous, axis, backward)


def per_device(state, adjoint, thickness, direction, design_map, levels, blocks):
    n_row, n_col = lax.axis_size(ROW), lax.axis_size("pcol")
    n_dev = n_row * n_col
    last = n_row - 1
    info = jnp.stack([levels[0, 0], lax.axis_index(ROW).astype(jnp.int32)])
    rows = functools.partial(pairwise, n_row)
    cols = functools.partial(ring, "pcol", n_col)

    own, frame, first, end = call(
        start_kernel, [(n_dev, 1, 2 * DV), (7, FR, CC), (EDGE + 8, CC), (EDGE + 8, CC)], [HBM] * 7,
        [
            pltpu.SMEM((1,), jnp.int32), pltpu.VMEM((6, CR, CC), F32),
            pltpu.VMEM((CR, CC), jnp.int32), pltpu.VMEM((2, 1, DV), F32),
            pltpu.VMEM((n_dev, 1, 2 * DV), F32), pltpu.VMEM((BLK, BLK, CC), F32),
            pltpu.SemaphoreType.DMA((7,)),
            pltpu.SemaphoreType.DMA((BLK // PIECE,)),
        ],
        work=10**9, limit=LARGE, outs=[HBM] + [VMEM] * 3,
    )(levels.reshape(1), thickness.reshape(1, DV), direction.reshape(1, DV), state, adjoint, design_map, blocks)
    table = lax.all_to_all(own, ROW + ("pcol",), 0, 0, tiled=True).reshape(n_dev, 2 * DV)
    if n_dev < 256:
        table = jnp.concatenate([table, jnp.zeros((256 - n_dev, 2 * DV), F32)], axis=0)
    from_left, from_right = cols(end, first)
    side, one, two, around, edge = call(
        rows_kernel, [(7, FR, CC), (2, 16, CC), (2, 16, CC), (8, CC), (3, BLK, CC)], [SMEM] + [VMEM] * 3,
        work=10**11,
    )(info, frame, from_left, from_right)

    solve_scratch = [pltpu.VMEM((2, BLK, CC), F32)] * 4
    pairs = len(PAIRS) + 1
    main_f, side_f, cells = call(
        functools.partial(place_kernel, last),
        [
            (6, FR, CC), (6, FR, CC), jax.ShapeDtypeStruct((pairs, 2 * CC), jnp.int32),
        ],
        [SMEM] + [VMEM] * 4, [pltpu.VMEM((2, FR, CC), F32)], work=3 * 10**9,
    )(info, frame, side, *rows(one, two))
    resid, local, one, two, tcell, dcell = call(
        functools.partial(first_kernel, last),
        [
            (6, EXT, CC), (2, 6, EXT, CC), (2, 24, CC), (2, 24, CC), (2, FR, CC), (2, FR, CC),
        ],
        [SMEM] + [VMEM] * 7, solve_scratch,
    )(info, table, main_f, side_f, cells, blocks, edge, around)

    def operands(count):
        return [pltpu.VMEM((256, CR * CC), BF16), pltpu.VMEM((2 * count * DV, CR * CC), BF16)]

    (sums0,) = call(
        functools.partial(known_sums_kernel, n_col), [(256, DV)], [SMEM] + [VMEM] * 5, operands(1),
        work=3 * 10**8,
    )(info, frame, tcell, dcell, main_f, side_f)
    zframe, zside, image, local, one, two = call(
        functools.partial(second_kernel, last),
        [(6, FR, CC), (6, FR, CC), (6, EXT, CC), (2, 6, EXT, CC), (2, 24, CC), (2, 24, CC)],
        [SMEM] + [VMEM] * 7,
        solve_scratch,
    )(info, local, *rows(one, two), tcell, blocks, edge, around)
    (sums1,) = call(
        functools.partial(solved_sums_kernel, n_col), [(256, 2 * DV)], [SMEM] + [VMEM] * 6,
        operands(2), work=5 * 10**8,
    )(info, frame, tcell, main_f, side_f, zframe, zside)
    wframe, keep, send = call(
        functools.partial(third_kernel, last, n_col),
        [(6, FR, CC)] + [(n_dev // 2, 6 * CC)] * 2, [SMEM] + [VMEM] * 12,
        [pltpu.VMEM((6, FR, CC), F32)] + operands(2),
    )(info, frame, resid, image, zframe, local, *rows(one, two), tcell, main_f, side_f, sums0, sums1)
    sums = keep + lax.ppermute(send, "core", [(0, 1), (1, 0)])
    got = lax.all_to_all(sums, ("y", "pcol"), 0, 0, tiled=True)
    tangent, second, owned = call(
        last_kernel, [(3, CR, CC), (3, CR, CC), (1, CC)], [VMEM] * 3
    )(got, zframe, wframe)
    return tangent, second, owned.reshape(DV)


def solution(mesh):
    n_row, n_col = mesh.devices.shape
    fine = jax.sharding.Mesh(mesh.devices.reshape(n_row // 2, 2, n_col), ("y", "core", "pcol"))
    field = P(None, ROW, "pcol")
    design = P(("y", "core", "pcol"))
    return jax.shard_map(
        per_device,
        mesh=fine,
        in_specs=(field, field, design, design, P(ROW, "pcol"), P(ROW, "pcol"), P(ROW, None, "pcol")),
        out_specs=(field, field, design),
        check_vma=False,
    )
```

```python
import functools

import jax
import jax.numpy as jnp
from jax import lax
from jax.experimental import pallas as pl
from jax.experimental.pallas import tpu as pltpu
from jax.sharding import PartitionSpec as P

CR = 22
CC = 128
DV = 128
BLK = 72
MAXLEVEL = 4
EXT = CR + 2
FR = 32
ROW = ("y", "core")
WIDE = 3
F32 = jnp.float32
BF16 = jnp.bfloat16

VMEM = pl.BlockSpec(memory_space=pltpu.VMEM)
SMEM = pl.BlockSpec(memory_space=pltpu.SMEM)
HBM = pl.BlockSpec(memory_space=pltpu.HBM)
SMALL = 20 * 1024 * 1024
LARGE = 62 * 1024 * 1024


def call(kernel, out_shapes, in_specs, scratch=(), work=None, limit=SMALL, outs=None):
    cost = None
    if work is not None:
        cost = pl.CostEstimate(flops=work, bytes_accessed=1 << 20, transcendentals=0)
    return pl.pallas_call(
        kernel,
        out_shape=[
            s if isinstance(s, jax.ShapeDtypeStruct) else jax.ShapeDtypeStruct(s, F32)
            for s in out_shapes
        ],
        in_specs=list(in_specs),
        out_specs=[VMEM] * len(out_shapes) if outs is None else outs,
        cost_estimate=cost,
        scratch_shapes=list(scratch),
        compiler_params=pltpu.CompilerParams(vmem_limit_bytes=limit),
    )


def iota(shape, dim):
    return lax.broadcasted_iota(jnp.int32, shape, dim)


def pack_edges(tiles, width):
    lane = iota((8, CC), 1)
    first = jnp.zeros((8, CC), F32)
    last = jnp.zeros((8, CC), F32)
    for k, tile in enumerate(tiles):
        at = k * width
        here = (lane >= at) & (lane < at + width)
        first = jnp.where(here, pltpu.roll(tile, at, 1) if at else tile, first)
        last = jnp.where(here, pltpu.roll(tile, at + width, 1), last)
    return first, last


def unpack_edges(from_left, from_right, count, width):
    lane = iota((8, CC), 1)
    tiles = []
    for k in range(count):
        at = k * width
        right = pltpu.roll(from_right, CC - at, 1) if at else from_right
        shift = (CC - width - at) % CC
        left = pltpu.roll(from_left, shift, 1) if shift else from_left
        tiles.append(jnp.where(lane < width, right, jnp.where(lane >= CC - width, left, 0.0)))
    return tiles


def lanes_of(x):
    return iota(x.shape, x.ndim - 1)


def left_of(main, side):
    dim = main.ndim - 1
    return jnp.where(lanes_of(main) == 0, pltpu.roll(side, 1, dim), pltpu.roll(main, 1, dim))


def right_of(main, side):
    dim = main.ndim - 1
    return jnp.where(
        lanes_of(main) == CC - 1, pltpu.roll(side, CC - 1, dim), pltpu.roll(main, CC - 1, dim)
    )


def grid_mask(prow, last, start, rows):
    row = iota((rows, CC), 0) + (start - 8)
    outside = ((row < 0) & (prow == 0)) | ((row >= CR) & (prow == last))
    return jnp.where(outside, 0.0, 1.0).astype(F32)


PIECE = 24
EDGE = 3 * BLK


def start_kernel(
    levels, thickness, direction, state, adjoint, dmap, blocks,
    own_out, frame_out, first_out, last_out,
    level, known, cells, own, many, mats, sems, block_sems,
):
    copies = [
        pltpu.make_async_copy(thickness, own.at[0], sems.at[0]),
        pltpu.make_async_copy(direction, own.at[1], sems.at[1]),
        pltpu.make_async_copy(state, known.at[0:3], sems.at[2]),
        pltpu.make_async_copy(adjoint, known.at[3:6], sems.at[3]),
        pltpu.make_async_copy(dmap, cells, sems.at[4]),
        pltpu.make_async_copy(levels, level, sems.at[5]),
    ]
    pieces = []
    for k in range(BLK // PIECE):
        cut = pl.ds(k * PIECE, PIECE)
        pieces.append(pltpu.make_async_copy(blocks.at[cut], mats.at[cut], block_sems.at[k]))
    for copy in copies + pieces:
        copy.start()
    frame_out[...] = jnp.zeros_like(frame_out)
    upper = iota((8, CC), 1) >= 64
    for copy in copies:
        copy.wait()
    for k in range(2):
        many[:, :, k * DV:(k + 1) * DV] = jnp.broadcast_to(own[k][None], (many.shape[0], 1, DV))
    written = pltpu.make_async_copy(many, own_out, sems.at[6])
    written.start()
    frame_out[0:6, 8:8 + CR, :] = known[...]
    frame_out[6, 8:8 + CR, :] = cells[...].astype(F32)
    tiles = [frame_out[f, 8 + 8 * g:16 + 8 * g, :] for f in range(7) for g in range(3)]
    first, last = pack_edges(tiles, WIDE)
    depth = level[0].astype(F32)
    first_out[EDGE:, :] = jnp.where(upper, depth, first)
    last_out[EDGE:, :] = jnp.where(upper, depth, last)
    lane = iota((BLK, CC), 1)
    for c in range(3):
        packed = jnp.zeros((BLK, CC), F32)
        for i in range(min(32, BLK - 32 * c)):
            at = 32 * c + i
            if at % PIECE == 0:
                pieces[at // PIECE].wait()
            mat = mats[at]
            here = ((lane - 4 * i + 2) & (CC - 1)) < 4
            packed = jnp.where(here, pltpu.roll(mat, 4 * i, 1) if i else mat, packed)
        first_out[c * BLK:(c + 1) * BLK, :] = packed
        last_out[c * BLK:(c + 1) * BLK, :] = packed
    written.wait()


def by_turn(prow, up, down):
    even = prow % 2 == 0
    return jnp.where(even, down, up), jnp.where(even, up, down)


def rows_kernel(
    info, frame, from_left, from_right, side_out, one_out, two_out, levels_out, edge_out,
):
    left_end, right_end = from_left[EDGE:, :], from_right[EDGE:, :]
    tiles = unpack_edges(left_end, right_end, 21, WIDE)
    side_out[...] = jnp.zeros_like(side_out)
    for f in range(7):
        for g in range(3):
            side_out[f, 8 + 8 * g:16 + 8 * g, :] = tiles[3 * f + g]
    one_out[...] = jnp.zeros_like(one_out)
    two_out[...] = jnp.zeros_like(two_out)
    for tile, ref in ((0, frame), (1, side_out)):
        for f in range(7):
            one, two = by_turn(info[1], ref[f, 8:10, :], ref[f, 6 + CR:8 + CR, :])
            one_out[tile, 2 * f:2 * f + 2, :] = one
            two_out[tile, 2 * f:2 * f + 2, :] = two
    upper = iota((8, CC), 1) >= 64
    levels_out[...] = jnp.where(upper, left_end, pltpu.roll(right_end, 64, 1))
    lane = iota((BLK, CC), 1)
    for c in range(3):
        cut = slice(c * BLK, (c + 1) * BLK)
        edge_out[c] = jnp.where(lane % 4 < 2, from_right[cut, :], pltpu.roll(from_left[cut, :], 4, 1))


def apply_blocks(mats, vec):
    one = jnp.zeros((BLK, CC), F32)
    two = jnp.zeros((BLK, CC), F32)
    for at in range(BLK):
        mat = mats[at]
        one = one + mat * vec[0, at:at + 1, :]
        two = two + mat * vec[1, at:at + 1, :]
    return one, two


def over_columns(x):
    same = (iota((2 * CC, CC), 0) - iota((2 * CC, CC), 1)) % 4 == 0
    top = x.astype(BF16)
    rest = (x - top.astype(F32)).astype(BF16)
    return jnp.dot(
        jnp.concatenate([top, rest], axis=1), jnp.where(same, 1.0, 0.0).astype(BF16),
        preferred_element_type=F32,
    )


def apply_edge(edge, vec):
    row = iota((BLK, CC), 0)
    place = iota((BLK, CC), 1) // 4
    out = jnp.zeros((BLK, CC), F32)
    for c in range(3):
        low, high = 32 * c, min(32 * c + 32, BLK)
        mine = row[low:high] == place[low:high] + 32 * c
        flat = jnp.sum(jnp.where(mine, vec[low:high], 0.0), axis=0, keepdims=True)
        out = out + edge[c] * flat
    return out


def local_solve(mats, edge, vec, total, side_vec, side_total, level, levels):
    lane = iota((BLK, CC), 1)
    ours = (lane < 2) | (lane >= CC - 2)
    kept = [jnp.where(ours, side_vec[n], 0.0) for n in range(2)]
    spread = over_columns(jnp.concatenate(kept, axis=0))
    side_vec[0] = spread[:BLK]
    side_vec[1] = spread[BLK:]
    total[...] = jnp.zeros_like(total)
    side_total[...] = jnp.zeros_like(side_total)

    def term(order, carry):
        scale = jnp.where(order == 0, 1.0, 0.5).astype(F32)
        keep = jnp.where(order < level, 1.0, 0.0).astype(F32)
        side_keep = levels[0:1, :] > order.astype(F32)
        parts = [apply_edge(edge, side_vec[n]) for n in range(2)]
        outs = scale * over_columns(jnp.concatenate(parts, axis=0))
        for n in range(2):
            out = outs[n * BLK:(n + 1) * BLK]
            side_vec[n] = out
            side_total[n] += jnp.where(side_keep, out, 0.0)
        for n, out in enumerate(apply_blocks(mats, vec)):
            out = scale * out
            vec[n] = out
            total[n] += keep * out
        return carry

    lax.fori_loop(0, MAXLEVEL, term, 0)


def put_results(prow, total, side_total, local_out, one_out, two_out):
    one_out[...] = jnp.zeros_like(one_out)
    two_out[...] = jnp.zeros_like(two_out)
    for tile, ref in ((0, total), (1, side_total)):
        local_out[tile] = ref[...].reshape(6, EXT, CC)
        for f in range(6):
            one, two = by_turn(prow, local_out[tile, f, 0:3, :], local_out[tile, f, EXT - 3:EXT, :])
            one_out[tile, 3 * f:3 * f + 3, :] = one
            two_out[tile, 3 * f:3 * f + 3, :] = two


def join(prow, last, local, got_one, got_two, frames):
    inside = grid_mask(prow, last, 0, FR)
    for tile, frame in enumerate(frames):
        frame[...] = jnp.zeros_like(frame)
        frame[:, 7:7 + EXT, :] = local[tile]
        for f in range(6):
            cut = slice(3 * f, 3 * f + 3)
            above, below = by_turn(prow, got_one[tile, cut, :], got_two[tile, cut, :])
            frame[f, 6:9, :] += jnp.where(prow == 0, 0.0, above)
            frame[f, 7 + CR:10 + CR, :] += jnp.where(prow == last, 0.0, below)
        frame[...] = frame[...] * inside[None]


PAIRS = range(6, FR, 2)


def place_cells(index, cells):
    lane1 = iota((1, CC), 1)
    vecs = [jnp.concatenate([index[0][r:r + 1], index[0][r + 1:r + 2]], axis=1) for r in PAIRS]
    packs = []
    for half in range(2):
        vec = jnp.zeros((1, CC), jnp.int32)
        for i in range(16):
            r = 16 * half + i
            vec = jnp.where(lane1 // 8 == i, pltpu.roll(index[1][r:r + 1], (8 * i + 4) % CC, 1), vec)
        packs.append(vec)
    vecs.append(jnp.concatenate(packs, axis=1))
    for k, vec in enumerate(vecs):
        cells[k:k + 1, :] = vec


def look_up(table, cells, tcell, dcell):
    flipped = table[...].T
    part0 = flipped.astype(BF16)
    part1 = (flipped - part0.astype(F32)).astype(BF16)
    lhs = jnp.concatenate([part0, part1], axis=0)
    lane1 = iota((1, CC), 1)

    def both(k):
        vec = cells[k:k + 1, :]
        hot = jnp.where(iota((256, 2 * CC), 0) == vec // DV, 1.0, 0.0).astype(BF16)
        got = jnp.dot(lhs, hot, preferred_element_type=F32)
        mine = iota((DV, 2 * CC), 0) == vec % DV
        tv = jnp.sum(jnp.where(mine, got[0:DV] + got[2 * DV:3 * DV], 0.0), axis=0, keepdims=True)
        dv = jnp.sum(jnp.where(mine, got[DV:2 * DV] + got[3 * DV:4 * DV], 0.0), axis=0, keepdims=True)
        return tv, dv

    for k, r in enumerate(PAIRS):
        tv, dv = both(k)
        for h in range(2):
            tcell[0, r + h:r + h + 1, :] = tv[:, h * CC:(h + 1) * CC]
            dcell[0, r + h:r + h + 1, :] = dv[:, h * CC:(h + 1) * CC]
    tv, dv = both(len(PAIRS))
    for half in range(2):
        for i in range(16):
            r = 16 * half + i
            shift = (CC - 8 * i - 4) % CC
            keep = (lane1 < 4) | (lane1 >= CC - 4)
            cut = slice(half * CC, (half + 1) * CC)
            tcell[1, r:r + 1, :] = jnp.where(keep, pltpu.roll(tv[:, cut], shift, 1), 0.0)
            dcell[1, r:r + 1, :] = jnp.where(keep, pltpu.roll(dv[:, cut], shift, 1), 0.0)


def weights_of(main, side, lo, hi):
    here = main[lo:hi]
    return [
        0.5 * (here + main[lo - 1:hi - 1]),
        0.5 * (here + main[lo + 1:hi + 1]),
        0.5 * (here + left_of(here, side[lo:hi])),
        0.5 * (here + right_of(here, side[lo:hi])),
    ]


def differences(main, side, lo, hi):
    here = main[:, lo:hi, :]
    beside = side[:, lo:hi, :]
    return [
        here - main[:, lo - 1:hi - 1, :],
        here - main[:, lo + 1:hi + 1, :],
        here - left_of(here, beside),
        here - right_of(here, beside),
    ]


def place_kernel(last, info, frame, side, got_one, got_two, main_f, side_f, cells, index_scr):
    inside = grid_mask(info[1], last, 0, FR)
    for tile, ref, source in ((0, main_f, frame), (1, side_f, side)):
        for f in range(7):
            out = ref.at[f] if f < 6 else index_scr.at[tile]
            out[...] = source[f]
            cut = slice(2 * f, 2 * f + 2)
            above, below = by_turn(info[1], got_one[tile, cut, :], got_two[tile, cut, :])
            out[6:8, :] = above * inside[6:8]
            out[8 + CR:10 + CR, :] = below * inside[8 + CR:10 + CR]
    place_cells([index_scr[tile].astype(jnp.int32) for tile in range(2)], cells)


def first_kernel(
    last, info, table, main_f, side_f, cells, mats, edge, levels,
    resid_out, local_out, one_out, two_out, tcell, dcell,
    vec, total, side_vec, side_total,
):
    level, prow = info[0], info[1]
    inside = grid_mask(prow, last, 0, FR)
    tcell[...] = jnp.zeros_like(tcell)
    dcell[...] = jnp.zeros_like(dcell)
    look_up(table, cells, tcell, dcell)
    for tile in range(2):
        tcell[tile] = tcell[tile] * inside
    slope = [3.0 * tcell[tile] * tcell[tile] * dcell[tile] for tile in range(2)]
    lo, hi = 7, 7 + EXT
    frames = (main_f, side_f)
    for tile, out in ((0, vec), (1, side_vec)):
        here, beside = frames[tile], frames[1 - tile]
        rhs = jnp.zeros((6, EXT, CC), F32)
        for weight, diff in zip(
            weights_of(slope[tile], slope[1 - tile], lo, hi), differences(here, beside, lo, hi)
        ):
            rhs = rhs - weight[None] * diff
        rhs = rhs * inside[lo:hi][None]
        if tile == 0:
            resid_out[...] = rhs
        out[...] = rhs.reshape(2, BLK, CC)
    local_solve(mats, edge, vec, total, side_vec, side_total, level, levels)
    put_results(prow, total, side_total, local_out, one_out, two_out)


def stiffness(main_f, side_f, main_t, side_t, lo, hi):
    stiff = [t * t * t for t in (main_t[...], side_t[...])]
    out = main_f[:, lo:hi, :]
    parts = differences(main_f, side_f, lo, hi)
    for weight, diff in zip(weights_of(stiff[0], stiff[1], lo, hi), parts):
        out = out + weight[None] * diff
    return out


def second_kernel(
    last, info, local, got_one, got_two, tcell, mats, edge, levels,
    main_f, side_f, image_out, local_out, one_out, two_out,
    vec, total, side_vec, side_total,
):
    level, prow = info[0], info[1]
    frames = (main_f, side_f)
    join(prow, last, local, got_one, got_two, frames)
    lo, hi = 7, 7 + EXT
    inside = grid_mask(prow, last, lo, EXT)
    for tile, out in ((0, vec), (1, side_vec)):
        image = stiffness(
            frames[tile], frames[1 - tile], tcell.at[tile], tcell.at[1 - tile], lo, hi
        ) * inside[None]
        if tile == 0:
            image_out[...] = image
        out[...] = image.reshape(2, BLK, CC)
    local_solve(mats, edge, vec, total, side_vec, side_total, level, levels)
    put_results(prow, total, side_total, local_out, one_out, two_out)


def dot3(a, b, i, j):
    out = jnp.zeros((CR, CC), F32)
    for an, bn in zip(a, b):
        for c in range(3):
            out = out + an[i + c] * bn[j + c]
    return out


def design_sums(n_col, info, frame, values, left_op, right_op):
    cells = frame[6, 8:8 + CR, :].astype(jnp.int32)
    owner = cells // DV
    low = cells % DV
    other = jnp.where((owner // n_col) % 2 == info[1] % 2, 0, 128)
    high = other + (owner // (2 * n_col)) * n_col + owner % n_col
    count = len(values)
    tops = [value.astype(BF16) for value in values]
    rests = [(value - top.astype(F32)).astype(BF16) for value, top in zip(values, tops)]
    for row in range(CR):
        cut = slice(CC * row, CC * row + CC)
        left_op[:, cut] = jnp.where(iota((256, CC), 0) == high[row:row + 1], 1.0, 0.0).astype(BF16)
        hot = jnp.where(iota((DV, CC), 0) == low[row:row + 1], 1.0, 0.0).astype(BF16)
        for k, part in enumerate(tops + rests):
            right_op[k * DV:(k + 1) * DV, cut] = hot * part[row:row + 1]
    sums = lax.dot_general(
        left_op[...], right_op[...], (((1,), (1,)), ((), ())), preferred_element_type=F32
    )
    return sums[:, :count * DV] + sums[:, count * DV:]


LO, HI = 8, 8 + CR


def known_sums_kernel(n_col, info, frame, tcell, dcell, main_f, side_f, out, left_op, right_op):
    known_d = differences(main_f, side_f, LO, HI)
    value = (-3.0 * tcell[0, LO:HI, :] * dcell[0, LO:HI, :]) * dot3(known_d, known_d, 3, 0)
    out[...] = design_sums(n_col, info, frame, [value], left_op, right_op)


def solved_values(tcell, known_d, solved_d):
    t = tcell[0, LO:HI, :]
    slope = -1.5 * t * t
    return [slope * dot3(solved_d, known_d, 3, 0), slope * dot3(known_d, solved_d, 3, 0)]


def solved_sums_kernel(
    n_col, info, frame, tcell, main_f, side_f, zframe, zside, out, left_op, right_op
):
    values = solved_values(
        tcell, differences(main_f, side_f, LO, HI), differences(zframe, zside, LO, HI)
    )
    out[...] = design_sums(n_col, info, frame, values, left_op, right_op)


def third_kernel(
    last, n_col, info, frame, resid, image, zframe, local, got_one, got_two,
    tcell, main_f, side_f, sums0, sums1,
    wframe, keep_out, send_out, wside, left_op, right_op,
):
    join(info[1], last, local, got_one, got_two, (wframe, wside))
    v = stiffness(wframe, wside, tcell.at[0], tcell.at[1], LO, HI)
    r = resid[:, 1:1 + CR, :]
    q = image[:, 1:1 + CR, :]
    z = zframe[:, LO:HI, :]
    w = wframe[:, LO:HI, :]
    lane = iota((1, CC), 1)
    dots = jnp.zeros((1, CC), F32)
    pairs = ((r, z), (z, q), (r, w), (q, w), (z, v), (w, v))
    for k, (a, b) in enumerate(pairs):
        ab = a * b
        for s in range(2):
            part = ab[3 * s] + ab[3 * s + 1] + ab[3 * s + 2]
            value = jnp.sum(jnp.sum(part, axis=0, keepdims=True), axis=1, keepdims=True)
            dots = jnp.where(lane == 2 * k + s, value, dots)
    values = solved_values(
        tcell, differences(main_f, side_f, LO, HI), differences(wframe, wside, LO, HI)
    )
    sums = design_sums(n_col, info, frame, values, left_op, right_op)
    for half, out in ((0, keep_out), (1, send_out)):
        count = out.shape[0]
        rows = slice(128 * half, 128 * half + count)
        out[:, 0:CC] = jnp.broadcast_to(dots, (count, CC))
        out[:, CC:2 * CC] = sums0[rows, :]
        out[:, 2 * CC:4 * CC] = sums1[rows, :]
        out[:, 4 * CC:] = sums[rows]


def last_kernel(got, zframe, wframe, tangent, second, owned):
    sums = jnp.sum(got[...], axis=0, keepdims=True)
    dots = sums[:, 0:CC]
    lane = iota((1, CC), 1)

    def pick(k):
        return jnp.sum(jnp.where(lane == k, dots, 0.0), axis=1, keepdims=True)

    coeffs = []
    for s in range(2):
        rz, zq, rw, qw, zv, wv = (pick(2 * k + s) for k in range(6))
        alpha = rz / zq
        rz1 = rz - alpha * (zq + rw) + alpha * alpha * qw
        grow = 1.0 + rz1 / rz
        pq = grow * grow * zq - grow * alpha * (zv + qw) + alpha * alpha * wv
        alpha1 = rz1 / pq
        coeffs.append((alpha + alpha1 * grow, -alpha1 * alpha))
    for s, out in ((0, tangent), (1, second)):
        c0, c1 = coeffs[s]
        for f in range(3):
            out[f] = c0 * zframe[3 * s + f, 8:8 + CR, :] + c1 * wframe[3 * s + f, 8:8 + CR, :]
    h = [sums[:, (k + 1) * CC:(k + 2) * CC] for k in range(5)]
    owned[...] = (
        h[0] + coeffs[1][0] * h[1] + coeffs[0][0] * h[2] + coeffs[1][1] * h[3] + coeffs[0][1] * h[4]
    )


def pairwise(count, one, two):
    first = [(i, i ^ 1) for i in range(count)]
    second = [(i, (i + (1 if i % 2 else -1)) % count) for i in range(count)]
    return lax.ppermute(one, ROW, first), lax.ppermute(two, ROW, second)


def ring(axis, count, to_next, to_previous):
    forward = [(i, (i + 1) % count) for i in range(count)]
    backward = [(b, a) for a, b in forward]
    return lax.ppermute(to_next, axis, forward), lax.ppermute(to_previous, axis, backward)


def per_device(state, adjoint, thickness, direction, design_map, levels, blocks):
    n_row, n_col = lax.axis_size(ROW), lax.axis_size("pcol")
    n_dev = n_row * n_col
    last = n_row - 1
    info = jnp.stack([levels[0, 0], lax.axis_index(ROW).astype(jnp.int32)])
    rows = functools.partial(pairwise, n_row)
    cols = functools.partial(ring, "pcol", n_col)

    own, frame, first, end = call(
        start_kernel, [(n_dev, 1, 2 * DV), (7, FR, CC), (EDGE + 8, CC), (EDGE + 8, CC)], [HBM] * 7,
        [
            pltpu.SMEM((1,), jnp.int32), pltpu.VMEM((6, CR, CC), F32),
            pltpu.VMEM((CR, CC), jnp.int32), pltpu.VMEM((2, 1, DV), F32),
            pltpu.VMEM((n_dev, 1, 2 * DV), F32), pltpu.VMEM((BLK, BLK, CC), F32),
            pltpu.SemaphoreType.DMA((7,)),
            pltpu.SemaphoreType.DMA((BLK // PIECE,)),
        ],
        work=10**9, limit=LARGE, outs=[HBM] + [VMEM] * 3,
    )(levels.reshape(1), thickness.reshape(1, DV), direction.reshape(1, DV), state, adjoint, design_map, blocks)
    table = lax.all_to_all(own, ROW + ("pcol",), 0, 0, tiled=True).reshape(n_dev, 2 * DV)
    if n_dev < 256:
        table = jnp.concatenate([table, jnp.zeros((256 - n_dev, 2 * DV), F32)], axis=0)
    from_left, from_right = cols(end, first)
    side, one, two, around, edge = call(
        rows_kernel, [(7, FR, CC), (2, 16, CC), (2, 16, CC), (8, CC), (3, BLK, CC)], [SMEM] + [VMEM] * 3,
        work=10**11,
    )(info, frame, from_left, from_right)

    solve_scratch = [pltpu.VMEM((2, BLK, CC), F32)] * 4
    pairs = len(PAIRS) + 1
    main_f, side_f, cells = call(
        functools.partial(place_kernel, last),
        [
            (6, FR, CC), (6, FR, CC), jax.ShapeDtypeStruct((pairs, 2 * CC), jnp.int32),
        ],
        [SMEM] + [VMEM] * 4, [pltpu.VMEM((2, FR, CC), F32)], work=3 * 10**9,
    )(info, frame, side, *rows(one, two))
    resid, local, one, two, tcell, dcell = call(
        functools.partial(first_kernel, last),
        [
            (6, EXT, CC), (2, 6, EXT, CC), (2, 24, CC), (2, 24, CC), (2, FR, CC), (2, FR, CC),
        ],
        [SMEM] + [VMEM] * 7, solve_scratch,
    )(info, table, main_f, side_f, cells, blocks, edge, around)

    def operands(count):
        return [pltpu.VMEM((256, CR * CC), BF16), pltpu.VMEM((2 * count * DV, CR * CC), BF16)]

    (sums0,) = call(
        functools.partial(known_sums_kernel, n_col), [(256, DV)], [SMEM] + [VMEM] * 5, operands(1),
        work=3 * 10**8,
    )(info, frame, tcell, dcell, main_f, side_f)
    zframe, zside, image, local, one, two = call(
        functools.partial(second_kernel, last),
        [(6, FR, CC), (6, FR, CC), (6, EXT, CC), (2, 6, EXT, CC), (2, 24, CC), (2, 24, CC)],
        [SMEM] + [VMEM] * 7,
        solve_scratch,
    )(info, local, *rows(one, two), tcell, blocks, edge, around)
    (sums1,) = call(
        functools.partial(solved_sums_kernel, n_col), [(256, 2 * DV)], [SMEM] + [VMEM] * 6,
        operands(2), work=5 * 10**8,
    )(info, frame, tcell, main_f, side_f, zframe, zside)
    wframe, keep, send = call(
        functools.partial(third_kernel, last, n_col),
        [(6, FR, CC)] + [(n_dev // 2, 6 * CC)] * 2, [SMEM] + [VMEM] * 12,
        [pltpu.VMEM((6, FR, CC), F32)] + operands(2),
    )(info, frame, resid, image, zframe, local, *rows(one, two), tcell, main_f, side_f, sums0, sums1)
    sums = keep + lax.ppermute(send, "core", [(0, 1), (1, 0)])
    got = lax.all_to_all(sums, ("y", "pcol"), 0, 0, tiled=True)
    tangent, second, owned = call(
        last_kernel, [(3, CR, CC), (3, CR, CC), (1, CC)], [VMEM] * 3
    )(got, zframe, wframe)
    return tangent, second, owned.reshape(DV)


def solution(mesh):
    n_row, n_col = mesh.devices.shape
    fine = jax.sharding.Mesh(mesh.devices.reshape(n_row // 2, 2, n_col), ("y", "core", "pcol"))
    field = P(None, ROW, "pcol")
    design = P(("y", "core", "pcol"))
    return jax.shard_map(
        per_device,
        mesh=fine,
        in_specs=(field, field, design, design, P(ROW, "pcol"), P(ROW, "pcol"), P(ROW, None, "pcol")),
        out_specs=(field, field, design),
        check_vma=False,
    )
```
